32 devices in a mesh: sp: 8 (over y, x, core), fs: 4 (over z).
Axes of the slice: x: 2, y: 2, z: 4, core: 2. Of those that a mesh axis runs over, the one named last changes fastest.
Arguments:
- tokens: bfloat16 [2, 4, 16, 192, 256], P(None, 'fs', 'sp'), may hold values from -6 to 6
- cotangent: float32 [2, 4, 16, 192, 256], P(None, 'fs', 'sp'), may hold values from -6 to 6
- image_sizes: int32 [2, 4, 2], P(None, 'fs'), may hold values from 8 to 192, as said below
- first_gain: bfloat16 [256], P('fs'), may hold values from 0.25 to 1.75
- first_bias: bfloat16 [256], P('fs'), may hold values from -0.109375 to 0.109375
- query_weight: bfloat16 [256, 256], P('fs'), may hold values from -0.375 to 0.375
- query_bias: bfloat16 [256], P('fs'), may hold values from -1.75 to 1.75
- reduce_weight: bfloat16 [1024, 256], P('fs'), may hold values from -0.1875 to 0.1875
- reduce_bias: bfloat16 [256], P('fs'), may hold values from -0.109375 to 0.109375
- keys_gain: bfloat16 [256], P('fs'), may hold values from 0.25 to 1.75
- keys_bias: bfloat16 [256], P('fs'), may hold values from -0.109375 to 0.109375
- keyval_weight: bfloat16 [256, 512], P('fs'), may hold values from -0.375 to 0.375
- value_bias: bfloat16 [256], P('fs'), may hold values from -0.109375 to 0.109375
- output_weight: bfloat16 [256, 256], P('fs'), may hold values from -6 to 6
- output_bias: bfloat16 [256], P('fs'), may hold values from -1.75 to 1.75
- second_gain: bfloat16 [256], P('fs'), may hold values from 0.25 to 1.75
- second_bias: bfloat16 [256], P('fs'), may hold values from -1.75 to 1.75
- hidden_weight: bfloat16 [256, 1024], P('fs'), may hold values from -0.375 to 0.375
- hidden_bias: bfloat16 [1024], P('fs'), may hold values from -1.75 to 1.75
- return_weight: bfloat16 [1024, 256], P('fs'), may hold values from -0.1875 to 0.1875
- return_bias: bfloat16 [256], P('fs'), may hold values from -1.75 to 1.75
Outputs:
- activations: float32 [2, 4, 16, 192, 256], P(None, 'fs', 'sp')
- input_grad: float32 [2, 4, 16, 192, 256], P(None, 'fs', 'sp')
- grad_first_gain: float32 [256], P('fs')
- grad_first_bias: float32 [256], P('fs')
- grad_query_weight: float32 [256, 256], P('fs')
- grad_query_bias: float32 [256], P('fs')
- grad_reduce_weight: float32 [1024, 256], P('fs')
- grad_reduce_bias: float32 [256], P('fs')
- grad_keys_gain: float32 [256], P('fs')
- grad_keys_bias: float32 [256], P('fs')
- grad_keyval_weight: float32 [256, 512], P('fs')
- grad_value_bias: float32 [256], P('fs')
- grad_output_weight: float32 [256, 256], P('fs')
- grad_output_bias: float32 [256], P('fs')
- grad_second_gain: float32 [256], P('fs')
- grad_second_bias: float32 [256], P('fs')
- grad_hidden_weight: float32 [256, 1024], P('fs')
- grad_hidden_bias: float32 [1024], P('fs')
- grad_return_weight: float32 [1024, 256], P('fs')
- grad_return_bias: float32 [256], P('fs')
The draws below stay inside these ranges and needn't reach their ends.
Inputs may be any that keep to these rules, and one draw needn't show every extreme that they name: image_sizes[b, i] = (height, width) in patches of image i of micro-batch b; heights from 8 to 16, widths from 96 to 192; for every i one micro-batch's image fills the whole 16 x 192 grid.
All inputs are finite; a program needn't handle non-finite values.
Results may differ from the reference program's by a relative error of at most 0.019.
Values may be sent and summed in bfloat16 or wider, within the bound.
No kernel may reach another device: no remote copies, remote signals or barrier semaphores. Data moves between devices by JAX's collectives and lax.ppermute only.
A program may use at most 128 MiB of HBM per device.

```python
import jax
import jax.numpy as jnp
from jax import lax

D = 256
HEADS = 8
HDIM = 32
FF = 1024
MB = 2
COLS = 192
ROWS = 16
KEYS = 768
IMAGES = 4


def draw_image_sizes(key, part):
    key = jax.random.fold_in(key, 11)
    key_height, key_width, key_full = jax.random.split(key, 3)
    heights = jax.random.randint(key_height, (MB, IMAGES), ROWS // 2, ROWS + 1)
    widths = jax.random.randint(key_width, (MB, IMAGES), COLS // 2, COLS + 1)
    chosen = jax.random.randint(key_full, (IMAGES,), 0, MB)
    picked = jnp.arange(MB, dtype=jnp.int32)[:, None] == chosen[None, :]
    heights = jnp.where(picked, ROWS, heights)
    widths = jnp.where(picked, COLS, widths)
    return jnp.stack([heights, widths], axis=-1).astype(jnp.int32)


def level_of(stream_key, extent, cuts, least, top_value):
    factor_of = 1.0
    for dim, blocks in cuts:
        steps = jax.random.uniform(jax.random.fold_in(jax.random.fold_in(stream_key, 6), dim), (blocks,), jnp.float32, least / len(cuts), top_value / len(cuts))
        factor_of = factor_of * jnp.repeat(jnp.exp(steps), extent[dim] // blocks).reshape((-1,) + (1,) * (len(extent) - 1 - dim))
    return factor_of


def gaussian(rng, dims, scale, limit, shards=(), kind=jnp.bfloat16):
    entries = jax.random.normal(rng, dims, jnp.float32) * scale
    if len(shards) > 0:
        entries = level_of(rng, dims, shards, -0.22, 0.18) * entries
    return jnp.clip(entries, min=-limit, max=limit).astype(kind)


def setup_inputs(seed: int = 0) -> dict:
    splits = jax.random.split(jax.random.key(seed), 22)
    return {
        "tokens": gaussian(splits[0], (MB, IMAGES, ROWS, COLS, D), 1.0, 6.0, ((1, 4), (2, 8))),
        "cotangent": gaussian(splits[1], (MB, IMAGES, ROWS, COLS, D), 1.0, 6.0, ((1, 4), (2, 8)), jnp.float32),
        "image_sizes": draw_image_sizes(jax.random.fold_in(splits[21], 71), 0),
        "first_gain": jnp.clip(1.0 + 0.15 * jax.random.normal(splits[3], (D,), jnp.float32), 0.25, 1.75).astype(jnp.bfloat16),
        "first_bias": gaussian(splits[4], (D,), (0.5 * KEYS ** -0.5), 0.109375, ((0, 4),)),
        "query_weight": gaussian(splits[5], (D, D), D ** -0.5, 0.375, ((0, 4),)),
        "query_bias": gaussian(splits[6], (D,), 0.3, 1.75, ((0, 4),)),
        "reduce_weight": gaussian(splits[7], (4 * D, D), (4 * D) ** -0.5, 0.1875, ((0, 4),)),
        "reduce_bias": gaussian(splits[8], (D,), (0.5 * KEYS ** -0.5), 0.109375, ((0, 4),)),
        "keys_gain": jnp.clip(1.0 + 0.15 * jax.random.normal(splits[9], (D,), jnp.float32), 0.25, 1.75).astype(jnp.bfloat16),
        "keys_bias": gaussian(splits[10], (D,), (0.5 * KEYS ** -0.5), 0.109375, ((0, 4),)),
        "keyval_weight": gaussian(splits[11], (D, 2 * D), D ** -0.5, 0.375, ((0, 4),)),
        "value_bias": gaussian(splits[12], (D,), (0.5 * KEYS ** -0.5), 0.109375, ((0, 4),)),
        "output_weight": gaussian(splits[13], (D, D), ((KEYS // 3) ** 0.5 * D ** -0.5), 6.0, ((0, 4),)),
        "output_bias": gaussian(splits[14], (D,), 0.3, 1.75, ((0, 4),)),
        "second_gain": jnp.clip(1.0 + 0.15 * jax.random.normal(splits[15], (D,), jnp.float32), 0.25, 1.75).astype(jnp.bfloat16),
        "second_bias": gaussian(splits[16], (D,), 0.3, 1.75, ((0, 4),)),
        "hidden_weight": gaussian(splits[17], (D, FF), D ** -0.5, 0.375, ((0, 4),)),
        "hidden_bias": gaussian(splits[18], (FF,), 0.3, 1.75, ((0, 4),)),
        "return_weight": gaussian(splits[19], (FF, D), FF ** -0.5, 0.1875, ((0, 4),)),
        "return_bias": gaussian(splits[20], (D,), 0.3, 1.75, ((0, 4),)),
    }


norm_eps = 1e-06
neg_large = -1e+30
highest = lax.Precision.HIGHEST

@jax.custom_vjp
def low(v):
    return lax.optimization_barrier(v.astype(jnp.bfloat16)).astype(jnp.float32)

@jax.custom_vjp
def low_back(v):
    return v

def low_keep(v):
    return (low(v), None)

def low_pass(kept, grad):
    return (grad,)

def back_keep(v):
    return (v, None)

def back_low(kept, grad):
    return (low(grad),)
low.defvjp(low_keep, low_pass)
low_back.defvjp(back_keep, back_low)

def product(left, right):
    return jnp.dot(left, right, precision=highest, preferred_element_type=jnp.float32)

def layer_norm(tensor, norm_gain, norm_shift):
    row_mean = lax.optimization_barrier(jnp.mean(tensor, axis=-1, keepdims=True))
    centered = tensor - row_mean
    variance = lax.optimization_barrier(jnp.mean(centered * centered, axis=-1, keepdims=True))
    return centered * lax.rsqrt(variance + norm_eps) * norm_gain + norm_shift

def forward_image(inputs, params, tok_mask, key_mask):
    first_gain, first_bias, query_weight, query_bias, reduce_weight, reduce_bias, keys_gain, keys_bias, keyval_weight, value_bias, output_weight, output_bias, second_gain, second_bias, hidden_weight, hidden_bias, return_weight, return_bias = params
    tokens_all = ROWS * COLS
    flat = inputs.reshape(tokens_all, D)
    normed = low(layer_norm(flat, first_gain, first_bias))
    queries = low_back(low(product(normed, query_weight) + query_bias))
    masked = normed * tok_mask[:, None]
    patches = masked.reshape(ROWS // 2, 2, COLS // 2, 2, D).transpose(0, 2, 1, 3, 4).reshape(KEYS, 4 * D)
    reduced = low_back(product(patches, reduce_weight) + reduce_bias)
    key_normed = low(layer_norm(reduced, keys_gain, keys_bias))
    shift_row = jnp.concatenate([jnp.zeros((D,), jnp.float32), value_bias])
    keyval = low_back(low(product(key_normed, keyval_weight) + shift_row))
    key_heads = keyval[:, :D].reshape(KEYS, HEADS, HDIM)
    value_heads = keyval[:, D:].reshape(KEYS, HEADS, HDIM)
    score_scale = HDIM ** (-0.5)

    @jax.checkpoint
    def attend(query_block):
        query_heads = query_block.reshape(-1, HEADS, HDIM)
        scores = low_back(jnp.einsum('qhd,khd->hqk', query_heads, key_heads, precision=highest) * score_scale)
        scores = jnp.where(key_mask[None, None, :], scores, neg_large)
        probs = low(jax.nn.softmax(scores, axis=-1))
        return jnp.einsum('hqk,khd->qhd', probs, value_heads, precision=highest).reshape(-1, D)
    query_rows = 512 if tokens_all % 512 == 0 else tokens_all
    blocks = tokens_all // query_rows
    attended = lax.map(attend, queries.reshape(blocks, query_rows, D)).reshape(tokens_all, D)
    attended = low_back(low(attended))
    branch = low_back(product(attended, output_weight) + output_bias)
    middle = flat + branch
    second = low(layer_norm(middle, second_gain, second_bias))
    hidden = low_back(product(second, hidden_weight) + hidden_bias)
    activated = low(jax.nn.gelu(hidden, approximate=False))
    mlp_out = low_back(product(activated, return_weight) + return_bias)
    return ((middle + mlp_out) * tok_mask[:, None]).reshape(ROWS, COLS, D)

def reference(tokens, cotangent, image_sizes, first_gain, first_bias, query_weight, query_bias, reduce_weight, reduce_bias, keys_gain, keys_bias, keyval_weight, value_bias, output_weight, output_bias, second_gain, second_bias, hidden_weight, hidden_bias, return_weight, return_bias):
    params = tuple((weight.astype(jnp.float32) for weight in (first_gain, first_bias, query_weight, query_bias, reduce_weight, reduce_bias, keys_gain, keys_bias, keyval_weight, value_bias, output_weight, output_bias, second_gain, second_bias, hidden_weight, hidden_bias, return_weight, return_bias)))
    images = MB * IMAGES
    flat_tokens = tokens.reshape(images, ROWS, COLS, D)
    flat_cot = cotangent.reshape(images, ROWS, COLS, D)
    flat_dims = image_sizes.reshape(images, 2)
    row_ids = jnp.arange(ROWS, dtype=jnp.int32)
    col_ids = jnp.arange(COLS, dtype=jnp.int32)
    key_rows = jnp.arange(ROWS // 2, dtype=jnp.int32)
    key_cols = jnp.arange(COLS // 2, dtype=jnp.int32)

    def one_image(running, scan_item):
        inputs, cot_rows, image_dims = scan_item
        height = image_dims[0]
        image_width = image_dims[1]
        tok_mask = ((row_ids[:, None] < height) & (col_ids[None, :] < image_width)).astype(jnp.float32).reshape(-1)
        key_mask = ((2 * key_rows[:, None] < height) & (2 * key_cols[None, :] < image_width)).reshape(-1)

        def image_fn(inputs_now, *weights):
            return forward_image(inputs_now, weights, tok_mask, key_mask)
        outputs, pullback = jax.vjp(image_fn, inputs.astype(jnp.float32), *params)
        grads = pullback(cot_rows)
        running = tuple((total + grad for total, grad in zip(running, grads[1:])))
        return (running, (outputs, grads[0]))
    start = tuple((jnp.zeros_like(weight) for weight in params))
    totals, (acts, input_grads) = lax.scan(one_image, start, (flat_tokens, flat_cot, flat_dims))
    return (acts.reshape(MB, IMAGES, ROWS, COLS, D), input_grads.reshape(MB, IMAGES, ROWS, COLS, D), totals[0], totals[1], totals[2], totals[3], totals[4], totals[5], totals[6], totals[7], totals[8], totals[9], totals[10], totals[11], totals[12], totals[13], totals[14], totals[15], totals[16], totals[17])
```

```python
import functools

import jax
import jax.numpy as jnp
from jax import lax
from jax.experimental import pallas as pl
from jax.experimental.pallas import tpu as pltpu
from jax.sharding import PartitionSpec as P

HEADS = 8
HDIM = 32
PAIRS = HEADS // 2
SCALE = HDIM ** (-0.5)
EXP_SCALE = SCALE * 1.4426950408889634
EPS = 1e-06
NEG = -1e30
KEY_BLOCK = 768
VMEM_LIMIT = 58 * 2**20

bf16 = jnp.bfloat16
f32 = jnp.float32

(
    FIRST_G,
    FIRST_B,
    QUERY_B,
    REDUCE_B,
    KEYS_G,
    KEYS_B,
    VALUE_B,
    OUTPUT_B,
    SECOND_G,
    SECOND_B,
    RETURN_B,
    HIDDEN_B,
) = range(12)
VECS = 16


def mm(left, right):
    return jnp.dot(left, right, preferred_element_type=f32)


def mm_tn(left, right):
    return lax.dot_general(left, right, (((0,), (0,)), ((), ())), preferred_element_type=f32)


def mm_nt(left, right):
    return lax.dot_general(left, right, (((1,), (1,)), ((), ())), preferred_element_type=f32)


def normalize(rows):
    mean = jnp.mean(rows, axis=-1, keepdims=True)
    centered = rows - mean
    var = jnp.mean(centered * centered, axis=-1, keepdims=True)
    rstd = lax.rsqrt(var + EPS)
    return centered * rstd, rstd


def normalize_back(grad, normal, rstd, gain):
    scaled = grad * gain
    mean_a = jnp.mean(scaled, axis=-1, keepdims=True)
    mean_b = jnp.mean(scaled * normal, axis=-1, keepdims=True)
    return (scaled - mean_a - normal * mean_b) * rstd


def token_mask(first_row, rows, cols, width, height, image_width):
    row_ids = lax.broadcasted_iota(jnp.int32, (rows, cols, width), 0) + first_row
    col_ids = lax.broadcasted_iota(jnp.int32, (rows, cols, width), 1)
    valid = (row_ids < height) & (col_ids < image_width)
    return jnp.where(valid, 1.0, 0.0).astype(f32).reshape(rows * cols, width)


def key_bias(rows, cols, width, height, image_width):
    row_ids = lax.broadcasted_iota(jnp.int32, (rows, cols, width), 0)
    col_ids = lax.broadcasted_iota(jnp.int32, (rows, cols, width), 1)
    valid = (2 * row_ids < height) & (2 * col_ids < image_width)
    return jnp.where(valid, 0.0, NEG).astype(f32).reshape(rows * cols, width)


def reduce_kernel(dims, sizes, tokens, own_w, own_v, *refs):
    n_fs, batches, row_dev, cols, dim = dims
    mine, other = refs[: n_fs - 1], refs[n_fs - 1 : 2 * n_fs - 2]
    normed_ref, patch_ref, reduced_ref, key_ref, weight_ref, vec_ref, wide = refs[2 * n_fs - 2 :]
    half = dim // 2
    tok = row_dev * cols
    half_cols = cols // 2
    key_dev = tok // 4
    fs = lax.axis_index("fs")
    sp = lax.axis_index("sp")
    is_low = sp % 2 == 0
    weight_ref[fs] = own_w[...]
    vec = own_v[...].astype(f32)
    for step in range(1, n_fs):
        a, b = mine[step - 1][...], other[step - 1][...]
        place = lax.rem(fs + n_fs - step, n_fs)
        weight_ref[place, :half] = jnp.where(is_low, a[:half], b[:half])
        weight_ref[place, half:] = jnp.where(is_low, b[:half], a[:half])
        vec = vec + a[half:].astype(f32)
    vec_ref[...] = vec
    for batch in range(batches):
        x = tokens[batch, 0].reshape(tok, dim).astype(f32)
        normal, _ = normalize(x)
        low = (normal * vec[FIRST_G : FIRST_G + 1] + vec[FIRST_B : FIRST_B + 1]).astype(bf16)
        normed_ref[batch * tok : (batch + 1) * tok] = low
        mask = token_mask(sp * row_dev, row_dev, cols, dim, sizes[batch, 0, 0], sizes[batch, 0, 1])
        masked = low.astype(f32) * mask
        for part in range(dim // 128):
            wide[part] = masked[:, part * 128 : (part + 1) * 128]
        for row in range(row_dev // 2):
            start = batch * key_dev + row * half_cols
            for offset in range(4):
                dr, dc = offset // 2, offset % 2
                for part in range(dim // 128):
                    piece = wide[part, pl.ds((2 * row + dr) * cols + dc, half_cols, stride=2), :]
                    lanes = slice(offset * dim + part * 128, offset * dim + (part + 1) * 128)
                    patch_ref[start : start + half_cols, lanes] = piece.astype(bf16)
    reduced = mm(patch_ref[...], weight_ref[...].reshape(4 * dim, dim)) + vec[REDUCE_B : REDUCE_B + 1]
    reduced_ref[...] = reduced
    normal, _ = normalize(reduced)
    key_ref[...] = (normal * vec[KEYS_G : KEYS_G + 1] + vec[KEYS_B : KEYS_B + 1]).astype(bf16)


def place_weights(place, lows, highs, wq, wkv, wo, wh, wr, shard):
    rows = pl.ds(pl.multiple_of(place * shard, shard), shard)
    dim = wq.shape[1]
    wq[rows, :] = lows[:shard]
    wkv[rows, :dim] = lows[shard : 2 * shard]
    wkv[rows, dim:] = lows[2 * shard : 3 * shard]
    wo[rows, :] = lows[3 * shard : 4 * shard]
    wh[rows, :dim] = lows[4 * shard : 5 * shard]
    wh[rows, dim : 2 * dim] = lows[5 * shard :]
    wh[rows, 2 * dim : 3 * dim] = highs[:shard]
    wh[rows, 3 * dim :] = highs[shard : 2 * shard]
    wr[pl.ds(pl.multiple_of(place * dim, dim), dim), :] = highs[2 * shard :]


def head_stack_t(values_t, pair, tok):
    both = jnp.concatenate([values_t, values_t], axis=1)
    head = lax.broadcasted_iota(jnp.int32, both.shape, 0) // HDIM
    want = 2 * pair + jnp.where(lax.broadcasted_iota(jnp.int32, both.shape, 1) >= tok, 1, 0)
    return jnp.where(head == want, both, jnp.zeros_like(both))


def head_stack(values, pair):
    head = lax.broadcasted_iota(jnp.int32, values.shape, 1) // HDIM
    zero = jnp.zeros_like(values)
    return jnp.concatenate(
        [jnp.where(head == 2 * pair, values, zero), jnp.where(head == 2 * pair + 1, values, zero)],
        axis=0,
    )


def split_pair(both, tok):
    return jnp.concatenate([both[:HDIM, :tok], both[HDIM:, tok:]], axis=0)


def main_kernel(dims, sizes, tokens, normed, keys_in, cotangent, vec_ref, own, mine, other, outs, scratch):
    n_fs, n_sp, batches, row_dev, cols, dim, hid = dims
    acts_ref, middle_ref, gnormed_ref, gkey_a, gkey_b, grad_a, grad_b, gvec_ref = outs
    (wq, wkv, wo, wh, wr, qs, kvs, attended, n2s, rstds, gmid, probs, stats, gatt, attf, gqs, dks, dvs) = (
        scratch
    )
    tok = row_dev * cols
    half_cols = cols // 2
    key_dev = tok // 4
    keys = n_sp * key_dev
    blocks = keys // KEY_BLOCK if keys > KEY_BLOCK else 1
    block = keys // blocks
    fs = lax.axis_index("fs")
    sp = lax.axis_index("sp")
    is_low = sp % 2 == 0
    shard = dim // n_fs

    own_q, own_kv, own_o, own_h, own_r = own
    first = pl.ds(pl.multiple_of(fs * shard, shard), shard)
    wq[first, :] = own_q[...]
    wkv[first, :] = own_kv[...]
    wo[first, :] = own_o[...]
    wh[first, :] = own_h[...]
    wr[pl.ds(pl.multiple_of(fs * dim, dim), dim), :] = own_r[...]
    for step in range(1, n_fs):
        a, b = mine[step - 1][...], other[step - 1][...]
        place = lax.rem(fs + n_fs - step, n_fs)
        place_weights(place, jnp.where(is_low, a, b), jnp.where(is_low, b, a), wq, wkv, wo, wh, wr, shard)

    def vec(index):
        return vec_ref[index : index + 1, :]

    masks = [
        token_mask(sp * row_dev, row_dev, cols, dim, sizes[b, 0, 0], sizes[b, 0, 1]) for b in range(batches)
    ]
    zero_row = jnp.zeros((1, dim), f32)
    lane = lax.broadcasted_iota(jnp.int32, (block, dim), 1)

    per_block = block // key_dev

    def key_piece(batch, piece):
        devices = slice(piece * per_block, (piece + 1) * per_block)
        return keys_in[devices, batch * key_dev : (batch + 1) * key_dev, :].reshape(block, dim)

    for batch in range(batches):
        rows = slice(batch * tok, (batch + 1) * tok)
        queries = (mm(normed[rows], wq[...]) + vec(QUERY_B)).astype(bf16)
        qs[rows] = queries
        queries_t = queries.T
        for piece in range(blocks):
            key_rows = key_piece(batch, piece)
            here = slice(piece * block, (piece + 1) * block)
            kvs[batch, here, :dim] = mm(key_rows, wkv[:, :dim]).astype(bf16)
            kvs[batch, here, dim:] = (mm(key_rows, wkv[:, dim:]) + vec(VALUE_B)).astype(bf16)
        height, image_width = sizes[batch, 0, 0], sizes[batch, 0, 1]

        def biased(index, lane_id, batch=batch, height=height, image_width=image_width):
            rows_in = block // half_cols
            row_ids = lax.broadcasted_iota(jnp.int32, (rows_in, half_cols, dim), 0) + index * rows_in
            col_ids = lax.broadcasted_iota(jnp.int32, (rows_in, half_cols, dim), 1)
            valid = (2 * row_ids < height) & (2 * col_ids < image_width)
            bias = jnp.where(valid, 0.0, NEG).astype(f32).reshape(block, dim)
            key_block = kvs[batch, pl.ds(index * block, block), :dim]
            return jnp.where(lane == lane_id, bias, key_block.astype(f32)).astype(bf16)

        def query_pair(pair, lane_id, queries_t=queries_t):
            stacked = head_stack_t(queries_t, pair, tok)
            row = lax.broadcasted_iota(jnp.int32, stacked.shape, 0)
            return jnp.where(row == lane_id, jnp.ones_like(stacked), stacked)

        if blocks == 1:
            key_high, key_low = biased(0, dim - 1), biased(0, 0)
            values_t = kvs[batch, :, dim:].T
            for pair in range(PAIRS):
                last = pair == PAIRS - 1
                scores = mm(key_low if last else key_high, query_pair(pair, 0 if last else dim - 1))
                top = jnp.max(scores, axis=0, keepdims=True)
                weights = jnp.exp2((scores - top) * EXP_SCALE)
                inverse = 1.0 / jnp.sum(weights, axis=0, keepdims=True)
                low = weights.astype(bf16)
                probs[batch, pair] = low
                stats[batch, pair, 0:1] = inverse
                mixed = mm(values_t[2 * HDIM * pair : 2 * HDIM * (pair + 1)], low) * inverse
                attf[batch, 2 * HDIM * pair : 2 * HDIM * (pair + 1)] = split_pair(mixed, tok)
        else:
            for pair in range(PAIRS):
                last = pair == PAIRS - 1
                lane_id = 0 if last else dim - 1
                stacked = query_pair(pair, lane_id)

                def find_top(index, top, stacked=stacked, lane_id=lane_id, biased=biased):
                    scores = mm(biased(index, lane_id), stacked)
                    return jnp.maximum(top, jnp.max(scores, axis=0, keepdims=True))

                top = lax.fori_loop(0, blocks, find_top, jnp.full((1, 2 * tok), NEG, f32))

                def add_block(index, carry, stacked=stacked, lane_id=lane_id, biased=biased, top=top, pair=pair, batch=batch):
                    total, mixed = carry
                    scores = mm(biased(index, lane_id), stacked)
                    weights = jnp.exp2((scores - top) * EXP_SCALE)
                    values = kvs[batch, pl.ds(index * block, block), dim:].T
                    mixed = mixed + mm(values[2 * HDIM * pair : 2 * HDIM * (pair + 1)], weights.astype(bf16))
                    return total + jnp.sum(weights, axis=0, keepdims=True), mixed

                total, mixed = lax.fori_loop(
                    0,
                    blocks,
                    add_block,
                    (jnp.zeros((1, 2 * tok), f32), jnp.zeros((2 * HDIM, 2 * tok), f32)),
                )
                inverse = 1.0 / total
                stats[batch, pair, 0:1] = inverse
                stats[batch, pair, 1:2] = top
                attf[batch, 2 * HDIM * pair : 2 * HDIM * (pair + 1)] = split_pair(mixed * inverse, tok)
        attended[rows] = attf[batch].T.astype(bf16)

    x = jnp.concatenate([tokens[b, 0].reshape(tok, dim).astype(f32) for b in range(batches)], axis=0)
    mask = jnp.concatenate(masks, axis=0)
    middle = x + mm(attended[...], wo[...]) + vec(OUTPUT_B)
    normal, rstd = normalize(middle)
    second = (normal * vec(SECOND_G) + vec(SECOND_B)).astype(bf16)
    grad_out = (
        jnp.concatenate([cotangent[b, 0].reshape(tok, dim) for b in range(batches)], axis=0) * mask
    )
    grad_mlp = grad_out.astype(bf16)
    total = middle + vec(RETURN_B)
    grad_second = jnp.zeros((batches * tok, dim), f32)
    low_rows = is_low

    def store(index, start, value):
        value = value.astype(bf16)
        rows = value.shape[0]
        half = 3 * dim // 2
        begin = start % half
        in_low = start < half
        keep = low_rows if in_low else jnp.logical_not(low_rows)

        @pl.when(keep)
        def _():
            grad_a[index, begin : begin + rows, :] = value

        @pl.when(jnp.logical_not(keep))
        def _():
            grad_b[index, begin : begin + rows, :] = value

    hidden_rows = []
    chunks = hid // dim
    for chunk in range(chunks):
        lanes = slice(chunk * dim, (chunk + 1) * dim)
        hidden = mm(second, wh[:, lanes]) + vec(HIDDEN_B + chunk)
        phi = 0.5 + 0.5 * lax.erf(hidden * 0.7071067811865476)
        density = 0.3989422804014327 * jnp.exp2(hidden * hidden * (-0.5 * 1.4426950408889634))
        activated = (hidden * phi).astype(bf16)
        total = total + mm(activated, wr[lanes, :])
        grad_activated = mm_nt(grad_mlp, wr[lanes, :])
        grad_hidden_wide = (phi + hidden * density) * grad_activated
        grad_hidden = grad_hidden_wide.astype(bf16)
        hidden_rows.append(jnp.sum(grad_hidden.astype(f32), axis=0, keepdims=True))
        grad_second = grad_second + mm_nt(grad_hidden, wh[:, lanes])
        grad_wr = mm_tn(activated, grad_mlp)
        store(chunk, 2 * dim, grad_wr[: dim])
        grad_wh = mm_tn(second, grad_hidden)
        for owner in range(n_fs):
            store(owner, 4 * shard + chunk * shard, grad_wh[owner * shard : (owner + 1) * shard])
    total = total * mask
    for batch in range(batches):
        acts_ref[batch, 0] = total[batch * tok : (batch + 1) * tok].reshape(row_dev, cols, dim)
    grad_middle = grad_out + normalize_back(grad_second, normal, rstd, vec(SECOND_G))
    middle_ref[...] = grad_middle
    grad_branch = grad_middle.astype(bf16)
    grad_wo = mm_tn(attended[...], grad_branch)
    for owner in range(n_fs):
        store(owner, 3 * shard, grad_wo[owner * shard : (owner + 1) * shard])
    gatt[...] = mm_nt(grad_branch, wo[...]).astype(bf16)
    bias_output = jnp.sum(grad_branch.astype(f32), axis=0, keepdims=True)
    gain_second = jnp.sum(grad_second * normal, axis=0, keepdims=True)
    bias_second = jnp.sum(grad_second, axis=0, keepdims=True)
    bias_return = jnp.sum(grad_mlp.astype(f32), axis=0, keepdims=True)

    bias_value = zero_row
    grad_wkv = [jnp.zeros((dim, dim), f32), jnp.zeros((dim, dim), f32)]
    for batch in range(batches):
        rows = slice(batch * tok, (batch + 1) * tok)
        queries = qs[rows]
        grad_att_t = gatt[rows].astype(f32).T
        product = grad_att_t * attf[batch]

        def pair_terms(pair, batch=batch, grad_att_t=grad_att_t, product=product):
            inverse = stats[batch, pair, 0:1]
            piece = product[2 * HDIM * pair : 2 * HDIM * (pair + 1)]
            delta = jnp.concatenate(
                [
                    jnp.sum(piece[:HDIM], axis=0, keepdims=True),
                    jnp.sum(piece[HDIM:], axis=0, keepdims=True),
                ],
                axis=1,
            )
            stacked = head_stack_t(grad_att_t, pair, tok) * inverse
            return delta * inverse, stacked.astype(bf16)

        if blocks == 1:
            keys_t = kvs[batch, :, :dim].T
            values = kvs[batch, :, dim:]
            grad_k = jnp.zeros((keys, dim), f32)
            grad_v = jnp.zeros((keys, dim), f32)
            for pair in range(PAIRS):
                delta, stacked = pair_terms(pair)
                low = probs[batch, pair]
                grad_probs = mm(values, stacked)
                grad_scores = (low.astype(f32) * (grad_probs - delta)).astype(bf16)
                gq = mm(keys_t[2 * HDIM * pair : 2 * HDIM * (pair + 1)], grad_scores)
                gqs[2 * HDIM * pair : 2 * HDIM * (pair + 1)] = split_pair(gq, tok)
                grad_k = grad_k + mm(grad_scores, head_stack(queries, pair))
                grad_v = grad_v + mm(low, stacked.T)
        else:
            dks[...] = jnp.zeros_like(dks)
            dvs[...] = jnp.zeros_like(dvs)
            queries_t = queries.T
            height, image_width = sizes[batch, 0, 0], sizes[batch, 0, 1]
            for pair in range(PAIRS):
                last = pair == PAIRS - 1
                lane_id = 0 if last else dim - 1
                delta, stacked = pair_terms(pair)
                stacked_n = stacked.T
                query_t = head_stack_t(queries_t, pair, tok)
                row = lax.broadcasted_iota(jnp.int32, query_t.shape, 0)
                query_t = jnp.where(row == lane_id, jnp.ones_like(query_t), query_t)
                query_n = head_stack(queries, pair)
                top = stats[batch, pair, 1:2]

                def back_block(index, gq, pair=pair, lane_id=lane_id, delta=delta, stacked=stacked, stacked_n=stacked_n, query_t=query_t, query_n=query_n, top=top, batch=batch, height=height, image_width=image_width):
                    here = pl.ds(index * block, block)
                    rows_in = block // half_cols
                    row_ids = lax.broadcasted_iota(jnp.int32, (rows_in, half_cols, dim), 0) + index * rows_in
                    col_ids = lax.broadcasted_iota(jnp.int32, (rows_in, half_cols, dim), 1)
                    valid = (2 * row_ids < height) & (2 * col_ids < image_width)
                    bias = jnp.where(valid, 0.0, NEG).astype(f32).reshape(block, dim)
                    key_block = kvs[batch, here, :dim]
                    masked = jnp.where(lane == lane_id, bias, key_block.astype(f32)).astype(bf16)
                    weights = jnp.exp2((mm(masked, query_t) - top) * EXP_SCALE)
                    grad_probs = mm(kvs[batch, here, dim:], stacked)
                    grad_scores = (weights * (grad_probs - delta)).astype(bf16)
                    keys_t = key_block.T[2 * HDIM * pair : 2 * HDIM * (pair + 1)]
                    dks[here, :] += mm(grad_scores, query_n)
                    dvs[here, :] += mm(weights.astype(bf16), stacked_n)
                    return gq + mm(keys_t, grad_scores)

                gq = lax.fori_loop(0, blocks, back_block, jnp.zeros((2 * HDIM, 2 * tok), f32))
                gqs[2 * HDIM * pair : 2 * HDIM * (pair + 1)] = split_pair(gq, tok)
        qs[rows] = (gqs[...].T * SCALE).astype(bf16)
        for piece in range(blocks):
            if blocks > 1:
                here = slice(piece * block, (piece + 1) * block)
                grad_k, grad_v = dks[here], dvs[here]
            grad_k = (grad_k * SCALE).astype(bf16)
            bias_value = bias_value + jnp.sum(grad_v, axis=0, keepdims=True)
            grad_v = grad_v.astype(bf16)
            key_rows = key_piece(batch, piece)
            grad_wkv[0] = grad_wkv[0] + mm_tn(key_rows, grad_k)
            grad_wkv[1] = grad_wkv[1] + mm_tn(key_rows, grad_v)
            grad_key = (mm_nt(grad_k, wkv[:, :dim]) + mm_nt(grad_v, wkv[:, dim:])).astype(bf16)
            here = slice(batch * key_dev, (batch + 1) * key_dev)
            if n_sp == 8:
                pairs = grad_key.reshape(n_sp // 2, 2, key_dev, dim)
                even, odd = pairs[:, 0], pairs[:, 1]
                gkey_a[:, here, :] = jnp.where(is_low, even, odd)
                gkey_b[:, here, :] = jnp.where(is_low, odd, even)
            else:
                devices = slice(piece * per_block, (piece + 1) * per_block)
                gkey_a[devices, here, :] = grad_key.reshape(per_block, key_dev, dim)
    grad_queries = qs[...]
    gnormed_ref[...] = mm_nt(grad_queries, wq[...])
    grad_wq = mm_tn(normed[...], grad_queries)
    for owner in range(n_fs):
        part = slice(owner * shard, (owner + 1) * shard)
        store(owner, 0, grad_wq[part])
        store(owner, shard, grad_wkv[0][part])
        store(owner, 2 * shard, grad_wkv[1][part])
    bias_query = jnp.sum(grad_queries.astype(f32), axis=0, keepdims=True)
    gvec_ref[...] = jnp.zeros_like(gvec_ref)
    for index, value in (
        (QUERY_B, bias_query),
        (VALUE_B, bias_value),
        (OUTPUT_B, bias_output),
        (SECOND_G, gain_second),
        (SECOND_B, bias_second),
        (RETURN_B, bias_return),
    ):
        gvec_ref[index : index + 1, :] = value
    for chunk in range(chunks):
        gvec_ref[HIDDEN_B + chunk : HIDDEN_B + chunk + 1, :] = hidden_rows[chunk]


def main_entry(dims, n_outs, n_scratch, *refs):
    n_fs = dims[0]
    sizes, tokens, normed, keys_in, cotangent, vec_ref = refs[:6]
    own = refs[6:11]
    mine = refs[11 : 11 + n_fs - 1]
    other = refs[11 + n_fs - 1 : 11 + 2 * n_fs - 2]
    outs = refs[11 + 2 * n_fs - 2 : 11 + 2 * n_fs - 2 + n_outs]
    scratch = refs[11 + 2 * n_fs - 2 + n_outs :]
    main_kernel(dims, sizes, tokens, normed, keys_in, cotangent, vec_ref, own, mine, other, outs, scratch)


def input_kernel(dims, sizes, tokens, middle, gnormed, patches, reduced, weight, vec_ref, gvec, *refs):
    n_fs, batches, row_dev, cols, dim, n_parts = dims
    parts = refs[:n_parts]
    grad_ref, keep_ref, send_ref, wide = refs[n_parts:]
    tok = row_dev * cols
    half_cols = cols // 2
    key_dev = tok // 4
    sp = lax.axis_index("sp")
    is_low = sp % 2 == 0
    half = dim // 2

    def vec(index):
        return vec_ref[index : index + 1, :]

    def part_sum():
        if n_parts == 1:
            total = parts[0][0].astype(f32)
            for index in range(1, parts[0].shape[0]):
                total = total + parts[0][index].astype(f32)
            return total
        total = parts[0][...].astype(f32)
        for part in parts[1:]:
            total = total + part[...].astype(f32)
        return total

    grad_key = part_sum()
    normal, rstd = normalize(reduced[...])
    grad_reduced = normalize_back(grad_key, normal, rstd, vec(KEYS_G))
    gain_keys = jnp.sum(grad_key * normal, axis=0, keepdims=True)
    bias_keys = jnp.sum(grad_key, axis=0, keepdims=True)
    grad_low = grad_reduced.astype(bf16)
    bias_reduce = jnp.sum(grad_low.astype(f32), axis=0, keepdims=True)
    gain_first = jnp.zeros((1, dim), f32)
    bias_first = jnp.zeros((1, dim), f32)
    for offset in range(4):
        grad_w = mm_tn(patches[:, offset * dim : (offset + 1) * dim], grad_low).astype(bf16)
        low, high = grad_w[:half], grad_w[half:]
        keep_ref[offset, :half] = jnp.where(is_low, low, high)
        send_ref[offset, :half] = jnp.where(is_low, high, low)
    for batch in range(batches):
        for offset in range(4):
            dr, dc = offset // 2, offset % 2
            back = mm_nt(grad_low[batch * key_dev : (batch + 1) * key_dev], weight[offset])
            for row in range(row_dev // 2):
                for part in range(dim // 128):
                    wide[part, pl.ds((2 * row + dr) * cols + dc, half_cols, stride=2), :] = back[
                        row * half_cols : (row + 1) * half_cols, part * 128 : (part + 1) * 128
                    ]
        mask = token_mask(sp * row_dev, row_dev, cols, dim, sizes[batch, 0, 0], sizes[batch, 0, 1])
        rows = slice(batch * tok, (batch + 1) * tok)
        spread = jnp.concatenate([wide[part] for part in range(dim // 128)], axis=1)
        grad_normed = gnormed[rows] + spread * mask
        x = tokens[batch, 0].reshape(tok, dim).astype(f32)
        normal, rstd = normalize(x)
        grad_x = middle[rows] + normalize_back(grad_normed, normal, rstd, vec(FIRST_G))
        grad_ref[batch, 0] = grad_x.reshape(row_dev, cols, dim)
        gain_first = gain_first + jnp.sum(grad_normed * normal, axis=0, keepdims=True)
        bias_first = bias_first + jnp.sum(grad_normed, axis=0, keepdims=True)
    index = lax.broadcasted_iota(jnp.int32, (VECS, dim), 0)
    vectors = gvec[...]
    for place, value in (
        (FIRST_G, gain_first),
        (FIRST_B, bias_first),
        (REDUCE_B, bias_reduce),
        (KEYS_G, gain_keys),
        (KEYS_B, bias_keys),
    ):
        vectors = jnp.where(index == place, value, vectors)
    vectors = vectors.astype(bf16)
    for owner in range(n_fs):
        keep_ref[owner, half:] = vectors
        send_ref[owner, half:] = vectors


def add_kernel(axis, n, keep, arrived, *outs):
    if axis == "fs":
        me = lax.axis_index("fs")
        places = [lax.rem(me + step, n) for step in range(n)]
    else:
        me = lax.axis_index("sp") // 2
        places = [me ^ step for step in range(n)]
    for place, out in zip(places, outs):
        out[...] = (keep[place].astype(f32) + arrived[place].astype(f32)).astype(out.dtype)


def add_chunks(axis, keep, arrived):
    n = keep.shape[0]
    shape = jax.ShapeDtypeStruct(keep.shape[1:], keep.dtype)
    return pl.pallas_call(
        functools.partial(add_kernel, axis, n),
        out_shape=[shape] * n,
        compiler_params=pltpu.CompilerParams(vmem_limit_bytes=VMEM_LIMIT),
    )(keep, arrived)


def final_kernel(dims, lo_a, hi_a, lo_b, hi_b, *outs):
    n_fs, dim = dims
    shard = dim // n_fs
    is_low = lax.axis_index("sp") % 2 == 0
    fs = lax.axis_index("fs")
    a, b = lo_a[...], hi_a[...]
    low = jnp.where(is_low, a, b).astype(f32)
    high = jnp.where(is_low, b, a).astype(f32)
    query_w, keyval_w, output_w, hidden_w, return_w, reduce_w, vectors = outs
    query_w[...] = low[:shard]
    keyval_w[:, :dim] = low[shard : 2 * shard]
    keyval_w[:, dim:] = low[2 * shard : 3 * shard]
    output_w[...] = low[3 * shard : 4 * shard]
    hidden_w[:, :dim] = low[4 * shard : 5 * shard]
    hidden_w[:, dim : 2 * dim] = low[5 * shard :]
    hidden_w[:, 2 * dim : 3 * dim] = high[:shard]
    hidden_w[:, 3 * dim :] = high[shard : 2 * shard]
    return_w[...] = high[2 * shard :]
    a, b = lo_b[...], hi_b[...]
    low = jnp.where(is_low, a, b).astype(f32)
    high = jnp.where(is_low, b, a).astype(f32)
    half = dim // 2
    reduce_w[:half] = low[:half]
    reduce_w[half:] = high[:half]
    vecs = low[half:]
    lane = lax.broadcasted_iota(jnp.int32, vecs.shape, 1)
    chosen = jnp.where(lane // shard == fs, vecs, 0.0)
    folded = chosen[:, :shard]
    for index in range(1, n_fs):
        folded = folded + chosen[:, index * shard : (index + 1) * shard]
    vectors[:, :shard] = folded
    row = lax.broadcasted_iota(jnp.int32, vecs.shape, 0)
    vectors[0:1, dim:] = jnp.sum(jnp.where(row == HIDDEN_B + fs, vecs, 0.0), axis=0, keepdims=True)


def rotate(value, n, step):
    return lax.ppermute(value, "fs", [(i, (i + step) % n) for i in range(n)])


def flip(value, n, bits):
    return lax.ppermute(value, "sp", [(i, i ^ bits) for i in range(n)])


def sum_over_rows(value, n_sp):
    bit = 2
    while bit < n_sp:
        if 2 * bit < n_sp:
            a, b, c = flip(value, n_sp, bit), flip(value, n_sp, 2 * bit), flip(value, n_sp, 3 * bit)
            value = (
                (value.astype(f32) + a.astype(f32)) + (b.astype(f32) + c.astype(f32))
            ).astype(value.dtype)
            bit = 4 * bit
        else:
            a = flip(value, n_sp, bit)
            value = (value.astype(f32) + a.astype(f32)).astype(value.dtype)
            bit = 2 * bit
    return value


def reduce_shards(keep, send, n_fs, n_sp):
    parts = add_chunks("fs", keep, flip(send, n_sp, 1))
    arrived = [rotate(parts[step], n_fs, step) for step in range(1, n_fs)]
    total = parts[0].astype(f32)
    for piece in arrived:
        total = total + piece.astype(f32)
    mine = sum_over_rows(total.astype(bf16), n_sp)
    return mine, flip(mine, n_sp, 1)


def on_device(
    n_fs,
    n_sp,
    tokens,
    cotangent,
    image_sizes,
    first_gain,
    first_bias,
    query_weight,
    query_bias,
    reduce_weight,
    reduce_bias,
    keys_gain,
    keys_bias,
    keyval_weight,
    value_bias,
    output_weight,
    output_bias,
    second_gain,
    second_bias,
    hidden_weight,
    hidden_bias,
    return_weight,
    return_bias,
):
    batches, _, row_dev, cols, dim = tokens.shape
    hid = hidden_weight.shape[1]
    tok = row_dev * cols
    key_dev = tok // 4
    keys = n_sp * key_dev
    shard = dim // n_fs
    half = dim // 2
    fs = lax.axis_index("fs")
    core = lax.axis_index("sp") % 2
    vmem = pl.BlockSpec(memory_space=pltpu.VMEM)
    smem = pl.BlockSpec(memory_space=pltpu.SMEM)
    params = pltpu.CompilerParams(vmem_limit_bytes=VMEM_LIMIT)

    def shape(*dims, dtype=bf16):
        return jax.ShapeDtypeStruct(dims, dtype)

    small = jnp.stack(
        [
            first_gain,
            first_bias,
            query_bias,
            reduce_bias,
            keys_gain,
            keys_bias,
            value_bias,
            output_bias,
            second_gain,
            second_bias,
            return_bias,
        ]
    )
    lane = jnp.arange(dim, dtype=jnp.int32)[None, :]
    small = jnp.where(lane // shard == fs, jnp.tile(small, (1, n_fs)), jnp.zeros((), bf16))
    row = jnp.arange(VECS - HIDDEN_B, dtype=jnp.int32)[:, None]
    wide = jnp.where(row == fs, hidden_bias[None, :], jnp.zeros((), bf16))
    own_vec = jnp.concatenate([small, wide], axis=0)

    first_half = jnp.concatenate(
        [lax.dynamic_slice_in_dim(reduce_weight, core * half, half, 0), own_vec], axis=0
    )
    mine_first = [rotate(first_half, n_fs, step) for step in range(1, n_fs)]
    other_first = [flip(piece, n_sp, 1) for piece in mine_first]

    packed = jnp.concatenate(
        [query_weight]
        + [keyval_weight[:, j * dim : (j + 1) * dim] for j in range(2)]
        + [output_weight]
        + [hidden_weight[:, j * dim : (j + 1) * dim] for j in range(hid // dim)]
        + [return_weight],
        axis=0,
    )
    second_half = lax.dynamic_slice_in_dim(packed, core * (3 * half), 3 * half, 0)
    mine_second = [rotate(second_half, n_fs, step) for step in range(1, n_fs)]
    other_second = [flip(piece, n_sp, 1) for piece in mine_second]

    normed, patches, reduced, key_low, whole_reduce, vec = pl.pallas_call(
        functools.partial(reduce_kernel, (n_fs, batches, row_dev, cols, dim)),
        out_shape=[
            shape(batches * tok, dim),
            shape(batches * key_dev, 4 * dim),
            shape(batches * key_dev, dim, dtype=f32),
            shape(batches * key_dev, dim),
            shape(n_fs, dim, dim),
            shape(VECS, dim, dtype=f32),
        ],
        in_specs=[smem] + [vmem] * (3 + 2 * (n_fs - 1)),
        out_specs=[vmem] * 6,
        scratch_shapes=[pltpu.VMEM((dim // 128, tok, 128), f32)],
        compiler_params=params,
    )(image_sizes, tokens, reduce_weight, own_vec, *mine_first, *other_first)

    keys_all = lax.all_gather(key_low, "sp")

    single = keys <= KEY_BLOCK
    split = n_sp == 8
    tiny = (8, 128)
    gkey_shapes = (
        [shape(n_sp // 2, batches * key_dev, dim)] * 2
        if split
        else [shape(n_sp, batches * key_dev, dim), shape(16, 128)]
    )
    out_shapes = (
        [
            shape(batches, 1, row_dev, cols, dim, dtype=f32),
            shape(batches * tok, dim, dtype=f32),
            shape(batches * tok, dim, dtype=f32),
        ]
        + gkey_shapes
        + [shape(n_fs, 3 * half, dim)] * 2
        + [shape(VECS, dim, dtype=f32)]
    )
    scratch = [
        pltpu.VMEM((dim, dim), bf16),
        pltpu.VMEM((dim, 2 * dim), bf16),
        pltpu.VMEM((dim, dim), bf16),
        pltpu.VMEM((dim, hid), bf16),
        pltpu.VMEM((hid, dim), bf16),
        pltpu.VMEM((batches * tok, dim), bf16),
        pltpu.VMEM((batches, keys, 2 * dim), bf16),
        pltpu.VMEM((batches * tok, dim), bf16),
        pltpu.VMEM(tiny, f32),
        pltpu.VMEM(tiny, f32),
        pltpu.VMEM(tiny, f32),
        pltpu.VMEM((batches, PAIRS, keys, 2 * tok) if single else (16, 128), bf16),
        pltpu.VMEM((batches, PAIRS, 8, 2 * tok), f32),
        pltpu.VMEM((batches * tok, dim), bf16),
        pltpu.VMEM((batches, dim, tok), f32),
        pltpu.VMEM((dim, tok), f32),
        pltpu.VMEM(tiny if single else (keys, dim), f32),
        pltpu.VMEM(tiny if single else (keys, dim), f32),
    ]
    n_in = 5 + 5 + 2 * (n_fs - 1)
    acts, middle, gnormed, gkey_keep, gkey_send, keep, send, gvec = pl.pallas_call(
        functools.partial(
            main_entry, (n_fs, n_sp, batches, row_dev, cols, dim, hid), len(out_shapes), len(scratch)
        ),
        out_shape=out_shapes,
        in_specs=[smem] + [vmem] * n_in,
        out_specs=[vmem] * len(out_shapes),
        scratch_shapes=scratch,
        compiler_params=params,
    )(
        image_sizes,
        tokens,
        normed,
        keys_all,
        cotangent,
        vec,
        query_weight,
        keyval_weight,
        output_weight,
        hidden_weight,
        return_weight,
        *mine_second,
        *other_second,
    )

    if split:
        pieces = add_chunks("sp", gkey_keep, flip(gkey_send, n_sp, 1))
        parts = [pieces[0]] + [flip(pieces[step], n_sp, 2 * step) for step in range(1, n_sp // 2)]
    else:
        parts = [lax.all_to_all(gkey_keep, "sp", 0, 0)]

    mine_a, other_a = reduce_shards(keep, send, n_fs, n_sp)

    grads, keep, send = pl.pallas_call(
        functools.partial(input_kernel, (n_fs, batches, row_dev, cols, dim, len(parts))),
        out_shape=[
            shape(batches, 1, row_dev, cols, dim, dtype=f32),
            shape(n_fs, half + VECS, dim),
            shape(n_fs, half + VECS, dim),
        ],
        in_specs=[smem] + [vmem] * (8 + len(parts)),
        out_specs=[vmem] * 3,
        scratch_shapes=[pltpu.VMEM((dim // 128, tok, 128), f32)],
        compiler_params=params,
    )(image_sizes, tokens, middle, gnormed, patches, reduced, whole_reduce, vec, gvec, *parts)

    mine_b, other_b = reduce_shards(keep, send, n_fs, n_sp)

    gquery, gkeyval, goutput, ghidden, greturn, greduce, gvecs = pl.pallas_call(
        functools.partial(final_kernel, (n_fs, dim)),
        out_shape=[
            shape(shard, dim, dtype=f32),
            shape(shard, 2 * dim, dtype=f32),
            shape(shard, dim, dtype=f32),
            shape(shard, hid, dtype=f32),
            shape(dim, dim, dtype=f32),
            shape(dim, dim, dtype=f32),
            shape(VECS, 2 * dim, dtype=f32),
        ],
        in_specs=[vmem] * 4,
        out_specs=[vmem] * 7,
        compiler_params=params,
    )(mine_a, other_a, mine_b, other_b)
    vectors = [gvecs[index, :shard] for index in range(HIDDEN_B)]
    return (
        acts,
        grads,
        vectors[FIRST_G],
        vectors[FIRST_B],
        gquery,
        vectors[QUERY_B],
        greduce,
        vectors[REDUCE_B],
        vectors[KEYS_G],
        vectors[KEYS_B],
        gkeyval,
        vectors[VALUE_B],
        goutput,
        vectors[OUTPUT_B],
        vectors[SECOND_G],
        vectors[SECOND_B],
        ghidden,
        gvecs[0, dim:],
        greturn,
        vectors[RETURN_B],
    )


def solution(mesh):
    vec, mat = P("fs"), P("fs", None)
    image = P(None, "fs", "sp", None, None)
    weights = (vec, vec, mat, vec, mat, vec, vec, vec, mat, vec, mat, vec, vec, vec, mat, vec, mat, vec)
    return jax.shard_map(
        functools.partial(on_device, mesh.shape["fs"], mesh.shape["sp"]),
        mesh=mesh,
        in_specs=(image, image, P(None, "fs", None)) + weights,
        out_specs=(image, image) + weights,
        check_vma=False,
    )
```

```python
import functools

import jax
import jax.numpy as jnp
from jax import lax
from jax.experimental import pallas as pl
from jax.experimental.pallas import tpu as pltpu
from jax.sharding import PartitionSpec as P

HEADS = 8
HDIM = 32
PAIRS = HEADS // 2
SCALE = HDIM ** (-0.5)
EXP_SCALE = SCALE * 1.4426950408889634
EPS = 1e-06
NEG = -1e30
KEY_BLOCK = 768
SMALL_VMEM = 12 * 2**20
MAIN_VMEM = 16 * 2**20
WHOLE_VMEM = 58 * 2**20

bf16 = jnp.bfloat16
f32 = jnp.float32

(
    FIRST_G,
    FIRST_B,
    QUERY_B,
    REDUCE_B,
    KEYS_G,
    KEYS_B,
    VALUE_B,
    OUTPUT_B,
    SECOND_G,
    SECOND_B,
    RETURN_B,
    HIDDEN_B,
) = range(12)
VECS = 16


def mm(left, right):
    return jnp.dot(left, right, preferred_element_type=f32)


def mm_tn(left, right):
    return lax.dot_general(left, right, (((0,), (0,)), ((), ())), preferred_element_type=f32)


def mm_nt(left, right):
    return lax.dot_general(left, right, (((1,), (1,)), ((), ())), preferred_element_type=f32)


def normalize(rows):
    mean = jnp.mean(rows, axis=-1, keepdims=True)
    centered = rows - mean
    var = jnp.mean(centered * centered, axis=-1, keepdims=True)
    rstd = lax.rsqrt(var + EPS)
    return centered * rstd, rstd


def normalize_back(grad, normal, rstd, gain):
    scaled = grad * gain
    mean_a = jnp.mean(scaled, axis=-1, keepdims=True)
    mean_b = jnp.mean(scaled * normal, axis=-1, keepdims=True)
    return (scaled - mean_a - normal * mean_b) * rstd


def token_mask(first_row, rows, cols, width, height, image_width):
    row_ids = lax.broadcasted_iota(jnp.int32, (rows, cols, width), 0) + first_row
    col_ids = lax.broadcasted_iota(jnp.int32, (rows, cols, width), 1)
    valid = (row_ids < height) & (col_ids < image_width)
    return jnp.where(valid, 1.0, 0.0).astype(f32).reshape(rows * cols, width)


def pack_first_kernel(n_fs, *refs):
    smalls, (hidden_b, reduce_w, query_w, keyval_w, first, wide) = take(refs, HIDDEN_B)
    dim = reduce_w.shape[1]
    shard = dim // n_fs
    half = dim // 2
    rest = half + VECS
    fs = lax.axis_index("fs")
    is_low = lax.axis_index("sp") % 2 == 0

    @pl.when(is_low)
    def _():
        first[:half] = reduce_w[:half]
        first[rest : rest + shard] = query_w[...]
        first[rest + shard :] = keyval_w[: shard // 2, :dim]

    @pl.when(jnp.logical_not(is_low))
    def _():
        first[:half] = reduce_w[half:]
        first[rest : rest + shard // 2] = keyval_w[shard // 2 :, :dim]
        first[rest + shard // 2 :] = keyval_w[:, dim:]

    wide[...] = jnp.zeros_like(wide)
    for index, small in enumerate(smalls):
        row = small[...].astype(f32).reshape(1, shard)
        wide[index : index + 1, :] = jnp.concatenate([row] * n_fs, axis=1)
    lane = lax.broadcasted_iota(jnp.int32, wide.shape, 1)
    row = lax.broadcasted_iota(jnp.int32, wide.shape, 0)
    vectors = jnp.where(lane // shard == fs, wide[...], 0.0)
    hidden_row = hidden_b[...].astype(f32).reshape(1, dim)
    first[half:rest] = jnp.where(row == HIDDEN_B + fs, hidden_row, vectors).astype(bf16)


def both_halves(mine, other):
    is_low = lax.axis_index("sp") % 2 == 0
    a, b = mine[...], other[...]
    return jnp.where(is_low, a, b), jnp.where(is_low, b, a)


def shard_rows(place, rows):
    return pl.ds(pl.multiple_of(place * rows, rows), rows)


def begin_kernel(dims, sizes, tokens, reduce_w, query_w, keyval_w, hidden_w, return_w, output_w, packed, *outs):
    n_sp, batches, row_dev, cols, dim = dims
    normal_ref, mask_ref, bias_ref, own_r, own_q, own_kv, own_vec, second = outs
    tok = row_dev * cols
    half_cols = cols // 2
    rows_dev = row_dev // 2
    half = dim // 2
    shard = hidden_w.shape[0]
    sp = lax.axis_index("sp")
    own_r[...] = reduce_w[...]
    own_q[...] = query_w[...]
    own_kv[...] = keyval_w[...]
    own_vec[...] = packed[half : half + VECS].astype(f32)

    @pl.when(sp % 2 == 0)
    def _():
        for chunk in range(hidden_w.shape[1] // dim):
            second[chunk * shard : (chunk + 1) * shard] = hidden_w[:, chunk * dim : (chunk + 1) * dim]
        second[dim:] = output_w[: shard // 2]

    @pl.when(sp % 2 == 1)
    def _():
        second[:dim] = return_w[...]
        second[dim:] = output_w[shard // 2 :]

    for batch in range(batches):
        height, image_width = sizes[batch, 0, 0], sizes[batch, 0, 1]
        rows = slice(batch * tok, (batch + 1) * tok)
        normal_ref[rows], _ = normalize(tokens[batch, 0].reshape(tok, dim).astype(f32))
        mask_ref[rows] = token_mask(sp * row_dev, row_dev, cols, dim, height, image_width)
        col_ids = lax.broadcasted_iota(jnp.int32, (half_cols, dim), 0)

        def key_row_bias(index, _, batch=batch, height=height, image_width=image_width, col_ids=col_ids):
            key_row = index
            if n_sp == 8:
                key_row = (sp ^ (index // rows_dev)) * rows_dev + lax.rem(index, rows_dev)
            width = jnp.where(2 * key_row < height, image_width, 0)
            here = pl.ds(pl.multiple_of(index * half_cols, half_cols), half_cols)
            bias_ref[batch, here, :] = jnp.where(2 * col_ids < width, 0.0, NEG).astype(bf16)
            return 0

        lax.fori_loop(0, n_sp * rows_dev, key_row_bias, 0)


def reduce_kernel(dims, *refs):
    n_fs, batches, row_dev, cols, dim = dims
    ins, mine, other, outs = take(refs, 7, n_fs - 1, n_fs - 1)
    normal_in, mask_ref, own_w, own_q, own_kv, own_vec, second_in = ins
    normed_ref, patch_ref, reduced_ref, key_ref, weight_ref, wq, wkv, vec_ref, second, wide = outs
    half = dim // 2
    shard = dim // n_fs
    rest = half + VECS
    tok = row_dev * cols
    half_cols = cols // 2
    key_dev = tok // 4
    fs = lax.axis_index("fs")
    second[...] = second_in[...]
    weight_ref[fs] = own_w[...]
    here = shard_rows(fs, shard)
    wq[here, :] = own_q[...]
    wkv[here, :] = own_kv[...]
    vec = own_vec[...]
    for step in range(1, n_fs):
        low, high = both_halves(mine[step - 1], other[step - 1])
        place = lax.rem(fs + n_fs - step, n_fs)
        weight_ref[place, :half] = low[:half]
        weight_ref[place, half:] = high[:half]
        vec = vec + low[half:rest].astype(f32)
        here = shard_rows(place, shard)
        wq[here, :] = low[rest : rest + shard]
        wkv[here, :dim] = jnp.concatenate([low[rest + shard :], high[rest : rest + shard // 2]], axis=0)
        wkv[here, dim:] = high[rest + shard // 2 :]
    vec_ref[...] = vec
    for batch in range(batches):
        rows = slice(batch * tok, (batch + 1) * tok)
        low = (normal_in[rows] * vec[FIRST_G : FIRST_G + 1] + vec[FIRST_B : FIRST_B + 1]).astype(bf16)
        normed_ref[rows] = low
        masked = low.astype(f32) * mask_ref[rows]
        for part in range(dim // 128):
            wide[part] = masked[:, part * 128 : (part + 1) * 128]
        for row in range(row_dev // 2):
            start = batch * key_dev + row * half_cols
            for offset in range(4):
                dr, dc = offset // 2, offset % 2
                for part in range(dim // 128):
                    piece = wide[part, pl.ds((2 * row + dr) * cols + dc, half_cols, stride=2), :]
                    lanes = slice(offset * dim + part * 128, offset * dim + (part + 1) * 128)
                    patch_ref[start : start + half_cols, lanes] = piece.astype(bf16)
    reduced = mm(patch_ref[...], weight_ref[...].reshape(4 * dim, dim)) + vec[REDUCE_B : REDUCE_B + 1]
    reduced_ref[...] = reduced
    normal, _ = normalize(reduced)
    key_ref[...] = (normal * vec[KEYS_G : KEYS_G + 1] + vec[KEYS_B : KEYS_B + 1]).astype(bf16)


def relay_kernel(n, *refs):
    for source, target in zip(refs[:n], refs[n + 1 :]):
        target[...] = source[...]


def head_stack_t(values_t, pair, tok):
    both = jnp.concatenate([values_t, values_t], axis=1)
    head = lax.broadcasted_iota(jnp.int32, both.shape, 0) // HDIM
    want = 2 * pair + jnp.where(lax.broadcasted_iota(jnp.int32, both.shape, 1) >= tok, 1, 0)
    return jnp.where(head == want, both, jnp.zeros_like(both))


def head_stack(values, pair):
    head = lax.broadcasted_iota(jnp.int32, values.shape, 1) // HDIM
    zero = jnp.zeros_like(values)
    return jnp.concatenate(
        [jnp.where(head == 2 * pair, values, zero), jnp.where(head == 2 * pair + 1, values, zero)],
        axis=0,
    )


def split_pair(both, tok):
    return jnp.concatenate([both[:HDIM, :tok], both[HDIM:, tok:]], axis=0)


def key_rows_of(pieces, key_dev, per_block, batch, index):
    here = slice(batch * key_dev, (batch + 1) * key_dev)
    if len(pieces) > 1:
        return jnp.concatenate([part[here] for part in pieces], axis=0)
    dim = pieces[0].shape[2]
    devices = slice(index * per_block, (index + 1) * per_block)
    return pieces[0][devices, here, :].reshape(per_block * key_dev, dim)


def mask_lane(pair, dim):
    return 0 if pair == PAIRS - 1 else dim - 1


def with_bias(key_block, bias, lane_id):
    lane = lax.broadcasted_iota(jnp.int32, key_block.shape, 1)
    return jnp.where(lane == lane_id, bias.astype(f32), key_block.astype(f32)).astype(bf16)


def query_stack(queries_t, pair, lane_id, tok):
    stacked = head_stack_t(queries_t, pair, tok)
    row = lax.broadcasted_iota(jnp.int32, stacked.shape, 0)
    return jnp.where(row == lane_id, jnp.ones_like(stacked), stacked)


def take(refs, *counts):
    refs = list(refs)
    groups = []
    for count in counts:
        groups.append(refs[:count])
        refs = refs[count:]
    return groups + [refs]


def forward_kernel(dims, *refs):
    batches, tok, key_dev, keys, block, n_pieces = dims
    (normed, vec_ref, bias_ref, wq, wkv), pieces, (attended, *kept) = take(refs, 5, n_pieces)
    queries_out, kvs, attf, stats, probs = (
        kept[index * batches : (index + 1) * batches] for index in range(5)
    )
    dim = wq.shape[0]
    blocks = keys // block
    per_block = block // key_dev
    for batch in range(batches):
        rows = slice(batch * tok, (batch + 1) * tok)
        queries = (mm(normed[rows], wq[...]) + vec_ref[QUERY_B : QUERY_B + 1]).astype(bf16)
        queries_out[batch][...] = queries
        queries_t = queries.T
        for index in range(blocks):
            key_rows = key_rows_of(pieces, key_dev, per_block, batch, index)
            here = slice(index * block, (index + 1) * block)
            kvs[batch][here, :dim] = mm(key_rows, wkv[:, :dim]).astype(bf16)
            value_rows = mm(key_rows, wkv[:, dim:]) + vec_ref[VALUE_B : VALUE_B + 1]
            kvs[batch][here, dim:] = value_rows.astype(bf16)
        if blocks == 1:
            key_block = kvs[batch][:, :dim]
            values_t = kvs[batch][:, dim:].T
            bias = bias_ref[batch]
            masked = {lane_id: with_bias(key_block, bias, lane_id) for lane_id in (0, dim - 1)}
            for pair in range(PAIRS):
                lane_id = mask_lane(pair, dim)
                heads = slice(2 * HDIM * pair, 2 * HDIM * (pair + 1))
                scores = mm(masked[lane_id], query_stack(queries_t, pair, lane_id, tok))
                top = jnp.max(scores, axis=0, keepdims=True)
                weights = jnp.exp2((scores - top) * EXP_SCALE)
                inverse = 1.0 / jnp.sum(weights, axis=0, keepdims=True)
                low = weights.astype(bf16)
                probs[batch][pair] = low
                stats[batch][pair, 0:1] = inverse
                mixed = mm(values_t[heads], low) * inverse
                attf[batch][heads] = split_pair(mixed, tok)
        else:
            for pair in range(PAIRS):
                lane_id = mask_lane(pair, dim)
                heads = slice(2 * HDIM * pair, 2 * HDIM * (pair + 1))
                stacked = query_stack(queries_t, pair, lane_id, tok)

                def block_scores(index, stacked=stacked, lane_id=lane_id, batch=batch):
                    here = pl.ds(pl.multiple_of(index * block, block), block)
                    masked = with_bias(kvs[batch][here, :dim], bias_ref[batch, here, :], lane_id)
                    return here, mm(masked, stacked)

                def find_top(index, top, block_scores=block_scores):
                    _, scores = block_scores(index)
                    return jnp.maximum(top, jnp.max(scores, axis=0, keepdims=True))

                top = lax.fori_loop(0, blocks, find_top, jnp.full((1, 2 * tok), 4 * NEG, f32))

                def add_block(index, carry, block_scores=block_scores, top=top, heads=heads, batch=batch):
                    total, mixed = carry
                    here, scores = block_scores(index)
                    weights = jnp.exp2((scores - top) * EXP_SCALE)
                    values_t = kvs[batch][here, dim:].T
                    mixed = mixed + mm(values_t[heads], weights.astype(bf16))
                    return total + jnp.sum(weights, axis=0, keepdims=True), mixed

                start = (jnp.zeros((1, 2 * tok), f32), jnp.zeros((2 * HDIM, 2 * tok), f32))
                total, mixed = lax.fori_loop(0, blocks, add_block, start)
                inverse = 1.0 / total
                stats[batch][pair, 0:1] = inverse
                stats[batch][pair, 1:2] = top
                attf[batch][heads] = split_pair(mixed * inverse, tok)
        attended[rows] = attf[batch][...].T.astype(bf16)


def mlp_kernel(dims, *refs):
    n_fs, batches, row_dev, cols, dim, hid = dims
    ins, own, mine, other, outs, scratch = take(refs, 5, 3, n_fs - 1, n_fs - 1, 7)
    tokens, cotangent, mask_ref, attended, vec_ref = ins
    acts_ref, normal_ref, rstd_ref, grad_ref, keep_ref, send_ref, wo = outs
    wh, wr, bias_rows = scratch
    tok = row_dev * cols
    shard = dim // n_fs
    chunks = hid // dim
    fs = lax.axis_index("fs")
    is_low = lax.axis_index("sp") % 2 == 0
    wh[shard_rows(fs, shard), :] = own[0][...]
    wr[shard_rows(fs, dim), :] = own[1][...]
    wo[shard_rows(fs, shard), :] = own[2][...]
    for step in range(1, n_fs):
        low, high = both_halves(mine[step - 1], other[step - 1])
        place = lax.rem(fs + n_fs - step, n_fs)
        here = shard_rows(place, shard)
        for chunk in range(chunks):
            wh[here, chunk * dim : (chunk + 1) * dim] = low[chunk * shard : (chunk + 1) * shard]
        wr[shard_rows(place, dim), :] = high[:dim]
        wo[here, :] = jnp.concatenate([low[dim:], high[dim:]], axis=0)

    def vec(index):
        return vec_ref[index : index + 1, :]

    def store(low_half, owner, start, value):
        value = value.astype(bf16)
        here = slice(start, start + value.shape[0])
        keep = is_low if low_half else jnp.logical_not(is_low)

        @pl.when(keep)
        def _():
            keep_ref[owner, here, :] = value

        @pl.when(jnp.logical_not(keep))
        def _():
            send_ref[owner, here, :] = value

    x = jnp.concatenate([tokens[b, 0].reshape(tok, dim).astype(f32) for b in range(batches)], axis=0)
    mask = mask_ref[...]
    middle = x + mm(attended[...], wo[...]) + vec(OUTPUT_B)
    normal, rstd = normalize(middle)
    normal_ref[...] = normal
    rstd_ref[...] = jnp.broadcast_to(rstd, rstd_ref.shape)
    second = (normal * vec(SECOND_G) + vec(SECOND_B)).astype(bf16)
    grad_out = jnp.concatenate([cotangent[b, 0].reshape(tok, dim) for b in range(batches)], axis=0) * mask
    grad_mlp = grad_out.astype(bf16)
    total = middle + vec(RETURN_B)
    grad_second = jnp.zeros((batches * tok, dim), f32)
    bias_rows[...] = jnp.zeros_like(bias_rows)
    for chunk in range(chunks):
        lanes = slice(chunk * dim, (chunk + 1) * dim)
        hidden = mm(second, wh[:, lanes]) + vec(HIDDEN_B + chunk)
        phi = 0.5 + 0.5 * lax.erf(hidden * 0.7071067811865476)
        density = 0.3989422804014327 * jnp.exp2(hidden * hidden * (-0.5 * 1.4426950408889634))
        activated = (hidden * phi).astype(bf16)
        total = total + mm(activated, wr[lanes, :])
        grad_activated = mm_nt(grad_mlp, wr[lanes, :])
        grad_hidden = ((phi + hidden * density) * grad_activated).astype(bf16)
        bias_rows[chunk : chunk + 1] = jnp.sum(grad_hidden.astype(f32), axis=0, keepdims=True)
        grad_second = grad_second + mm_nt(grad_hidden, wh[:, lanes])
        store(False, chunk, 0, mm_tn(activated, grad_mlp))
        grad_wh = mm_tn(second, grad_hidden)
        for owner in range(n_fs):
            store(True, owner, chunk * shard, grad_wh[owner * shard : (owner + 1) * shard])
    total = total * mask
    for batch in range(batches):
        acts_ref[batch, 0] = total[batch * tok : (batch + 1) * tok].reshape(row_dev, cols, dim)
    rows = batches * tok
    grad_ref[:rows] = grad_second
    grad_ref[rows:] = bias_rows[...]


def middle_kernel(dims, cotangent, mask_ref, normal_ref, rstd_ref, grad_ref, vec_ref, wo, middle_ref, gatt, gvec_ref):
    batches, tok, chunks = dims
    dim = wo.shape[0]
    rows = batches * tok
    grad_out = jnp.concatenate([cotangent[b, 0].reshape(tok, dim) for b in range(batches)], axis=0)
    grad_out = grad_out * mask_ref[...]
    grad_second, normal = grad_ref[:rows], normal_ref[...]
    rstd = jnp.concatenate([rstd_ref[...]] * (dim // rstd_ref.shape[1]), axis=1)
    back = normalize_back(grad_second, normal, rstd, vec_ref[SECOND_G : SECOND_G + 1])
    grad_middle = grad_out + back
    middle_ref[...] = grad_middle
    grad_branch = grad_middle.astype(bf16)
    gatt[...] = mm_nt(grad_branch, wo[...]).astype(bf16)
    gvec_ref[...] = jnp.zeros_like(gvec_ref)
    for index, value in (
        (OUTPUT_B, grad_branch.astype(f32)),
        (SECOND_G, grad_second * normal),
        (SECOND_B, grad_second),
        (RETURN_B, grad_out.astype(bf16).astype(f32)),
    ):
        gvec_ref[index : index + 1] = jnp.sum(value, axis=0, keepdims=True)
    gvec_ref[HIDDEN_B : HIDDEN_B + chunks] = grad_ref[rows : rows + chunks]


def backward_kernel(dims, *refs):
    n_fs, n_sp, batch, last, tok, key_dev, keys, block, n_pieces, batches = dims
    ins, pieces, more, refs = take(refs, 8, n_pieces, 8 if last else 0)
    gatt, queries_ref, kvs, attf, stats, probs, bias_ref, wkv = ins
    if last:
        first_gq, first_gkv, first_gvec, normed, wq, attended, middle, _ = more
        keep_ref, send_ref, gnormed_ref, near_ref, far_ref, gvec_ref = refs[:6]
        gqs, gks, gvs = refs[6:]
    else:
        gq_ref, gkv_ref, gvec_ref, near_ref, far_ref = refs[:5]
        gqs, gks, gvs = refs[5:]
    dim = wkv.shape[0]
    shard = dim // n_fs
    blocks = keys // block
    per_block = block // key_dev
    rows = slice(batch * tok, (batch + 1) * tok)
    queries = queries_ref[...]
    grad_att_t = gatt[rows].astype(f32).T
    product = grad_att_t * attf[...]

    def pair_terms(pair):
        inverse = stats[pair, 0:1]
        piece = product[2 * HDIM * pair : 2 * HDIM * (pair + 1)]
        delta = jnp.concatenate(
            [jnp.sum(piece[:HDIM], axis=0, keepdims=True), jnp.sum(piece[HDIM:], axis=0, keepdims=True)],
            axis=1,
        )
        stacked = head_stack_t(grad_att_t, pair, tok) * inverse
        return delta * inverse, stacked.astype(bf16)

    if blocks == 1:
        keys_t = kvs[:, :dim].T
        values = kvs[:, dim:]
        grad_k = jnp.zeros((keys, dim), f32)
        grad_v = jnp.zeros((keys, dim), f32)
        for pair in range(PAIRS):
            heads = slice(2 * HDIM * pair, 2 * HDIM * (pair + 1))
            delta, stacked = pair_terms(pair)
            low = probs[pair]
            grad_probs = mm(values, stacked)
            grad_scores = (low.astype(f32) * (grad_probs - delta)).astype(bf16)
            gqs[heads] = split_pair(mm(keys_t[heads], grad_scores), tok)
            grad_k = grad_k + mm(grad_scores, head_stack(queries, pair))
            grad_v = grad_v + mm(low, stacked.T)
    else:
        gks[...] = jnp.zeros_like(gks)
        gvs[...] = jnp.zeros_like(gvs)
        queries_t = queries.T
        for pair in range(PAIRS):
            heads = slice(2 * HDIM * pair, 2 * HDIM * (pair + 1))
            lane_id = mask_lane(pair, dim)
            delta, stacked = pair_terms(pair)
            stacked_n = stacked.T
            query_t = query_stack(queries_t, pair, lane_id, tok)
            query_n = head_stack(queries, pair)
            top = stats[pair, 1:2]

            def back_block(index, gq, heads=heads, lane_id=lane_id, delta=delta, stacked=stacked, stacked_n=stacked_n, query_t=query_t, query_n=query_n, top=top):
                here = pl.ds(pl.multiple_of(index * block, block), block)
                key_block = kvs[here, :dim]
                masked = with_bias(key_block, bias_ref[batch, here, :], lane_id)
                weights = jnp.exp2((mm(masked, query_t) - top) * EXP_SCALE)
                grad_probs = mm(kvs[here, dim:], stacked)
                grad_scores = (weights * (grad_probs - delta)).astype(bf16)
                gks[here, :] += mm(grad_scores, query_n)
                gvs[here, :] += mm(weights.astype(bf16), stacked_n)
                return gq + mm(key_block.T[heads], grad_scores)

            gq = lax.fori_loop(0, blocks, back_block, jnp.zeros((2 * HDIM, 2 * tok), f32))
            gqs[heads] = split_pair(gq, tok)
    grad_queries = (gqs[...].T * SCALE).astype(bf16)
    grad_wk = jnp.zeros((dim, dim), f32)
    grad_wv = jnp.zeros((dim, dim), f32)
    bias_value = jnp.zeros((1, dim), f32)
    for index in range(blocks):
        if blocks > 1:
            here = slice(index * block, (index + 1) * block)
            grad_k, grad_v = gks[here], gvs[here]
        grad_k = (grad_k * SCALE).astype(bf16)
        bias_value = bias_value + jnp.sum(grad_v, axis=0, keepdims=True)
        grad_v = grad_v.astype(bf16)
        grad_key = (mm_nt(grad_k, wkv[:, :dim]) + mm_nt(grad_v, wkv[:, dim:])).astype(bf16)
        if n_pieces > 1:
            pairs = grad_key.reshape(n_sp // 2, 2, key_dev, dim)
            near_ref[...] = pairs[:, 0]
            far_ref[...] = pairs[:, 1]
        else:
            near_ref[index * per_block : (index + 1) * per_block] = grad_key.reshape(per_block, key_dev, dim)
        key_rows = key_rows_of(pieces, key_dev, per_block, batch, index)
        grad_wk = grad_wk + mm_tn(key_rows, grad_k)
        grad_wv = grad_wv + mm_tn(key_rows, grad_v)
    if not last:
        gq_ref[...] = grad_queries
        gkv_ref[:, :dim] = grad_wk
        gkv_ref[:, dim:] = grad_wv
        gvec_ref[...] = jnp.zeros_like(gvec_ref)
        gvec_ref[0:1] = bias_value
        return
    is_low = lax.axis_index("sp") % 2 == 0
    grad_wk = grad_wk + first_gkv[:, :dim]
    grad_wv = grad_wv + first_gkv[:, dim:]
    bias_value = bias_value + first_gvec[0:1]
    grad_queries = jnp.concatenate([first_gq[...], grad_queries], axis=0)
    grad_wq = mm_tn(normed[...], grad_queries)
    grad_wo = mm_tn(attended[...], middle[...].astype(bf16))
    for owner in range(n_fs):
        part = slice(owner * shard, (owner + 1) * shard)
        low = jnp.concatenate([grad_wq[part], grad_wk[part]], axis=0).astype(bf16)
        high = jnp.concatenate([grad_wv[part], grad_wo[part]], axis=0).astype(bf16)
        keep_ref[owner] = jnp.where(is_low, low, high)
        send_ref[owner] = jnp.where(is_low, high, low)
    gnormed_ref[...] = mm_nt(grad_queries, wq[...])
    gvec_ref[...] = jnp.zeros_like(gvec_ref)
    gvec_ref[QUERY_B : QUERY_B + 1] = jnp.sum(grad_queries.astype(f32), axis=0, keepdims=True)
    gvec_ref[VALUE_B : VALUE_B + 1] = bias_value


def sum_parts(parts):
    if len(parts) == 1:
        total = parts[0][0].astype(f32)
        for index in range(1, parts[0].shape[0]):
            total = total + parts[0][index].astype(f32)
        return total
    total = parts[0][...].astype(f32)
    for part in parts[1:]:
        total = total + part[...].astype(f32)
    return total


def reduction_kernel(n_parts, n_fs, patches, reduced, vec_ref, *refs):
    parts = refs[:n_parts]
    grad_ref, gvec_ref, keep_ref, send_ref = refs[-4:]
    dim = reduced.shape[1]
    half = dim // 2
    is_low = lax.axis_index("sp") % 2 == 0
    grad_key = sum_parts(parts)
    normal, rstd = normalize(reduced[...])
    grad_low = normalize_back(grad_key, normal, rstd, vec_ref[KEYS_G : KEYS_G + 1]).astype(bf16)
    grad_ref[...] = grad_low
    for owner in range(n_fs):
        grad_w = mm_tn(patches[:, owner * dim : (owner + 1) * dim], grad_low).astype(bf16)
        low, high = grad_w[:half], grad_w[half:]
        keep_ref[owner] = jnp.where(is_low, low, high)
        send_ref[owner] = jnp.where(is_low, high, low)
    gvec_ref[...] = jnp.zeros_like(gvec_ref)
    for index, value in (
        (REDUCE_B, grad_low.astype(f32)),
        (KEYS_G, grad_key * normal),
        (KEYS_B, grad_key),
    ):
        gvec_ref[index : index + 1] = jnp.sum(value, axis=0, keepdims=True)


def input_kernel(dims, tokens, middle, gnormed, mask_ref, grad_reduced, weight, vec_ref, vec_a, vec_b, vec_c, grad_ref, gvec_ref, wide):
    batches, row_dev, cols, dim = dims
    tok = row_dev * cols
    half_cols = cols // 2
    key_dev = tok // 4
    gain_first = jnp.zeros((1, dim), f32)
    bias_first = jnp.zeros((1, dim), f32)
    for batch in range(batches):
        for offset in range(4):
            dr, dc = offset // 2, offset % 2
            back = mm_nt(grad_reduced[batch * key_dev : (batch + 1) * key_dev], weight[offset])
            for row in range(row_dev // 2):
                for part in range(dim // 128):
                    wide[part, pl.ds((2 * row + dr) * cols + dc, half_cols, stride=2), :] = back[
                        row * half_cols : (row + 1) * half_cols, part * 128 : (part + 1) * 128
                    ]
        rows = slice(batch * tok, (batch + 1) * tok)
        spread = jnp.concatenate([wide[part] for part in range(dim // 128)], axis=1)
        grad_normed = gnormed[rows] + spread * mask_ref[rows]
        x = tokens[batch, 0].reshape(tok, dim).astype(f32)
        normal, rstd = normalize(x)
        grad_x = middle[rows] + normalize_back(grad_normed, normal, rstd, vec_ref[FIRST_G : FIRST_G + 1])
        grad_ref[batch, 0] = grad_x.reshape(row_dev, cols, dim)
        gain_first = gain_first + jnp.sum(grad_normed * normal, axis=0, keepdims=True)
        bias_first = bias_first + jnp.sum(grad_normed, axis=0, keepdims=True)
    index = lax.broadcasted_iota(jnp.int32, (VECS, dim), 0)
    vectors = vec_a[...] + vec_b[...] + vec_c[...]
    vectors = jnp.where(index == FIRST_G, gain_first, vectors)
    vectors = jnp.where(index == FIRST_B, bias_first, vectors)
    gvec_ref[...] = vectors.astype(bf16)


def key_sum_kernel(batches, *refs):
    near, far, outs = take(refs, batches, batches)
    for step, out in enumerate(outs):
        rows = near[0].shape[1]
        for batch in range(batches):
            total = near[batch][step].astype(f32) + far[batch][step].astype(f32)
            out[batch * rows : (batch + 1) * rows] = total.astype(out.dtype)


def owner_kernel(n, tail, keep, arrived, *refs):
    fs = lax.axis_index("fs")
    outs = refs[tail:]
    rows = keep.shape[1]
    for step, out in enumerate(outs):
        place = lax.rem(fs + step, n)
        out[:rows] = (keep[place].astype(f32) + arrived[place].astype(f32)).astype(out.dtype)
        if tail:
            out[rows:] = refs[0][...]


def chip_kernel(keep, arrived, *outs):
    chip = lax.axis_index("sp") // 2
    rows = outs[0].shape[1]
    for step, out in enumerate(outs):
        here = shard_rows(chip ^ step, rows)
        out[...] = (keep[:, here, :].astype(f32) + arrived[:, here, :].astype(f32)).astype(out.dtype)


def chip_sum_kernel(*refs):
    refs[-1][...] = sum_parts(refs[:-1]).astype(refs[-1].dtype)


def owners_kernel(total, keep, arrived, *outs):
    fs = lax.axis_index("fs")
    rows = total.shape[1]
    for step, out in enumerate(outs):
        place = lax.rem(fs + step, len(outs))
        out[:rows] = total[place]
        out[rows:] = (keep[place].astype(f32) + arrived[place].astype(f32)).astype(out.dtype)


def join_kernel(n, *refs):
    group_a, group_b, (out,) = take(refs, n, n)
    rows = group_a[0].shape[0]
    out[:rows] = sum_parts(group_a).astype(out.dtype)
    out[rows:] = sum_parts(group_b).astype(out.dtype)


def merge_kernel(rows, *refs):
    parts, out = refs[:4], refs[4]
    chip = lax.axis_index("sp") // 2
    for step, part in enumerate(parts):
        out[shard_rows(chip ^ step, rows), :] = part[:rows]
    rest = [part[rows:].astype(f32) for part in parts]
    out[4 * rows :] = ((rest[0] + rest[1]) + (rest[2] + rest[3])).astype(out.dtype)


def final_kernel(n_fs, mine, other, *outs):
    query_w, keyval_w, output_w, hidden_w, return_w, reduce_w = outs[:6]
    smalls, hidden_b = outs[6:-1], outs[-1]
    shard, dim = query_w.shape
    half = dim // 2
    fs = lax.axis_index("fs")
    low, high = both_halves(mine, other)
    low, high = low.astype(f32), high.astype(f32)
    for chunk in range(hidden_w.shape[1] // dim):
        hidden_w[:, chunk * dim : (chunk + 1) * dim] = low[chunk * shard : (chunk + 1) * shard]
    return_w[...] = high[:dim]
    low, high = low[dim:], high[dim:]
    query_w[...] = low[:shard]
    keyval_w[:, :dim] = low[shard : 2 * shard]
    keyval_w[:, dim:] = high[:shard]
    output_w[...] = high[shard : 2 * shard]
    low, high = low[2 * shard :], high[2 * shard :]
    reduce_w[:half] = low[:half]
    reduce_w[half:] = high[:half]
    vecs = low[half:] + high[half:]
    lane = lax.broadcasted_iota(jnp.int32, vecs.shape, 1)
    chosen = jnp.where(lane // shard == fs, vecs, 0.0)
    folded = chosen[:, :shard]
    for index in range(1, n_fs):
        folded = folded + chosen[:, index * shard : (index + 1) * shard]
    for index, small in enumerate(smalls):
        small[...] = folded[index : index + 1].reshape(shard)
    row = lax.broadcasted_iota(jnp.int32, vecs.shape, 0)
    hidden_b[...] = jnp.sum(jnp.where(row == HIDDEN_B + fs, vecs, 0.0), axis=0)


def rotate(value, n, step):
    return lax.ppermute(value, "fs", [(i, (i + step) % n) for i in range(n)])


def flip(value, n, bits):
    return lax.ppermute(value, "sp", [(i, i ^ bits) for i in range(n)])


def sum_over_rows(value, n_sp):
    bit = 2
    while bit < n_sp:
        if 2 * bit < n_sp:
            a, b, c = flip(value, n_sp, bit), flip(value, n_sp, 2 * bit), flip(value, n_sp, 3 * bit)
            value = (
                (value.astype(f32) + a.astype(f32)) + (b.astype(f32) + c.astype(f32))
            ).astype(value.dtype)
            bit = 4 * bit
        else:
            a = flip(value, n_sp, bit)
            value = (value.astype(f32) + a.astype(f32)).astype(value.dtype)
            bit = 2 * bit
    return value


def exchange(pieces, n_sp):
    return [pieces[0]] + [flip(pieces[step], n_sp, 2 * step) for step in range(1, n_sp // 2)]


def to_owners(pieces, n_fs):
    return [pieces[0]] + [rotate(pieces[step], n_fs, step) for step in range(1, n_fs)]


def call(kernel, out_shape, in_specs=None, scratch=(), limit=SMALL_VMEM):
    specs = {} if in_specs is None else {"in_specs": in_specs}
    return pl.pallas_call(
        kernel,
        out_shape=out_shape,
        **specs,
        scratch_shapes=scratch,
        compiler_params=pltpu.CompilerParams(vmem_limit_bytes=limit),
        cost_estimate=pl.CostEstimate(flops=0, bytes_accessed=0, transcendentals=0),
    )


def on_device(
    n_fs,
    n_sp,
    tokens,
    cotangent,
    image_sizes,
    first_gain,
    first_bias,
    query_weight,
    query_bias,
    reduce_weight,
    reduce_bias,
    keys_gain,
    keys_bias,
    keyval_weight,
    value_bias,
    output_weight,
    output_bias,
    second_gain,
    second_bias,
    hidden_weight,
    hidden_bias,
    return_weight,
    return_bias,
):
    batches, _, row_dev, cols, dim = tokens.shape
    hid = hidden_weight.shape[1]
    tok = row_dev * cols
    key_dev = tok // 4
    keys = n_sp * key_dev
    shard = dim // n_fs
    half = dim // 2
    vmem = pl.BlockSpec(memory_space=pltpu.VMEM)
    smem = pl.BlockSpec(memory_space=pltpu.SMEM)
    single = keys <= KEY_BLOCK
    split = n_sp == 8
    block = keys if single else KEY_BLOCK
    limit = MAIN_VMEM if single else WHOLE_VMEM

    def shape(*dims, dtype=bf16):
        return jax.ShapeDtypeStruct(dims, dtype)

    smalls = (
        first_gain,
        first_bias,
        query_bias,
        reduce_bias,
        keys_gain,
        keys_bias,
        value_bias,
        output_bias,
        second_gain,
        second_bias,
        return_bias,
    )
    first_half = call(
        functools.partial(pack_first_kernel, n_fs),
        shape(half + VECS + 3 * shard // 2, dim),
        scratch=[pltpu.VMEM((VECS, dim), f32)],
        limit=WHOLE_VMEM,
    )(*smalls, hidden_bias, reduce_weight, query_weight, keyval_weight)
    mine_first = to_owners([first_half] * n_fs, n_fs)[1:]

    begun = call(
        functools.partial(begin_kernel, (n_sp, batches, row_dev, cols, dim)),
        [
            shape(batches * tok, dim, dtype=f32),
            shape(batches * tok, dim, dtype=f32),
            shape(batches, keys, dim),
            shape(dim, dim),
            shape(shard, dim),
            shape(shard, 2 * dim),
            shape(VECS, dim, dtype=f32),
            shape(dim + shard // 2, dim),
        ],
        in_specs=[smem] + [vmem] * 8,
        limit=SMALL_VMEM if single else WHOLE_VMEM,
    )(
        image_sizes,
        tokens,
        reduce_weight,
        query_weight,
        keyval_weight,
        hidden_weight,
        return_weight,
        output_weight,
        first_half,
    )
    normal_first, mask, bias, own_r, own_q, own_kv, own_vec, second_half = begun
    mine_first = call(functools.partial(relay_kernel, n_fs - 1), [shape(*first_half.shape)] * (n_fs - 1))(
        *mine_first, own_vec
    )
    other_first = [flip(piece, n_sp, 1) for piece in mine_first]
    normed, patches, reduced, key_low, whole_reduce, wq, wkv, vec, second_half = call(
        functools.partial(reduce_kernel, (n_fs, batches, row_dev, cols, dim)),
        [
            shape(batches * tok, dim),
            shape(batches * key_dev, 4 * dim),
            shape(batches * key_dev, dim, dtype=f32),
            shape(batches * key_dev, dim),
            shape(n_fs, dim, dim),
            shape(dim, dim),
            shape(dim, 2 * dim),
            shape(VECS, dim, dtype=f32),
            shape(dim + shard // 2, dim),
        ],
        scratch=[pltpu.VMEM((dim // 128, tok, 128), f32)],
    )(normal_first, mask, own_r, own_q, own_kv, own_vec, second_half, *mine_first, *other_first)
    mine_second = to_owners([second_half] * n_fs, n_fs)[1:]

    if split:
        same = exchange([key_low] * (n_sp // 2), n_sp)
        key_pieces = [piece for part in same for piece in (part, flip(part, n_sp, 1))]
    else:
        key_pieces = [lax.all_gather(key_low, "sp")]
    n_pieces = len(key_pieces)

    attended, *kept = call(
        functools.partial(forward_kernel, (batches, tok, key_dev, keys, block, n_pieces)),
        [shape(batches * tok, dim)]
        + [shape(tok, dim)] * batches
        + [shape(keys, 2 * dim)] * batches
        + [shape(dim, tok, dtype=f32)] * batches
        + [shape(PAIRS, 8, 2 * tok, dtype=f32)] * batches
        + [shape(PAIRS, keys, 2 * tok) if single else shape(16, 128)] * batches,
        limit=limit,
    )(normed, vec, bias, wq, wkv, *key_pieces)
    kept = [kept[batch::batches] for batch in range(batches)]
    mine_second = call(functools.partial(relay_kernel, n_fs - 1), [shape(dim + shard // 2, dim)] * (n_fs - 1))(
        *mine_second, kept[0][3]
    )
    other_second = [flip(piece, n_sp, 1) for piece in mine_second]

    acts, normal, rstd, grad_second, keep_a, send_a, wo = call(
        functools.partial(mlp_kernel, (n_fs, batches, row_dev, cols, dim, hid)),
        [
            shape(batches, 1, row_dev, cols, dim, dtype=f32),
            shape(batches * tok, dim, dtype=f32),
            shape(batches * tok, 128, dtype=f32),
            shape(batches * tok + 8, dim, dtype=f32),
            shape(n_fs, dim, dim),
            shape(n_fs, dim, dim),
            shape(dim, dim),
        ],
        scratch=[pltpu.VMEM((dim, hid), bf16), pltpu.VMEM((hid, dim), bf16), pltpu.VMEM((8, dim), f32)],
        limit=limit,
    )(
        tokens,
        cotangent,
        mask,
        attended,
        vec,
        hidden_weight,
        return_weight,
        output_weight,
        *mine_second,
        *other_second,
    )
    arrived_a = flip(send_a, n_sp, 1)
    middle, gatt, gvec_a = call(
        functools.partial(middle_kernel, (batches, tok, hid // dim)),
        [shape(batches * tok, dim, dtype=f32), shape(batches * tok, dim), shape(VECS, dim, dtype=f32)],
        limit=limit,
    )(cotangent, mask, normal, rstd, grad_second, vec, wo)

    if split:
        pieces_a = call(chip_kernel, [shape(n_fs, dim // 4, dim)] * 4)(keep_a, arrived_a)
        total_a = call(chip_sum_kernel, shape(n_fs, dim // 4, dim))(*exchange(pieces_a, n_sp))
    else:
        total_a = vec
    near, far = [], []
    carried = ()
    gkey_dims = (n_sp // 2, key_dev, dim) if split else (n_sp, key_dev, dim)
    for batch in range(batches):
        last = batch == batches - 1
        scratch = [
            pltpu.VMEM((dim, tok), f32),
            pltpu.VMEM((8, 128) if single else (keys, dim), f32),
            pltpu.VMEM((8, 128) if single else (keys, dim), f32),
        ]
        if last:
            more = (*carried, normed, wq, attended, middle, total_a)
            out_shape = [
                shape(n_fs, half, dim),
                shape(n_fs, half, dim),
                shape(batches * tok, dim, dtype=f32),
                shape(*gkey_dims),
                shape(*(gkey_dims if split else (16, 128))),
                shape(VECS, dim, dtype=f32),
            ]
        else:
            more = ()
            out_shape = [
                shape(tok, dim),
                shape(dim, 2 * dim, dtype=f32),
                shape(8, dim, dtype=f32),
                shape(*gkey_dims),
                shape(*(gkey_dims if split else (16, 128))),
            ]
        queries, kvs, attf, stats, probs = kept[batch]
        results = call(
            functools.partial(
                backward_kernel,
                (n_fs, n_sp, batch, last, tok, key_dev, keys, block, n_pieces, batches),
            ),
            out_shape,
            scratch=scratch,
            limit=limit,
        )(gatt, queries, kvs, attf, stats, probs, bias, wkv, *key_pieces, *more)
        if last:
            keep_c, send_c, gnormed, near_b, far_b, gvec_c = results
        else:
            near_b, far_b = results[3:]
            carried = results[:3]
        near.append(near_b)
        far.append(flip(far_b, n_sp, 1) if split else far_b)

    arrived_c = flip(send_c, n_sp, 1)
    if split:
        sums = call(functools.partial(key_sum_kernel, batches), [shape(batches * key_dev, dim)] * 4)(*near, *far)
        parts = exchange(sums, n_sp)
        chunks = call(owners_kernel, [shape(dim // 4 + half, dim)] * n_fs)(total_a, keep_c, arrived_c)
        after = [chunks[0]]
    else:
        parts = [lax.all_to_all(jnp.concatenate(near, axis=1), "sp", 0, 0)]
        after = []

    grad_reduced, gvec_b, keep_b, send_b = call(
        functools.partial(reduction_kernel, len(parts), n_fs),
        [
            shape(batches * key_dev, dim),
            shape(VECS, dim, dtype=f32),
            shape(n_fs, half, dim),
            shape(n_fs, half, dim),
        ],
    )(patches, reduced, vec, *parts, *after)
    arrived_b = flip(send_b, n_sp, 1)
    grads, vectors = call(
        functools.partial(input_kernel, (batches, row_dev, cols, dim)),
        [shape(batches, 1, row_dev, cols, dim, dtype=f32), shape(VECS, dim)],
        scratch=[pltpu.VMEM((dim // 128, tok, 128), f32)],
    )(tokens, middle, gnormed, mask, grad_reduced, whole_reduce, vec, gvec_a, gvec_b, gvec_c)

    chunks_b = call(functools.partial(owner_kernel, n_fs, 1), [shape(half + VECS, dim)] * n_fs)(
        keep_b, arrived_b, vectors
    )
    group_b = to_owners(chunks_b, n_fs)
    if split:
        group_a = to_owners(chunks, n_fs)
        rows = group_a[0].shape[0] + group_b[0].shape[0]
        joined = call(functools.partial(join_kernel, n_fs), shape(rows, dim))(*group_a, *group_b)
        mine = call(functools.partial(merge_kernel, dim // 4), shape(rows + 3 * (dim // 4), dim))(
            *exchange([joined] * 4, n_sp)
        )
    else:
        groups = [group_b]
        for keep, arrived in ((keep_c, arrived_c), (keep_a, arrived_a)):
            pieces = call(functools.partial(owner_kernel, n_fs, 0), [shape(*keep.shape[1:])] * n_fs)(keep, arrived)
            groups.insert(0, to_owners(pieces, n_fs))
        mine = jnp.concatenate(
            [
                sum_over_rows(sum(piece.astype(f32) for piece in group).astype(bf16), n_sp)
                for group in groups
            ],
            axis=0,
        )

    gquery, gkeyval, goutput, ghidden, greturn, greduce, *vectors = call(
        functools.partial(final_kernel, n_fs),
        [
            shape(shard, dim, dtype=f32),
            shape(shard, 2 * dim, dtype=f32),
            shape(shard, dim, dtype=f32),
            shape(shard, hid, dtype=f32),
            shape(dim, dim, dtype=f32),
            shape(dim, dim, dtype=f32),
        ]
        + [shape(shard, dtype=f32)] * HIDDEN_B
        + [shape(dim, dtype=f32)],
    )(mine, flip(mine, n_sp, 1))
    return (
        acts,
        grads,
        vectors[FIRST_G],
        vectors[FIRST_B],
        gquery,
        vectors[QUERY_B],
        greduce,
        vectors[REDUCE_B],
        vectors[KEYS_G],
        vectors[KEYS_B],
        gkeyval,
        vectors[VALUE_B],
        goutput,
        vectors[OUTPUT_B],
        vectors[SECOND_G],
        vectors[SECOND_B],
        ghidden,
        vectors[HIDDEN_B],
        greturn,
        vectors[RETURN_B],
    )


def solution(mesh):
    vec, mat = P("fs"), P("fs", None)
    image = P(None, "fs", "sp", None, None)
    weights = (vec, vec, mat, vec, mat, vec, vec, vec, mat, vec, mat, vec, vec, vec, mat, vec, mat, vec)
    return jax.shard_map(
        functools.partial(on_device, mesh.shape["fs"], mesh.shape["sp"]),
        mesh=mesh,
        in_specs=(image, image, P(None, "fs", None)) + weights,
        out_specs=(image, image) + weights,
        check_vma=False,
    )
```

```python
import functools

import jax
import jax.numpy as jnp
from jax import lax
from jax.experimental import pallas as pl
from jax.experimental.pallas import tpu as pltpu
from jax.sharding import PartitionSpec as P

HEADS = 8
HDIM = 32
PAIRS = HEADS // 2
SCALE = HDIM ** (-0.5)
EXP_SCALE = SCALE * 1.4426950408889634
EPS = 1e-06
NEG = -1e30
KEY_BLOCK = 768
SMALL_VMEM = 12 * 2**20
MAIN_VMEM = 16 * 2**20
WHOLE_VMEM = 58 * 2**20

bf16 = jnp.bfloat16
f32 = jnp.float32

(
    FIRST_G,
    FIRST_B,
    QUERY_B,
    REDUCE_B,
    KEYS_G,
    KEYS_B,
    VALUE_B,
    OUTPUT_B,
    SECOND_G,
    SECOND_B,
    RETURN_B,
    HIDDEN_B,
) = range(12)
VECS = 16


def mm(left, right):
    return jnp.dot(left, right, preferred_element_type=f32)


def mm_tn(left, right):
    return lax.dot_general(left, right, (((0,), (0,)), ((), ())), preferred_element_type=f32)


def mm_nt(left, right):
    return lax.dot_general(left, right, (((1,), (1,)), ((), ())), preferred_element_type=f32)


def normalize(rows):
    mean = jnp.mean(rows, axis=-1, keepdims=True)
    centered = rows - mean
    var = jnp.mean(centered * centered, axis=-1, keepdims=True)
    rstd = lax.rsqrt(var + EPS)
    return centered * rstd, rstd


def normalize_back(grad, normal, rstd, gain):
    scaled = grad * gain
    mean_a = jnp.mean(scaled, axis=-1, keepdims=True)
    mean_b = jnp.mean(scaled * normal, axis=-1, keepdims=True)
    return (scaled - mean_a - normal * mean_b) * rstd


def token_mask(first_row, rows, cols, width, height, image_width):
    row_ids = lax.broadcasted_iota(jnp.int32, (rows, cols, width), 0) + first_row
    col_ids = lax.broadcasted_iota(jnp.int32, (rows, cols, width), 1)
    valid = (row_ids < height) & (col_ids < image_width)
    return jnp.where(valid, 1.0, 0.0).astype(f32).reshape(rows * cols, width)


def pack_first_kernel(n_fs, *refs):
    smalls, (hidden_b, reduce_w, query_w, keyval_w, first, wide) = take(refs, HIDDEN_B)
    dim = reduce_w.shape[1]
    shard = dim // n_fs
    half = dim // 2
    rest = half + VECS
    fs = lax.axis_index("fs")
    is_low = lax.axis_index("sp") % 2 == 0

    @pl.when(is_low)
    def _():
        first[:half] = reduce_w[:half]
        first[rest : rest + shard] = query_w[...]
        first[rest + shard :] = keyval_w[: shard // 2, :dim]

    @pl.when(jnp.logical_not(is_low))
    def _():
        first[:half] = reduce_w[half:]
        first[rest : rest + shard // 2] = keyval_w[shard // 2 :, :dim]
        first[rest + shard // 2 :] = keyval_w[:, dim:]

    wide[...] = jnp.zeros_like(wide)
    for index, small in enumerate(smalls):
        row = small[...].astype(f32).reshape(1, shard)
        wide[index : index + 1, :] = jnp.concatenate([row] * n_fs, axis=1)
    lane = lax.broadcasted_iota(jnp.int32, wide.shape, 1)
    row = lax.broadcasted_iota(jnp.int32, wide.shape, 0)
    vectors = jnp.where(lane // shard == fs, wide[...], 0.0)
    hidden_row = hidden_b[...].astype(f32).reshape(1, dim)
    first[half:rest] = jnp.where(row == HIDDEN_B + fs, hidden_row, vectors).astype(bf16)


def both_halves(mine, other):
    is_low = lax.axis_index("sp") % 2 == 0
    a, b = mine[...], other[...]
    return jnp.where(is_low, a, b), jnp.where(is_low, b, a)


def shard_rows(place, rows):
    return pl.ds(pl.multiple_of(place * rows, rows), rows)


def begin_kernel(dims, sizes, tokens, reduce_w, query_w, keyval_w, hidden_w, return_w, output_w, packed, *outs):
    n_sp, batches, row_dev, cols, dim = dims
    normal_ref, rstd_ref, mask_ref, bias_ref, own_r, own_q, own_kv, own_vec, second = outs
    tok = row_dev * cols
    half_cols = cols // 2
    rows_dev = row_dev // 2
    half = dim // 2
    shard = hidden_w.shape[0]
    sp = lax.axis_index("sp")
    own_r[...] = reduce_w[...]
    own_q[...] = query_w[...]
    own_kv[...] = keyval_w[...]
    own_vec[...] = packed[half : half + VECS].astype(f32)

    @pl.when(sp % 2 == 0)
    def _():
        for chunk in range(hidden_w.shape[1] // dim):
            second[chunk * shard : (chunk + 1) * shard] = hidden_w[:, chunk * dim : (chunk + 1) * dim]
        second[dim:] = output_w[: shard // 2]

    @pl.when(sp % 2 == 1)
    def _():
        second[:dim] = return_w[...]
        second[dim:] = output_w[shard // 2 :]

    for batch in range(batches):
        height, image_width = sizes[batch, 0, 0], sizes[batch, 0, 1]
        rows = slice(batch * tok, (batch + 1) * tok)
        normal, rstd = normalize(tokens[batch, 0].reshape(tok, dim).astype(f32))
        normal_ref[rows] = normal
        rstd_ref[rows] = jnp.broadcast_to(rstd, (tok, 128))
        mask_ref[rows] = token_mask(sp * row_dev, row_dev, cols, dim, height, image_width)
        col_ids = lax.broadcasted_iota(jnp.int32, (half_cols, dim), 0)

        def key_row_bias(index, _, batch=batch, height=height, image_width=image_width, col_ids=col_ids):
            key_row = index
            if n_sp == 8:
                key_row = (sp ^ (index // rows_dev)) * rows_dev + lax.rem(index, rows_dev)
            width = jnp.where(2 * key_row < height, image_width, 0)
            here = pl.ds(pl.multiple_of(index * half_cols, half_cols), half_cols)
            bias_ref[batch, here, :] = jnp.where(2 * col_ids < width, 0.0, NEG).astype(bf16)
            return 0

        lax.fori_loop(0, n_sp * rows_dev, key_row_bias, 0)


def reduce_kernel(dims, *refs):
    n_fs, batches, row_dev, cols, dim = dims
    ins, mine, other, outs = take(refs, 7, n_fs - 1, n_fs - 1)
    normal_in, mask_ref, own_w, own_q, own_kv, own_vec, second_in = ins
    normed_ref, cols_ref, send_ref, reduced_ref, key_ref, weight_ref, wq, wkv, vec_ref, second, patch_ref, wide = outs
    half = dim // 2
    shard = dim // n_fs
    rest = half + VECS
    tok = row_dev * cols
    half_cols = cols // 2
    key_dev = tok // 4
    fs = lax.axis_index("fs")
    second[...] = second_in[...]
    weight_ref[fs] = own_w[...]
    here = shard_rows(fs, shard)
    wq[here, :] = own_q[...]
    wkv[here, :] = own_kv[...]
    vec = own_vec[...]
    for step in range(1, n_fs):
        low, high = both_halves(mine[step - 1], other[step - 1])
        place = lax.rem(fs + n_fs - step, n_fs)
        weight_ref[place, :half] = low[:half]
        weight_ref[place, half:] = high[:half]
        vec = vec + low[half:rest].astype(f32)
        here = shard_rows(place, shard)
        wq[here, :] = low[rest : rest + shard]
        wkv[here, :dim] = jnp.concatenate([low[rest + shard :], high[rest : rest + shard // 2]], axis=0)
        wkv[here, dim:] = high[rest + shard // 2 :]
    vec_ref[...] = vec
    for batch in range(batches):
        rows = slice(batch * tok, (batch + 1) * tok)
        low = (normal_in[rows] * vec[FIRST_G : FIRST_G + 1] + vec[FIRST_B : FIRST_B + 1]).astype(bf16)
        normed_ref[rows] = low
        masked = low.astype(f32) * mask_ref[rows]
        for part in range(dim // 128):
            wide[part] = masked[:, part * 128 : (part + 1) * 128]
        for row in range(row_dev // 2):
            start = batch * key_dev + row * half_cols
            for offset in range(4):
                dr, dc = offset // 2, offset % 2
                for part in range(dim // 128):
                    piece = wide[part, pl.ds((2 * row + dr) * cols + dc, half_cols, stride=2), :]
                    lanes = slice(offset * dim + part * 128, offset * dim + (part + 1) * 128)
                    patch_ref[start : start + half_cols, lanes] = piece.astype(bf16)
    is_low = lax.axis_index("sp") % 2 == 0
    for offset in range(4):
        low = patch_ref[:, offset * dim : offset * dim + half]
        high = patch_ref[:, offset * dim + half : (offset + 1) * dim]
        cols_ref[offset] = jnp.where(is_low, low, high)
        send_ref[offset] = jnp.where(is_low, high, low)
    reduced = mm(patch_ref[...], weight_ref[...].reshape(4 * dim, dim)) + vec[REDUCE_B : REDUCE_B + 1]
    reduced_ref[...] = reduced
    normal, _ = normalize(reduced)
    key_ref[...] = (normal * vec[KEYS_G : KEYS_G + 1] + vec[KEYS_B : KEYS_B + 1]).astype(bf16)


def relay_kernel(n, *refs):
    for source, target in zip(refs[:n], refs[n + 1 :]):
        target[...] = source[...]


def head_stack_t(values_t, pair, tok):
    both = jnp.concatenate([values_t, values_t], axis=1)
    head = lax.broadcasted_iota(jnp.int32, both.shape, 0) // HDIM
    want = 2 * pair + jnp.where(lax.broadcasted_iota(jnp.int32, both.shape, 1) >= tok, 1, 0)
    return jnp.where(head == want, both, jnp.zeros_like(both))


def head_stack(values, pair):
    head = lax.broadcasted_iota(jnp.int32, values.shape, 1) // HDIM
    zero = jnp.zeros_like(values)
    return jnp.concatenate(
        [jnp.where(head == 2 * pair, values, zero), jnp.where(head == 2 * pair + 1, values, zero)],
        axis=0,
    )


def split_pair(both, tok):
    return jnp.concatenate([both[:HDIM, :tok], both[HDIM:, tok:]], axis=0)


def key_rows_of(pieces, key_dev, per_block, batch, index):
    here = slice(batch * key_dev, (batch + 1) * key_dev)
    if len(pieces) > 1:
        return jnp.concatenate([part[here] for part in pieces], axis=0)
    dim = pieces[0].shape[2]
    devices = slice(index * per_block, (index + 1) * per_block)
    return pieces[0][devices, here, :].reshape(per_block * key_dev, dim)


def mask_lane(pair, dim):
    return 0 if pair == PAIRS - 1 else dim - 1


def with_bias(key_block, bias, lane_id):
    lane = lax.broadcasted_iota(jnp.int32, key_block.shape, 1)
    return jnp.where(lane == lane_id, bias.astype(f32), key_block.astype(f32)).astype(bf16)


def query_stack(queries_t, pair, lane_id, tok):
    stacked = head_stack_t(queries_t, pair, tok)
    row = lax.broadcasted_iota(jnp.int32, stacked.shape, 0)
    return jnp.where(row == lane_id, jnp.ones_like(stacked), stacked)


def take(refs, *counts):
    refs = list(refs)
    groups = []
    for count in counts:
        groups.append(refs[:count])
        refs = refs[count:]
    return groups + [refs]


def forward_kernel(dims, *refs):
    batches, tok, key_dev, keys, block, n_pieces = dims
    (normed, vec_ref, bias_ref, wq, wkv), pieces, (attended, *kept, wide) = take(refs, 5, n_pieces)
    queries_out, kvs, attf, stats, probs = (
        kept[index * batches : (index + 1) * batches] for index in range(5)
    )
    dim = wq.shape[0]
    blocks = keys // block
    per_block = block // key_dev
    queries_t, values_t, masked = [], [], []
    for batch in range(batches):
        rows = slice(batch * tok, (batch + 1) * tok)
        queries = (mm(normed[rows], wq[...]) + vec_ref[QUERY_B : QUERY_B + 1]).astype(bf16)
        queries_out[batch][...] = queries
        queries_t.append(queries.T)
        for index in range(blocks):
            key_rows = key_rows_of(pieces, key_dev, per_block, batch, index)
            here = slice(index * block, (index + 1) * block)
            kvs[batch][here, :dim] = mm(key_rows, wkv[:, :dim]).astype(bf16)
            value_rows = mm(key_rows, wkv[:, dim:]) + vec_ref[VALUE_B : VALUE_B + 1]
            kvs[batch][here, dim:] = value_rows.astype(bf16)
    if blocks == 1:
        for batch in range(batches):
            key_block = kvs[batch][:, :dim]
            bias = bias_ref[batch]
            values_t.append(kvs[batch][:, dim:].T)
            masked.append({lane_id: with_bias(key_block, bias, lane_id) for lane_id in (0, dim - 1)})
        todo = [(batch, pair) for batch in range(batches) for pair in range(PAIRS)]

        def score(index):
            batch, pair = todo[index]
            lane_id = mask_lane(pair, dim)
            wide[index % 2] = mm(masked[batch][lane_id], query_stack(queries_t[batch], pair, lane_id, tok))

        score(0)
        for index, (batch, pair) in enumerate(todo):
            if index + 1 < len(todo):
                score(index + 1)
            heads = slice(2 * HDIM * pair, 2 * HDIM * (pair + 1))
            scores = wide[index % 2]
            top = jnp.max(scores, axis=0, keepdims=True)
            weights = jnp.exp2((scores - top) * EXP_SCALE)
            inverse = 1.0 / jnp.sum(weights, axis=0, keepdims=True)
            low = weights.astype(bf16)
            probs[batch][pair] = low
            stats[batch][pair, 0:1] = inverse
            mixed = mm(values_t[batch][heads], low) * inverse
            attf[batch][heads] = split_pair(mixed, tok)
    else:
        for batch in range(batches):
            for pair in range(PAIRS):
                lane_id = mask_lane(pair, dim)
                heads = slice(2 * HDIM * pair, 2 * HDIM * (pair + 1))
                stacked = query_stack(queries_t[batch], pair, lane_id, tok)

                def block_scores(index, stacked=stacked, lane_id=lane_id, batch=batch):
                    here = pl.ds(pl.multiple_of(index * block, block), block)
                    masked = with_bias(kvs[batch][here, :dim], bias_ref[batch, here, :], lane_id)
                    return here, mm(masked, stacked)

                def find_top(index, top, block_scores=block_scores):
                    _, scores = block_scores(index)
                    return jnp.maximum(top, jnp.max(scores, axis=0, keepdims=True))

                top = lax.fori_loop(0, blocks, find_top, jnp.full((1, 2 * tok), 4 * NEG, f32))

                def add_block(index, carry, block_scores=block_scores, top=top, heads=heads, batch=batch):
                    total, mixed = carry
                    here, scores = block_scores(index)
                    weights = jnp.exp2((scores - top) * EXP_SCALE)
                    values_t = kvs[batch][here, dim:].T
                    mixed = mixed + mm(values_t[heads], weights.astype(bf16))
                    return total + jnp.sum(weights, axis=0, keepdims=True), mixed

                start = (jnp.zeros((1, 2 * tok), f32), jnp.zeros((2 * HDIM, 2 * tok), f32))
                total, mixed = lax.fori_loop(0, blocks, add_block, start)
                inverse = 1.0 / total
                stats[batch][pair, 0:1] = inverse
                stats[batch][pair, 1:2] = top
                attf[batch][heads] = split_pair(mixed * inverse, tok)
    for batch in range(batches):
        attended[batch * tok : (batch + 1) * tok] = attf[batch][...].T.astype(bf16)


def mlp_kernel(dims, *refs):
    n_fs, batches, row_dev, cols, dim, hid = dims
    ins, own, mine, other, _, outs, scratch = take(refs, 5, 3, n_fs - 1, n_fs - 1, 1, 7)
    tokens, cotangent, mask_ref, attended, vec_ref = ins
    acts_ref, normal_ref, rstd_ref, grad_ref, keep_ref, send_ref, wo = outs
    wh, wr, bias_rows, lows, highs = scratch
    tok = row_dev * cols
    shard = dim // n_fs
    chunks = hid // dim
    fs = lax.axis_index("fs")
    is_low = lax.axis_index("sp") % 2 == 0
    wh[shard_rows(fs, shard), :] = own[0][...]
    wr[shard_rows(fs, dim), :] = own[1][...]
    wo[shard_rows(fs, shard), :] = own[2][...]
    for step in range(1, n_fs):
        low, high = both_halves(mine[step - 1], other[step - 1])
        place = lax.rem(fs + n_fs - step, n_fs)
        here = shard_rows(place, shard)
        for chunk in range(chunks):
            wh[here, chunk * dim : (chunk + 1) * dim] = low[chunk * shard : (chunk + 1) * shard]
        wr[shard_rows(place, dim), :] = high[:dim]
        wo[here, :] = jnp.concatenate([low[dim:], high[dim:]], axis=0)

    def vec(index):
        return vec_ref[index : index + 1, :]

    x = jnp.concatenate([tokens[b, 0].reshape(tok, dim).astype(f32) for b in range(batches)], axis=0)
    mask = mask_ref[...]
    middle = x + mm(attended[...], wo[...]) + vec(OUTPUT_B)
    normal, rstd = normalize(middle)
    normal_ref[...] = normal
    rstd_ref[...] = jnp.broadcast_to(rstd, rstd_ref.shape)
    second = (normal * vec(SECOND_G) + vec(SECOND_B)).astype(bf16)
    grad_out = jnp.concatenate([cotangent[b, 0].reshape(tok, dim) for b in range(batches)], axis=0) * mask
    grad_mlp = grad_out.astype(bf16)
    total = middle + vec(RETURN_B)
    grad_second = jnp.zeros((batches * tok, dim), f32)
    bias_rows[...] = jnp.zeros_like(bias_rows)
    for chunk in range(chunks):
        lanes = slice(chunk * dim, (chunk + 1) * dim)
        hidden = mm(second, wh[:, lanes]) + vec(HIDDEN_B + chunk)
        phi = 0.5 + 0.5 * lax.erf(hidden * 0.7071067811865476)
        density = 0.3989422804014327 * jnp.exp2(hidden * hidden * (-0.5 * 1.4426950408889634))
        activated = (hidden * phi).astype(bf16)
        total = total + mm(activated, wr[lanes, :])
        grad_activated = mm_nt(grad_mlp, wr[lanes, :])
        grad_hidden = ((phi + hidden * density) * grad_activated).astype(bf16)
        bias_rows[chunk : chunk + 1] = jnp.sum(grad_hidden.astype(f32), axis=0, keepdims=True)
        grad_second = grad_second + mm_nt(grad_hidden, wh[:, lanes])
        highs[chunk] = mm_tn(activated, grad_mlp).astype(bf16)
        grad_wh = mm_tn(second, grad_hidden).astype(bf16)
        for owner in range(n_fs):
            lows[owner, chunk * shard : (chunk + 1) * shard] = grad_wh[owner * shard : (owner + 1) * shard]
    low, high = lows[...], highs[...]
    keep_ref[...] = jnp.where(is_low, low, high)
    send_ref[...] = jnp.where(is_low, high, low)
    total = total * mask
    for batch in range(batches):
        acts_ref[batch, 0] = total[batch * tok : (batch + 1) * tok].reshape(row_dev, cols, dim)
    rows = batches * tok
    grad_ref[:rows] = grad_second
    grad_ref[rows:] = bias_rows[...]


def middle_kernel(dims, cotangent, mask_ref, normal_ref, rstd_ref, grad_ref, vec_ref, wo, middle_ref, gatt, gvec_ref):
    batches, tok, chunks = dims
    dim = wo.shape[0]
    rows = batches * tok
    grad_out = jnp.concatenate([cotangent[b, 0].reshape(tok, dim) for b in range(batches)], axis=0)
    grad_out = grad_out * mask_ref[...]
    grad_second, normal = grad_ref[:rows], normal_ref[...]
    rstd = jnp.concatenate([rstd_ref[...]] * (dim // rstd_ref.shape[1]), axis=1)
    back = normalize_back(grad_second, normal, rstd, vec_ref[SECOND_G : SECOND_G + 1])
    grad_middle = grad_out + back
    middle_ref[...] = grad_middle
    grad_branch = grad_middle.astype(bf16)
    gatt[...] = mm_nt(grad_branch, wo[...]).astype(bf16)
    gvec_ref[...] = jnp.zeros_like(gvec_ref)
    for index, value in (
        (OUTPUT_B, grad_branch.astype(f32)),
        (SECOND_G, grad_second * normal),
        (SECOND_B, grad_second),
        (RETURN_B, grad_out.astype(bf16).astype(f32)),
    ):
        gvec_ref[index : index + 1] = jnp.sum(value, axis=0, keepdims=True)
    gvec_ref[HIDDEN_B : HIDDEN_B + chunks] = grad_ref[rows : rows + chunks]


def backward_kernel(dims, *refs):
    n_sp, batch, tok, key_dev, keys, block, n_pieces = dims
    gatt, queries_ref, kvs, attf, stats, probs, bias_ref, wkv, _ = refs[:9]
    near_ref, far_ref, scores_ref, gks, gvs, gvec_ref = refs[9:15]
    dim = wkv.shape[0]
    blocks = keys // block
    per_block = block // key_dev
    rows = slice(batch * tok, (batch + 1) * tok)
    queries = queries_ref[...]
    grad_att_t = gatt[rows].astype(f32).T
    product = grad_att_t * attf[...]

    def pair_terms(pair):
        inverse = stats[pair, 0:1]
        piece = product[2 * HDIM * pair : 2 * HDIM * (pair + 1)]
        delta = jnp.concatenate(
            [jnp.sum(piece[:HDIM], axis=0, keepdims=True), jnp.sum(piece[HDIM:], axis=0, keepdims=True)],
            axis=1,
        )
        stacked = head_stack_t(grad_att_t, pair, tok) * inverse
        return delta * inverse, stacked.astype(bf16)

    if blocks == 1:
        values = kvs[:, dim:]
        grad_k = jnp.zeros((keys, dim), f32)
        grad_v = jnp.zeros((keys, dim), f32)
        for pair in range(PAIRS):
            delta, stacked = pair_terms(pair)
            low = probs[pair]
            grad_probs = mm(values, stacked)
            grad_scores = (low.astype(f32) * (grad_probs - delta)).astype(bf16)
            scores_ref[pair] = grad_scores
            grad_k = grad_k + mm(grad_scores, head_stack(queries, pair))
            grad_v = grad_v + mm(low, stacked.T)
    else:
        wide_k, wide_v = refs[15:]
        wide_k[...] = jnp.zeros_like(wide_k)
        wide_v[...] = jnp.zeros_like(wide_v)
        queries_t = queries.T
        for pair in range(PAIRS):
            heads = slice(2 * HDIM * pair, 2 * HDIM * (pair + 1))
            lane_id = mask_lane(pair, dim)
            delta, stacked = pair_terms(pair)
            stacked_n = stacked.T
            query_t = query_stack(queries_t, pair, lane_id, tok)
            query_n = head_stack(queries, pair)
            top = stats[pair, 1:2]

            def back_block(index, gq, heads=heads, lane_id=lane_id, delta=delta, stacked=stacked, stacked_n=stacked_n, query_t=query_t, query_n=query_n, top=top):
                here = pl.ds(pl.multiple_of(index * block, block), block)
                key_block = kvs[here, :dim]
                masked = with_bias(key_block, bias_ref[batch, here, :], lane_id)
                weights = jnp.exp2((mm(masked, query_t) - top) * EXP_SCALE)
                grad_probs = mm(kvs[here, dim:], stacked)
                grad_scores = (weights * (grad_probs - delta)).astype(bf16)
                wide_k[here, :] += mm(grad_scores, query_n)
                wide_v[here, :] += mm(weights.astype(bf16), stacked_n)
                return gq + mm(key_block.T[heads], grad_scores)

            gq = lax.fori_loop(0, blocks, back_block, jnp.zeros((2 * HDIM, 2 * tok), f32))
            scores_ref[heads] = split_pair(gq, tok)
    bias_value = jnp.zeros((1, dim), f32)
    for index in range(blocks):
        here = slice(index * block, (index + 1) * block)
        if blocks > 1:
            grad_k, grad_v = wide_k[here], wide_v[here]
        grad_k = (grad_k * SCALE).astype(bf16)
        bias_value = bias_value + jnp.sum(grad_v, axis=0, keepdims=True)
        grad_v = grad_v.astype(bf16)
        gks[here] = grad_k
        gvs[here] = grad_v
        grad_key = (mm_nt(grad_k, wkv[:, :dim]) + mm_nt(grad_v, wkv[:, dim:])).astype(bf16)
        if n_pieces > 1:
            pairs = grad_key.reshape(n_sp // 2, 2, key_dev, dim)
            near_ref[...] = pairs[:, 0]
            far_ref[...] = pairs[:, 1]
        else:
            near_ref[index * per_block : (index + 1) * per_block] = grad_key.reshape(per_block, key_dev, dim)
    gvec_ref[...] = jnp.broadcast_to(bias_value, gvec_ref.shape)


def query_kernel(dims, *refs):
    n_fs, batches, tok, key_dev, keys, block, n_pieces = dims
    ins, kvs, scores, gks, gvs, gvecs, pieces, outs = take(refs, 5, *([batches] * 5), n_pieces)
    normed, wq, attended, middle, _ = ins
    keep_ref, send_ref, gnormed_ref, gvec_ref, wide = outs
    dim = wq.shape[0]
    shard = dim // n_fs
    blocks = keys // block
    per_block = block // key_dev
    grad_queries = []
    grad_wk = jnp.zeros((dim, dim), f32)
    grad_wv = jnp.zeros((dim, dim), f32)
    for batch in range(batches):
        if blocks == 1:
            keys_t = kvs[batch][:, :dim].T
            for pair in range(PAIRS):
                heads = slice(2 * HDIM * pair, 2 * HDIM * (pair + 1))
                wide[heads] = split_pair(mm(keys_t[heads], scores[batch][pair]), tok)
            grad_t = wide[...]
        else:
            grad_t = scores[batch][...]
        grad_queries.append((grad_t.T * SCALE).astype(bf16))
        for index in range(blocks):
            here = slice(index * block, (index + 1) * block)
            key_rows = key_rows_of(pieces, key_dev, per_block, batch, index)
            grad_wk = grad_wk + mm_tn(key_rows, gks[batch][here])
            grad_wv = grad_wv + mm_tn(key_rows, gvs[batch][here])
    grad_queries = jnp.concatenate(grad_queries, axis=0)
    grad_wq = mm_tn(normed[...], grad_queries)
    grad_wo = mm_tn(attended[...], middle[...].astype(bf16))
    is_low = lax.axis_index("sp") % 2 == 0
    for owner in range(n_fs):
        part = slice(owner * shard, (owner + 1) * shard)
        low = jnp.concatenate([grad_wq[part], grad_wk[part]], axis=0).astype(bf16)
        high = jnp.concatenate([grad_wv[part], grad_wo[part]], axis=0).astype(bf16)
        keep_ref[owner] = jnp.where(is_low, low, high)
        send_ref[owner] = jnp.where(is_low, high, low)
    gnormed_ref[...] = mm_nt(grad_queries, wq[...])
    gvec_ref[...] = jnp.zeros_like(gvec_ref)
    gvec_ref[QUERY_B : QUERY_B + 1] = jnp.sum(grad_queries.astype(f32), axis=0, keepdims=True)
    bias_value = gvecs[0][0:1]
    for gvec in gvecs[1:]:
        bias_value = bias_value + gvec[0:1]
    gvec_ref[VALUE_B : VALUE_B + 1] = bias_value


def sum_parts(parts):
    if len(parts) == 1:
        total = parts[0][0].astype(f32)
        for index in range(1, parts[0].shape[0]):
            total = total + parts[0][index].astype(f32)
        return total
    total = parts[0][...].astype(f32)
    for part in parts[1:]:
        total = total + part[...].astype(f32)
    return total


def reduction_kernel(n_parts, batches, reduced, vec_ref, *refs):
    parts, gvec_ref, outs = refs[:n_parts], refs[-1], refs[-1 - batches : -1]
    grad_key = sum_parts(parts)
    normal, rstd = normalize(reduced[...])
    grad_low = normalize_back(grad_key, normal, rstd, vec_ref[KEYS_G : KEYS_G + 1]).astype(bf16)
    rows = outs[0].shape[0]
    for batch, out in enumerate(outs):
        out[...] = grad_low[batch * rows : (batch + 1) * rows]
    gvec_ref[...] = jnp.zeros_like(gvec_ref)
    for index, value in (
        (REDUCE_B, grad_low.astype(f32)),
        (KEYS_G, grad_key * normal),
        (KEYS_B, grad_key),
    ):
        gvec_ref[index : index + 1] = jnp.sum(value, axis=0, keepdims=True)


def weight_kernel(batches, *refs):
    (own_cols, other_cols), own, other, (vectors, *outs) = take(refs, 2, batches, batches)
    fs = lax.axis_index("fs")
    own = jnp.concatenate([part[...] for part in own], axis=0)
    other = jnp.concatenate([part[...] for part in other], axis=0)
    rows = own_cols.shape[2]
    for step, out in enumerate(outs):
        place = lax.rem(fs + step, len(outs))
        out[:rows] = (mm_tn(own_cols[place], own) + mm_tn(other_cols[place], other)).astype(out.dtype)
        out[rows:] = vectors[...]


def normed_kernel(dims, gnormed, mask_ref, weight, normal_ref, vec_a, vec_b, vec_c, *refs):
    batches, row_dev, cols, dim = dims
    grads, (grad_ref, gvec_ref, wide) = take(refs, batches)
    tok = row_dev * cols
    half_cols = cols // 2
    gain_first = jnp.zeros((1, dim), f32)
    bias_first = jnp.zeros((1, dim), f32)
    for batch in range(batches):
        for offset in range(4):
            dr, dc = offset // 2, offset % 2
            back = mm_nt(grads[batch][...], weight[offset])
            for row in range(row_dev // 2):
                for part in range(dim // 128):
                    wide[part, pl.ds((2 * row + dr) * cols + dc, half_cols, stride=2), :] = back[
                        row * half_cols : (row + 1) * half_cols, part * 128 : (part + 1) * 128
                    ]
        rows = slice(batch * tok, (batch + 1) * tok)
        spread = jnp.concatenate([wide[part] for part in range(dim // 128)], axis=1)
        grad_normed = gnormed[rows] + spread * mask_ref[rows]
        grad_ref[rows] = grad_normed
        gain_first = gain_first + jnp.sum(grad_normed * normal_ref[rows], axis=0, keepdims=True)
        bias_first = bias_first + jnp.sum(grad_normed, axis=0, keepdims=True)
    index = lax.broadcasted_iota(jnp.int32, (VECS, dim), 0)
    vectors = vec_a[...] + vec_b[...] + vec_c[...]
    vectors = jnp.where(index == FIRST_G, gain_first, vectors)
    vectors = jnp.where(index == FIRST_B, bias_first, vectors)
    gvec_ref[...] = vectors.astype(bf16)


def input_kernel(dims, middle, grad_normed, normal_ref, rstd_ref, vec_ref, grad_ref, done_ref):
    batches, row_dev, cols, dim = dims
    tok = row_dev * cols
    rstd = jnp.concatenate([rstd_ref[...]] * (dim // rstd_ref.shape[1]), axis=1)
    back = normalize_back(grad_normed[...], normal_ref[...], rstd, vec_ref[FIRST_G : FIRST_G + 1])
    grad_x = middle[...] + back
    for batch in range(batches):
        grad_ref[batch, 0] = grad_x[batch * tok : (batch + 1) * tok].reshape(row_dev, cols, dim)
    done_ref[...] = jnp.zeros_like(done_ref)


def key_sum_kernel(batches, *refs):
    near, far, _, outs = take(refs, batches, batches, 2)
    for step, out in enumerate(outs):
        rows = near[0].shape[1]
        for batch in range(batches):
            total = near[batch][step].astype(f32) + far[batch][step].astype(f32)
            out[batch * rows : (batch + 1) * rows] = total.astype(out.dtype)


def owner_kernel(keep, arrived, *outs):
    fs = lax.axis_index("fs")
    for step, out in enumerate(outs):
        place = lax.rem(fs + step, len(outs))
        out[...] = (keep[place].astype(f32) + arrived[place].astype(f32)).astype(out.dtype)


def chip_kernel(keep, arrived, _, *outs):
    chip = lax.axis_index("sp") // 2
    rows = outs[0].shape[1]
    for step, out in enumerate(outs):
        here = shard_rows(chip ^ step, rows)
        out[...] = (keep[:, here, :].astype(f32) + arrived[:, here, :].astype(f32)).astype(out.dtype)


def chip_sum_kernel(*refs):
    refs[-1][...] = sum_parts(refs[:-1]).astype(refs[-1].dtype)


def owners_kernel(total, keep, arrived, *outs):
    fs = lax.axis_index("fs")
    rows = total.shape[1]
    for step, out in enumerate(outs):
        place = lax.rem(fs + step, len(outs))
        out[:rows] = total[place]
        out[rows:] = (keep[place].astype(f32) + arrived[place].astype(f32)).astype(out.dtype)


def join_kernel(n, *refs):
    refs[-1][...] = sum_parts(refs[:n]).astype(refs[-1].dtype)


def merge_kernel(rows, *refs):
    parts, out = refs[:4], refs[5]
    chip = lax.axis_index("sp") // 2
    if rows:
        for step, part in enumerate(parts):
            out[shard_rows(chip ^ step, rows), :] = part[:rows]
    rest = [part[rows:].astype(f32) for part in parts]
    out[4 * rows :] = ((rest[0] + rest[1]) + (rest[2] + rest[3])).astype(out.dtype)


def final_kernel(mine, other, query_w, keyval_w, output_w, hidden_w, return_w):
    shard, dim = query_w.shape
    low, high = both_halves(mine, other)
    low, high = low.astype(f32), high.astype(f32)
    for chunk in range(hidden_w.shape[1] // dim):
        hidden_w[:, chunk * dim : (chunk + 1) * dim] = low[chunk * shard : (chunk + 1) * shard]
    return_w[...] = high[:dim]
    low, high = low[dim:], high[dim:]
    query_w[...] = low[:shard]
    keyval_w[:, :dim] = low[shard : 2 * shard]
    keyval_w[:, dim:] = high[:shard]
    output_w[...] = high[shard : 2 * shard]


def final_small_kernel(n_fs, mine, other, reduce_w, *outs):
    smalls, hidden_b = outs[:-1], outs[-1]
    dim = reduce_w.shape[0]
    shard = dim // n_fs
    half = dim // 2
    fs = lax.axis_index("fs")
    low, high = both_halves(mine, other)
    low, high = low.astype(f32), high.astype(f32)
    reduce_w[:half] = low[:half]
    reduce_w[half:] = high[:half]
    vecs = low[half:] + high[half:]
    lane = lax.broadcasted_iota(jnp.int32, vecs.shape, 1)
    chosen = jnp.where(lane // shard == fs, vecs, 0.0)
    folded = chosen[:, :shard]
    for index in range(1, n_fs):
        folded = folded + chosen[:, index * shard : (index + 1) * shard]
    for index, small in enumerate(smalls):
        small[...] = folded[index : index + 1].reshape(shard)
    row = lax.broadcasted_iota(jnp.int32, vecs.shape, 0)
    hidden_b[...] = jnp.sum(jnp.where(row == HIDDEN_B + fs, vecs, 0.0), axis=0)


def rotate(value, n, step):
    return lax.ppermute(value, "fs", [(i, (i + step) % n) for i in range(n)])


def flip(value, n, bits):
    return lax.ppermute(value, "sp", [(i, i ^ bits) for i in range(n)])


def sum_over_rows(value, n_sp):
    bit = 2
    while bit < n_sp:
        if 2 * bit < n_sp:
            a, b, c = flip(value, n_sp, bit), flip(value, n_sp, 2 * bit), flip(value, n_sp, 3 * bit)
            value = (
                (value.astype(f32) + a.astype(f32)) + (b.astype(f32) + c.astype(f32))
            ).astype(value.dtype)
            bit = 4 * bit
        else:
            a = flip(value, n_sp, bit)
            value = (value.astype(f32) + a.astype(f32)).astype(value.dtype)
            bit = 2 * bit
    return value


def exchange(pieces, n_sp):
    return [pieces[0]] + [flip(pieces[step], n_sp, 2 * step) for step in range(1, n_sp // 2)]


def to_owners(pieces, n_fs):
    return [pieces[0]] + [rotate(pieces[step], n_fs, step) for step in range(1, n_fs)]


def call(kernel, out_shape, in_specs=None, scratch=(), limit=SMALL_VMEM, micros=0):
    specs = {} if in_specs is None else {"in_specs": in_specs}
    return pl.pallas_call(
        kernel,
        out_shape=out_shape,
        **specs,
        scratch_shapes=scratch,
        compiler_params=pltpu.CompilerParams(vmem_limit_bytes=limit),
        cost_estimate=pl.CostEstimate(flops=int(micros * 1e9), bytes_accessed=0, transcendentals=0),
    )


def on_device(
    n_fs,
    n_sp,
    tokens,
    cotangent,
    image_sizes,
    first_gain,
    first_bias,
    query_weight,
    query_bias,
    reduce_weight,
    reduce_bias,
    keys_gain,
    keys_bias,
    keyval_weight,
    value_bias,
    output_weight,
    output_bias,
    second_gain,
    second_bias,
    hidden_weight,
    hidden_bias,
    return_weight,
    return_bias,
):
    batches, _, row_dev, cols, dim = tokens.shape
    hid = hidden_weight.shape[1]
    tok = row_dev * cols
    key_dev = tok // 4
    keys = n_sp * key_dev
    shard = dim // n_fs
    half = dim // 2
    vmem = pl.BlockSpec(memory_space=pltpu.VMEM)
    smem = pl.BlockSpec(memory_space=pltpu.SMEM)
    single = keys <= KEY_BLOCK
    split = n_sp == 8
    block = keys if single else KEY_BLOCK
    limit = MAIN_VMEM if single else WHOLE_VMEM

    def shape(*dims, dtype=bf16):
        return jax.ShapeDtypeStruct(dims, dtype)

    smalls = (
        first_gain,
        first_bias,
        query_bias,
        reduce_bias,
        keys_gain,
        keys_bias,
        value_bias,
        output_bias,
        second_gain,
        second_bias,
        return_bias,
    )
    first_half = call(
        functools.partial(pack_first_kernel, n_fs),
        shape(half + VECS + 3 * shard // 2, dim),
        scratch=[pltpu.VMEM((VECS, dim), f32)],
        limit=WHOLE_VMEM,
    )(*smalls, hidden_bias, reduce_weight, query_weight, keyval_weight)
    mine_first = to_owners([first_half] * n_fs, n_fs)[1:]

    begun = call(
        functools.partial(begin_kernel, (n_sp, batches, row_dev, cols, dim)),
        [
            shape(batches * tok, dim, dtype=f32),
            shape(batches * tok, 128, dtype=f32),
            shape(batches * tok, dim, dtype=f32),
            shape(batches, keys, dim),
            shape(dim, dim),
            shape(shard, dim),
            shape(shard, 2 * dim),
            shape(VECS, dim, dtype=f32),
            shape(dim + shard // 2, dim),
        ],
        in_specs=[smem] + [vmem] * 8,
        limit=SMALL_VMEM if single else WHOLE_VMEM,
    )(
        image_sizes,
        tokens,
        reduce_weight,
        query_weight,
        keyval_weight,
        hidden_weight,
        return_weight,
        output_weight,
        first_half,
    )
    normal_first, rstd_first, mask, bias, own_r, own_q, own_kv, own_vec, second_half = begun
    mine_first = call(functools.partial(relay_kernel, n_fs - 1), [shape(*first_half.shape)] * (n_fs - 1))(
        *mine_first, own_vec
    )
    other_first = [flip(piece, n_sp, 1) for piece in mine_first]
    normed, patch_cols, patch_send, reduced, key_low, whole_reduce, wq, wkv, vec, second_half = call(
        functools.partial(reduce_kernel, (n_fs, batches, row_dev, cols, dim)),
        [
            shape(batches * tok, dim),
            shape(4, batches * key_dev, half),
            shape(4, batches * key_dev, half),
            shape(batches * key_dev, dim, dtype=f32),
            shape(batches * key_dev, dim),
            shape(n_fs, dim, dim),
            shape(dim, dim),
            shape(dim, 2 * dim),
            shape(VECS, dim, dtype=f32),
            shape(dim + shard // 2, dim),
        ],
        scratch=[pltpu.VMEM((batches * key_dev, 4 * dim), bf16), pltpu.VMEM((dim // 128, tok, 128), f32)],
    )(normal_first, mask, own_r, own_q, own_kv, own_vec, second_half, *mine_first, *other_first)
    mine_second = to_owners([second_half] * n_fs, n_fs)[1:]

    if split:
        same = exchange([key_low] * (n_sp // 2), n_sp)
        key_pieces = [piece for part in same for piece in (part, flip(part, n_sp, 1))]
    else:
        key_pieces = [lax.all_gather(key_low, "sp")]
    n_pieces = len(key_pieces)

    attended, *kept = call(
        functools.partial(forward_kernel, (batches, tok, key_dev, keys, block, n_pieces)),
        [shape(batches * tok, dim)]
        + [shape(tok, dim)] * batches
        + [shape(keys, 2 * dim)] * batches
        + [shape(dim, tok, dtype=f32)] * batches
        + [shape(PAIRS, 8, 2 * tok, dtype=f32)] * batches
        + [shape(PAIRS, keys, 2 * tok) if single else shape(16, 128)] * batches,
        scratch=[pltpu.VMEM((2, block, 2 * tok) if single else (8, 128), f32)],
        limit=limit,
    )(normed, vec, bias, wq, wkv, *key_pieces)
    kept = [kept[batch::batches] for batch in range(batches)]
    mine_second = call(functools.partial(relay_kernel, n_fs - 1), [shape(dim + shard // 2, dim)] * (n_fs - 1))(
        *mine_second, kept[0][3]
    )
    patch_other = flip(patch_send, n_sp, 1)
    other_second = [flip(piece, n_sp, 1) for piece in mine_second]

    acts, normal, rstd, grad_second, keep_a, send_a, wo = call(
        functools.partial(mlp_kernel, (n_fs, batches, row_dev, cols, dim, hid)),
        [
            shape(batches, 1, row_dev, cols, dim, dtype=f32),
            shape(batches * tok, dim, dtype=f32),
            shape(batches * tok, 128, dtype=f32),
            shape(batches * tok + 8, dim, dtype=f32),
            shape(n_fs, dim, dim),
            shape(n_fs, dim, dim),
            shape(dim, dim),
        ],
        scratch=[
            pltpu.VMEM((dim, hid), bf16),
            pltpu.VMEM((hid, dim), bf16),
            pltpu.VMEM((8, dim), f32),
            pltpu.VMEM((n_fs, dim, dim), bf16),
            pltpu.VMEM((n_fs, dim, dim), bf16),
        ],
        limit=limit,
    )(
        tokens,
        cotangent,
        mask,
        attended,
        vec,
        hidden_weight,
        return_weight,
        output_weight,
        *mine_second,
        *other_second,
        patch_other,
    )
    arrived_a = flip(send_a, n_sp, 1)
    middle, gatt, gvec_a = call(
        functools.partial(middle_kernel, (batches, tok, hid // dim)),
        [shape(batches * tok, dim, dtype=f32), shape(batches * tok, dim), shape(VECS, dim, dtype=f32)],
        limit=limit,
    )(cotangent, mask, normal, rstd, grad_second, vec, wo)

    gkey_dims = (n_sp // 2, key_dev, dim) if split else (n_sp, key_dev, dim)
    back = []
    for batch in range(batches):
        queries, kvs, attf, stats, probs = kept[batch]
        order = vec
        if split and batch == batches - 1:
            pieces_a = call(chip_kernel, [shape(n_fs, dim // 4, dim)] * 4)(keep_a, arrived_a, back[0][5])
            total_a = call(chip_sum_kernel, shape(n_fs, dim // 4, dim), micros=5)(*exchange(pieces_a, n_sp))
            order = pieces_a[0]
        back.append(
            call(
                functools.partial(backward_kernel, (n_sp, batch, tok, key_dev, keys, block, n_pieces)),
                [
                    shape(*gkey_dims),
                    shape(*(gkey_dims if split else (16, 128))),
                    shape(PAIRS, keys, 2 * tok) if single else shape(dim, tok, dtype=f32),
                    shape(keys, dim),
                    shape(keys, dim),
                    shape(8, dim, dtype=f32),
                ],
                scratch=() if single else [pltpu.VMEM((keys, dim), f32)] * 2,
                limit=limit,
            )(gatt, queries, kvs, attf, stats, probs, bias, wkv, order)
        )
    near = [results[0] for results in back]
    keep_c, send_c, gnormed, gvec_c = call(
        functools.partial(query_kernel, (n_fs, batches, tok, key_dev, keys, block, n_pieces)),
        [
            shape(n_fs, half, dim),
            shape(n_fs, half, dim),
            shape(batches * tok, dim, dtype=f32),
            shape(VECS, dim, dtype=f32),
        ],
        scratch=[pltpu.VMEM((dim, tok), f32)],
        limit=limit,
    )(
        normed,
        wq,
        attended,
        middle,
        vec,
        *[kept[batch][1] for batch in range(batches)],
        *[results[2] for results in back],
        *[results[3] for results in back],
        *[results[4] for results in back],
        *[results[5] for results in back],
        *key_pieces,
    )
    arrived_c = flip(send_c, n_sp, 1)
    if split:
        far = [flip(results[1], n_sp, 1) for results in back]
        sums = call(functools.partial(key_sum_kernel, batches), [shape(batches * key_dev, dim)] * 4)(
            *near, *far, total_a, gvec_c
        )
        parts = exchange(sums, n_sp)
    else:
        parts = [lax.all_to_all(jnp.concatenate(near, axis=1), "sp", 0, 0)]
    *grad_reduced, gvec_b = call(
        functools.partial(reduction_kernel, len(parts), batches),
        [shape(key_dev, dim)] * batches + [shape(VECS, dim, dtype=f32)],
    )(reduced, vec, *parts)
    grad_other = [flip(part, n_sp, 1) for part in grad_reduced]
    grad_normed, vectors = call(
        functools.partial(normed_kernel, (batches, row_dev, cols, dim)),
        [shape(batches * tok, dim, dtype=f32), shape(VECS, dim)],
        scratch=[pltpu.VMEM((dim // 128, tok, 128), f32)],
    )(gnormed, mask, whole_reduce, normal_first, gvec_a, gvec_b, gvec_c, *grad_reduced)
    grads, done = call(
        functools.partial(input_kernel, (batches, row_dev, cols, dim)),
        [shape(batches, 1, row_dev, cols, dim, dtype=f32), shape(8, 128, dtype=f32)],
    )(middle, grad_normed, normal_first, rstd_first, vec)

    chunks_b = call(functools.partial(weight_kernel, batches), [shape(half + VECS, dim)] * n_fs)(
        patch_cols, patch_other, *grad_reduced, *grad_other, vectors
    )
    if split:
        rows = dim // 4
        chunks = call(owners_kernel, [shape(rows + half, dim)] * n_fs)(total_a, keep_c, arrived_c)
        join = functools.partial(join_kernel, n_fs)
        joined_a = call(join, shape(rows + half, dim))(*to_owners(chunks, n_fs), done)
        joined_b = call(join, shape(half + VECS, dim), micros=1)(*to_owners(chunks_b, n_fs), done)
        mine = call(functools.partial(merge_kernel, rows), shape(4 * rows + half, dim))(
            *exchange([joined_a] * 4, n_sp), joined_b
        )
        mine_b = call(functools.partial(merge_kernel, 0), shape(half + VECS, dim))(
            *exchange([joined_b] * 4, n_sp), mine
        )
    else:
        groups = [to_owners(chunks_b, n_fs)]
        for keep, arrived in ((keep_c, arrived_c), (keep_a, arrived_a)):
            pieces = call(owner_kernel, [shape(*keep.shape[1:])] * n_fs)(keep, arrived)
            groups.insert(0, to_owners(pieces, n_fs))
        mine_a, mine_c, mine_b = (
            sum_over_rows(sum(piece.astype(f32) for piece in group).astype(bf16), n_sp) for group in groups
        )
        mine = jnp.concatenate([mine_a, mine_c], axis=0)

    gquery, gkeyval, goutput, ghidden, greturn = call(
        final_kernel,
        [
            shape(shard, dim, dtype=f32),
            shape(shard, 2 * dim, dtype=f32),
            shape(shard, dim, dtype=f32),
            shape(shard, hid, dtype=f32),
            shape(dim, dim, dtype=f32),
        ],
    )(mine, flip(mine, n_sp, 1))
    greduce, *vectors = call(
        functools.partial(final_small_kernel, n_fs),
        [shape(dim, dim, dtype=f32)] + [shape(shard, dtype=f32)] * HIDDEN_B + [shape(dim, dtype=f32)],
        micros=10,
    )(mine_b, flip(mine_b, n_sp, 1))
    return (
        acts,
        grads,
        vectors[FIRST_G],
        vectors[FIRST_B],
        gquery,
        vectors[QUERY_B],
        greduce,
        vectors[REDUCE_B],
        vectors[KEYS_G],
        vectors[KEYS_B],
        gkeyval,
        vectors[VALUE_B],
        goutput,
        vectors[OUTPUT_B],
        vectors[SECOND_G],
        vectors[SECOND_B],
        ghidden,
        vectors[HIDDEN_B],
        greturn,
        vectors[RETURN_B],
    )


def solution(mesh):
    vec, mat = P("fs"), P("fs", None)
    image = P(None, "fs", "sp", None, None)
    weights = (vec, vec, mat, vec, mat, vec, vec, vec, mat, vec, mat, vec, vec, vec, mat, vec, mat, vec)
    return jax.shard_map(
        functools.partial(on_device, mesh.shape["fs"], mesh.shape["sp"]),
        mesh=mesh,
        in_specs=(image, image, P(None, "fs", None)) + weights,
        out_specs=(image, image) + weights,
        check_vma=False,
    )
```

```python
import functools

import jax
import jax.numpy as jnp
from jax import lax
from jax.experimental import pallas as pl
from jax.experimental.pallas import tpu as pltpu
from jax.sharding import PartitionSpec as P

HEADS = 8
HDIM = 32
PAIRS = HEADS // 2
SCALE = HDIM ** (-0.5)
EXP_SCALE = SCALE * 1.4426950408889634
EPS = 1e-06
NEG = -1e30
KEY_BLOCK = 768
SMALL_VMEM = 12 * 2**20
MAIN_VMEM = 16 * 2**20
WHOLE_VMEM = 58 * 2**20

bf16 = jnp.bfloat16
f32 = jnp.float32

(
    FIRST_G,
    FIRST_B,
    QUERY_B,
    REDUCE_B,
    KEYS_G,
    KEYS_B,
    VALUE_B,
    OUTPUT_B,
    SECOND_G,
    SECOND_B,
    RETURN_B,
    HIDDEN_B,
) = range(12)
VECS = 16


def mm(left, right):
    return jnp.dot(left, right, preferred_element_type=f32)


def mm_tn(left, right):
    return lax.dot_general(left, right, (((0,), (0,)), ((), ())), preferred_element_type=f32)


def mm_nt(left, right):
    return lax.dot_general(left, right, (((1,), (1,)), ((), ())), preferred_element_type=f32)


def normalize(rows):
    mean = jnp.mean(rows, axis=-1, keepdims=True)
    centered = rows - mean
    var = jnp.mean(centered * centered, axis=-1, keepdims=True)
    rstd = lax.rsqrt(var + EPS)
    return centered * rstd, rstd


def normalize_back(grad, normal, rstd, gain):
    scaled = grad * gain
    mean_a = jnp.mean(scaled, axis=-1, keepdims=True)
    mean_b = jnp.mean(scaled * normal, axis=-1, keepdims=True)
    return (scaled - mean_a - normal * mean_b) * rstd


def token_mask(first_row, rows, cols, width, height, image_width):
    row_ids = lax.broadcasted_iota(jnp.int32, (rows, cols, width), 0) + first_row
    col_ids = lax.broadcasted_iota(jnp.int32, (rows, cols, width), 1)
    valid = (row_ids < height) & (col_ids < image_width)
    return jnp.where(valid, 1.0, 0.0).astype(f32).reshape(rows * cols, width)


def pack_first_kernel(n_fs, *refs):
    smalls, (hidden_b, reduce_w, query_w, keyval_w, first, wide) = take(refs, HIDDEN_B)
    dim = reduce_w.shape[1]
    shard = dim // n_fs
    half = dim // 2
    rest = half + VECS
    fs = lax.axis_index("fs")
    is_low = lax.axis_index("sp") % 2 == 0

    @pl.when(is_low)
    def _():
        first[:half] = reduce_w[:half]
        first[rest : rest + shard] = query_w[...]
        first[rest + shard :] = keyval_w[: shard // 2, :dim]

    @pl.when(jnp.logical_not(is_low))
    def _():
        first[:half] = reduce_w[half:]
        first[rest : rest + shard // 2] = keyval_w[shard // 2 :, :dim]
        first[rest + shard // 2 :] = keyval_w[:, dim:]

    wide[...] = jnp.zeros_like(wide)
    for index, small in enumerate(smalls):
        row = small[...].astype(f32).reshape(1, shard)
        wide[index : index + 1, :] = jnp.concatenate([row] * n_fs, axis=1)
    lane = lax.broadcasted_iota(jnp.int32, wide.shape, 1)
    row = lax.broadcasted_iota(jnp.int32, wide.shape, 0)
    vectors = jnp.where(lane // shard == fs, wide[...], 0.0)
    hidden_row = hidden_b[...].astype(f32).reshape(1, dim)
    first[half:rest] = jnp.where(row == HIDDEN_B + fs, hidden_row, vectors).astype(bf16)


def both_halves(mine, other):
    is_low = lax.axis_index("sp") % 2 == 0
    a, b = mine[...], other[...]
    return jnp.where(is_low, a, b), jnp.where(is_low, b, a)


def shard_rows(place, rows):
    return pl.ds(pl.multiple_of(place * rows, rows), rows)


def begin_kernel(dims, sizes, tokens, reduce_w, query_w, keyval_w, hidden_w, return_w, output_w, packed, *outs):
    n_sp, batches, row_dev, cols, dim = dims
    normal_ref, rstd_ref, mask_ref, bias_ref, own_r, own_q, own_kv, own_vec, second = outs
    tok = row_dev * cols
    half_cols = cols // 2
    rows_dev = row_dev // 2
    half = dim // 2
    shard = hidden_w.shape[0]
    sp = lax.axis_index("sp")
    own_r[...] = reduce_w[...]
    own_q[...] = query_w[...]
    own_kv[...] = keyval_w[...]
    own_vec[...] = packed[half : half + VECS].astype(f32)

    @pl.when(sp % 2 == 0)
    def _():
        for chunk in range(hidden_w.shape[1] // dim):
            second[chunk * shard : (chunk + 1) * shard] = hidden_w[:, chunk * dim : (chunk + 1) * dim]
        second[dim:] = output_w[: shard // 2]

    @pl.when(sp % 2 == 1)
    def _():
        second[:dim] = return_w[...]
        second[dim:] = output_w[shard // 2 :]

    for batch in range(batches):
        height, image_width = sizes[batch, 0, 0], sizes[batch, 0, 1]
        rows = slice(batch * tok, (batch + 1) * tok)
        normal, rstd = normalize(tokens[batch, 0].reshape(tok, dim).astype(f32))
        normal_ref[rows] = normal
        rstd_ref[rows] = jnp.broadcast_to(rstd, (tok, 128))
        mask_ref[rows] = token_mask(sp * row_dev, row_dev, cols, dim, height, image_width)
        col_ids = lax.broadcasted_iota(jnp.int32, (half_cols, dim), 0)

        def key_row_bias(index, _, batch=batch, height=height, image_width=image_width, col_ids=col_ids):
            key_row = index
            if n_sp == 8:
                key_row = (sp ^ (index // rows_dev)) * rows_dev + lax.rem(index, rows_dev)
            width = jnp.where(2 * key_row < height, image_width, 0)
            here = pl.ds(pl.multiple_of(index * half_cols, half_cols), half_cols)
            bias_ref[batch, here, :] = jnp.where(2 * col_ids < width, 0.0, NEG).astype(bf16)
            return 0

        lax.fori_loop(0, n_sp * rows_dev, key_row_bias, 0)


def reduce_kernel(dims, *refs):
    n_fs, batches, row_dev, cols, dim = dims
    ins, mine, other, outs = take(refs, 6, n_fs - 1, n_fs - 1)
    normal_in, mask_ref, own_w, own_q, own_kv, own_vec = ins
    normed_ref, cols_ref, send_ref, reduced_ref, key_ref, weight_ref, wq, wkv, vec_ref, patch_ref, wide = outs
    half = dim // 2
    shard = dim // n_fs
    rest = half + VECS
    tok = row_dev * cols
    half_cols = cols // 2
    key_dev = tok // 4
    fs = lax.axis_index("fs")
    weight_ref[fs] = own_w[...]
    here = shard_rows(fs, shard)
    wq[here, :] = own_q[...]
    wkv[here, :] = own_kv[...]
    vec = own_vec[...]
    for step in range(1, n_fs):
        low, high = both_halves(mine[step - 1], other[step - 1])
        place = lax.rem(fs + n_fs - step, n_fs)
        weight_ref[place, :half] = low[:half]
        weight_ref[place, half:] = high[:half]
        vec = vec + low[half:rest].astype(f32)
        here = shard_rows(place, shard)
        wq[here, :] = low[rest : rest + shard]
        wkv[here, :dim] = jnp.concatenate([low[rest + shard :], high[rest : rest + shard // 2]], axis=0)
        wkv[here, dim:] = high[rest + shard // 2 :]
    vec_ref[...] = vec
    for batch in range(batches):
        rows = slice(batch * tok, (batch + 1) * tok)
        low = (normal_in[rows] * vec[FIRST_G : FIRST_G + 1] + vec[FIRST_B : FIRST_B + 1]).astype(bf16)
        normed_ref[rows] = low
        masked = low.astype(f32) * mask_ref[rows]
        for part in range(dim // 128):
            wide[part] = masked[:, part * 128 : (part + 1) * 128]
        for row in range(row_dev // 2):
            start = batch * key_dev + row * half_cols
            for offset in range(4):
                dr, dc = offset // 2, offset % 2
                for part in range(dim // 128):
                    piece = wide[part, pl.ds((2 * row + dr) * cols + dc, half_cols, stride=2), :]
                    lanes = slice(offset * dim + part * 128, offset * dim + (part + 1) * 128)
                    patch_ref[start : start + half_cols, lanes] = piece.astype(bf16)
    is_low = lax.axis_index("sp") % 2 == 0
    for offset in range(4):
        low = patch_ref[:, offset * dim : offset * dim + half]
        high = patch_ref[:, offset * dim + half : (offset + 1) * dim]
        cols_ref[offset] = jnp.where(is_low, low, high)
        send_ref[offset] = jnp.where(is_low, high, low)
    reduced = mm(patch_ref[...], weight_ref[...].reshape(4 * dim, dim)) + vec[REDUCE_B : REDUCE_B + 1]
    reduced_ref[...] = reduced
    normal, _ = normalize(reduced)
    key_ref[...] = (normal * vec[KEYS_G : KEYS_G + 1] + vec[KEYS_B : KEYS_B + 1]).astype(bf16)


def relay_kernel(n, *refs):
    for source, target in zip(refs[:n], refs[n + 1 :]):
        target[...] = source[...]


def head_stack_t(values_t, pair, tok):
    both = jnp.concatenate([values_t, values_t], axis=1)
    head = lax.broadcasted_iota(jnp.int32, both.shape, 0) // HDIM
    want = 2 * pair + jnp.where(lax.broadcasted_iota(jnp.int32, both.shape, 1) >= tok, 1, 0)
    return jnp.where(head == want, both, jnp.zeros_like(both))


def head_stack(values, pair):
    head = lax.broadcasted_iota(jnp.int32, values.shape, 1) // HDIM
    zero = jnp.zeros_like(values)
    return jnp.concatenate(
        [jnp.where(head == 2 * pair, values, zero), jnp.where(head == 2 * pair + 1, values, zero)],
        axis=0,
    )


def split_pair(both, tok):
    return jnp.concatenate([both[:HDIM, :tok], both[HDIM:, tok:]], axis=0)


def key_rows_of(pieces, key_dev, per_block, batch, index):
    here = slice(batch * key_dev, (batch + 1) * key_dev)
    if len(pieces) > 1:
        return jnp.concatenate([part[here] for part in pieces], axis=0)
    dim = pieces[0].shape[2]
    devices = slice(index * per_block, (index + 1) * per_block)
    return pieces[0][devices, here, :].reshape(per_block * key_dev, dim)


def mask_lane(pair, dim):
    return 0 if pair == PAIRS - 1 else dim - 1


def with_bias(key_block, bias, lane_id):
    lane = lax.broadcasted_iota(jnp.int32, key_block.shape, 1)
    return jnp.where(lane == lane_id, bias.astype(f32), key_block.astype(f32)).astype(bf16)


def query_stack(queries_t, pair, lane_id, tok):
    stacked = head_stack_t(queries_t, pair, tok)
    row = lax.broadcasted_iota(jnp.int32, stacked.shape, 0)
    return jnp.where(row == lane_id, jnp.ones_like(stacked), stacked)


def take(refs, *counts):
    refs = list(refs)
    groups = []
    for count in counts:
        groups.append(refs[:count])
        refs = refs[count:]
    return groups + [refs]


def forward_kernel(dims, *refs):
    batch, tok, key_dev, keys, block, n_pieces = dims
    (normed, vec_ref, bias_ref, wq, wkv), pieces, outs = take(refs, 5, n_pieces)
    attended, queries_out, kvs, attf, stats, probs, wide = outs
    dim = wq.shape[0]
    blocks = keys // block
    per_block = block // key_dev
    queries = (mm(normed[batch * tok : (batch + 1) * tok], wq[...]) + vec_ref[QUERY_B : QUERY_B + 1]).astype(bf16)
    queries_out[...] = queries
    queries_t = queries.T
    for index in range(blocks):
        key_rows = key_rows_of(pieces, key_dev, per_block, batch, index)
        here = slice(index * block, (index + 1) * block)
        kvs[here, :dim] = mm(key_rows, wkv[:, :dim]).astype(bf16)
        value_rows = mm(key_rows, wkv[:, dim:]) + vec_ref[VALUE_B : VALUE_B + 1]
        kvs[here, dim:] = value_rows.astype(bf16)
    if blocks == 1:
        key_block = kvs[:, :dim]
        values_t = kvs[:, dim:].T
        masked = {lane_id: with_bias(key_block, bias_ref[batch], lane_id) for lane_id in (0, dim - 1)}

        def score(pair):
            lane_id = mask_lane(pair, dim)
            wide[pair % 2] = mm(masked[lane_id], query_stack(queries_t, pair, lane_id, tok))

        score(0)
        for pair in range(PAIRS):
            if pair + 1 < PAIRS:
                score(pair + 1)
            heads = slice(2 * HDIM * pair, 2 * HDIM * (pair + 1))
            scores = wide[pair % 2]
            top = jnp.max(scores, axis=0, keepdims=True)
            weights = jnp.exp2((scores - top) * EXP_SCALE)
            inverse = 1.0 / jnp.sum(weights, axis=0, keepdims=True)
            low = weights.astype(bf16)
            probs[pair] = low
            stats[pair, 0:1] = inverse
            mixed = mm(values_t[heads], low) * inverse
            attf[heads] = split_pair(mixed, tok)
    else:
        for pair in range(PAIRS):
            lane_id = mask_lane(pair, dim)
            heads = slice(2 * HDIM * pair, 2 * HDIM * (pair + 1))
            stacked = query_stack(queries_t, pair, lane_id, tok)

            def block_scores(index, stacked=stacked, lane_id=lane_id):
                here = pl.ds(pl.multiple_of(index * block, block), block)
                masked = with_bias(kvs[here, :dim], bias_ref[batch, here, :], lane_id)
                return here, mm(masked, stacked)

            def find_top(index, top, block_scores=block_scores):
                _, scores = block_scores(index)
                return jnp.maximum(top, jnp.max(scores, axis=0, keepdims=True))

            top = lax.fori_loop(0, blocks, find_top, jnp.full((1, 2 * tok), 4 * NEG, f32))

            def add_block(index, carry, block_scores=block_scores, top=top, heads=heads):
                total, mixed = carry
                here, scores = block_scores(index)
                weights = jnp.exp2((scores - top) * EXP_SCALE)
                values_t = kvs[here, dim:].T
                mixed = mixed + mm(values_t[heads], weights.astype(bf16))
                return total + jnp.sum(weights, axis=0, keepdims=True), mixed

            start = (jnp.zeros((1, 2 * tok), f32), jnp.zeros((2 * HDIM, 2 * tok), f32))
            total, mixed = lax.fori_loop(0, blocks, add_block, start)
            inverse = 1.0 / total
            stats[pair, 0:1] = inverse
            stats[pair, 1:2] = top
            attf[heads] = split_pair(mixed * inverse, tok)
    attended[...] = attf[...].T.astype(bf16)


def mlp_kernel(dims, *refs):
    n_fs, batches, row_dev, cols, dim, hid = dims
    ins, attended, own, mine, other, _, outs, scratch = take(refs, 4, batches, 3, n_fs - 1, n_fs - 1, 1, 6)
    tokens, cotangent, mask_ref, vec_ref = ins
    acts_ref, middle_ref, gatt, keep_ref, send_ref, gvec_ref = outs
    wh, wr, wo, lows, highs = scratch
    tok = row_dev * cols
    shard = dim // n_fs
    chunks = hid // dim
    fs = lax.axis_index("fs")
    is_low = lax.axis_index("sp") % 2 == 0
    wh[shard_rows(fs, shard), :] = own[0][...]
    wr[shard_rows(fs, dim), :] = own[1][...]
    wo[shard_rows(fs, shard), :] = own[2][...]
    for step in range(1, n_fs):
        low, high = both_halves(mine[step - 1], other[step - 1])
        place = fs ^ step
        here = shard_rows(place, shard)
        for chunk in range(chunks):
            wh[here, chunk * dim : (chunk + 1) * dim] = low[chunk * shard : (chunk + 1) * shard]
        wr[shard_rows(place, dim), :] = high[:dim]
        wo[here, :] = jnp.concatenate([low[dim:], high[dim:]], axis=0)

    def vec(index):
        return vec_ref[index : index + 1, :]

    x = jnp.concatenate([tokens[b, 0].reshape(tok, dim).astype(f32) for b in range(batches)], axis=0)
    mask = mask_ref[...]
    attended = jnp.concatenate([part[...] for part in attended], axis=0)
    middle = x + mm(attended, wo[...]) + vec(OUTPUT_B)
    normal, rstd = normalize(middle)
    second = (normal * vec(SECOND_G) + vec(SECOND_B)).astype(bf16)
    grad_out = jnp.concatenate([cotangent[b, 0].reshape(tok, dim) for b in range(batches)], axis=0) * mask
    grad_mlp = grad_out.astype(bf16)
    total = middle + vec(RETURN_B)
    grad_second = jnp.zeros((batches * tok, dim), f32)
    gvec_ref[...] = jnp.zeros_like(gvec_ref)
    for chunk in range(chunks):
        lanes = slice(chunk * dim, (chunk + 1) * dim)
        hidden = mm(second, wh[:, lanes]) + vec(HIDDEN_B + chunk)
        phi = 0.5 + 0.5 * lax.erf(hidden * 0.7071067811865476)
        density = 0.3989422804014327 * jnp.exp2(hidden * hidden * (-0.5 * 1.4426950408889634))
        activated = (hidden * phi).astype(bf16)
        total = total + mm(activated, wr[lanes, :])
        grad_activated = mm_nt(grad_mlp, wr[lanes, :])
        grad_hidden = ((phi + hidden * density) * grad_activated).astype(bf16)
        gvec_ref[HIDDEN_B + chunk : HIDDEN_B + chunk + 1] = jnp.sum(
            grad_hidden.astype(f32), axis=0, keepdims=True
        )
        grad_second = grad_second + mm_nt(grad_hidden, wh[:, lanes])
        highs[chunk] = mm_tn(activated, grad_mlp).astype(bf16)
        grad_wh = mm_tn(second, grad_hidden).astype(bf16)
        for owner in range(n_fs):
            lows[owner, chunk * shard : (chunk + 1) * shard] = grad_wh[owner * shard : (owner + 1) * shard]
    low, high = lows[...], highs[...]
    keep_ref[...] = jnp.where(is_low, low, high)
    send_ref[...] = jnp.where(is_low, high, low)
    total = total * mask
    for batch in range(batches):
        acts_ref[batch, 0] = total[batch * tok : (batch + 1) * tok].reshape(row_dev, cols, dim)
    grad_middle = grad_out + normalize_back(grad_second, normal, rstd, vec(SECOND_G))
    middle_ref[...] = grad_middle
    grad_branch = grad_middle.astype(bf16)
    gatt[...] = mm_nt(grad_branch, wo[...]).astype(bf16)
    for index, value in (
        (OUTPUT_B, grad_branch.astype(f32)),
        (SECOND_G, grad_second * normal),
        (SECOND_B, grad_second),
        (RETURN_B, grad_mlp.astype(f32)),
    ):
        gvec_ref[index : index + 1] = jnp.sum(value, axis=0, keepdims=True)


def backward_kernel(dims, *refs):
    n_sp, batch, tok, key_dev, keys, block, n_pieces = dims
    gatt, queries_ref, kvs, attf, stats, probs, bias_ref, wkv, _ = refs[:9]
    near_ref, far_ref, scores_ref, gks, gvs, gvec_ref = refs[9:15]
    dim = wkv.shape[0]
    blocks = keys // block
    per_block = block // key_dev
    rows = slice(batch * tok, (batch + 1) * tok)
    queries = queries_ref[...]
    grad_att_t = gatt[rows].astype(f32).T
    product = grad_att_t * attf[...]

    def pair_terms(pair):
        inverse = stats[pair, 0:1]
        piece = product[2 * HDIM * pair : 2 * HDIM * (pair + 1)]
        delta = jnp.concatenate(
            [jnp.sum(piece[:HDIM], axis=0, keepdims=True), jnp.sum(piece[HDIM:], axis=0, keepdims=True)],
            axis=1,
        )
        stacked = head_stack_t(grad_att_t, pair, tok) * inverse
        return delta * inverse, stacked.astype(bf16)

    if blocks == 1:
        (wide,) = refs[15:]
        values = kvs[:, dim:]
        grad_k = jnp.zeros((keys, dim), f32)
        grad_v = jnp.zeros((keys, dim), f32)
        terms = []

        def grad_prob(pair):
            delta, stacked = pair_terms(pair)
            wide[pair % 2] = mm(values, stacked)
            terms.append((delta, stacked))

        grad_prob(0)
        for pair in range(PAIRS):
            if pair + 1 < PAIRS:
                grad_prob(pair + 1)
            delta, stacked = terms[pair]
            low = probs[pair]
            grad_scores = (low.astype(f32) * (wide[pair % 2] - delta)).astype(bf16)
            scores_ref[pair] = grad_scores
            grad_k = grad_k + mm(grad_scores, head_stack(queries, pair))
            grad_v = grad_v + mm(low, stacked.T)
    else:
        wide_k, wide_v = refs[15:]
        wide_k[...] = jnp.zeros_like(wide_k)
        wide_v[...] = jnp.zeros_like(wide_v)
        queries_t = queries.T
        for pair in range(PAIRS):
            heads = slice(2 * HDIM * pair, 2 * HDIM * (pair + 1))
            lane_id = mask_lane(pair, dim)
            delta, stacked = pair_terms(pair)
            stacked_n = stacked.T
            query_t = query_stack(queries_t, pair, lane_id, tok)
            query_n = head_stack(queries, pair)
            top = stats[pair, 1:2]

            def back_block(index, gq, heads=heads, lane_id=lane_id, delta=delta, stacked=stacked, stacked_n=stacked_n, query_t=query_t, query_n=query_n, top=top):
                here = pl.ds(pl.multiple_of(index * block, block), block)
                key_block = kvs[here, :dim]
                masked = with_bias(key_block, bias_ref[batch, here, :], lane_id)
                weights = jnp.exp2((mm(masked, query_t) - top) * EXP_SCALE)
                grad_probs = mm(kvs[here, dim:], stacked)
                grad_scores = (weights * (grad_probs - delta)).astype(bf16)
                wide_k[here, :] += mm(grad_scores, query_n)
                wide_v[here, :] += mm(weights.astype(bf16), stacked_n)
                return gq + mm(key_block.T[heads], grad_scores)

            gq = lax.fori_loop(0, blocks, back_block, jnp.zeros((2 * HDIM, 2 * tok), f32))
            scores_ref[heads] = split_pair(gq, tok)
    bias_value = jnp.zeros((1, dim), f32)
    for index in range(blocks):
        here = slice(index * block, (index + 1) * block)
        if blocks > 1:
            grad_k, grad_v = wide_k[here], wide_v[here]
        grad_k = (grad_k * SCALE).astype(bf16)
        bias_value = bias_value + jnp.sum(grad_v, axis=0, keepdims=True)
        grad_v = grad_v.astype(bf16)
        gks[here] = grad_k
        gvs[here] = grad_v
        grad_key = (mm_nt(grad_k, wkv[:, :dim]) + mm_nt(grad_v, wkv[:, dim:])).astype(bf16)
        if n_pieces > 1:
            pairs = grad_key.reshape(n_sp // 2, 2, key_dev, dim)
            near_ref[...] = pairs[:, 0]
            far_ref[...] = pairs[:, 1]
        else:
            near_ref[index * per_block : (index + 1) * per_block] = grad_key.reshape(per_block, key_dev, dim)
    gvec_ref[...] = jnp.broadcast_to(bias_value, gvec_ref.shape)


def query_kernel(dims, *refs):
    n_fs, batches, tok, key_dev, keys, block, n_pieces = dims
    ins, attended, kvs, scores, gks, gvs, gvecs, pieces, outs = take(refs, 3, *([batches] * 6), n_pieces)
    normed, wq, middle = ins
    keep_ref, send_ref, gnormed_ref, gvec_ref, wide = outs
    dim = wq.shape[0]
    shard = dim // n_fs
    blocks = keys // block
    per_block = block // key_dev
    grad_queries = []
    grad_wk = jnp.zeros((dim, dim), f32)
    grad_wv = jnp.zeros((dim, dim), f32)
    for batch in range(batches):
        if blocks == 1:
            keys_t = kvs[batch][:, :dim].T
            for pair in range(PAIRS):
                heads = slice(2 * HDIM * pair, 2 * HDIM * (pair + 1))
                wide[heads] = split_pair(mm(keys_t[heads], scores[batch][pair]), tok)
            grad_t = wide[...]
        else:
            grad_t = scores[batch][...]
        grad_queries.append((grad_t.T * SCALE).astype(bf16))
        for index in range(blocks):
            here = slice(index * block, (index + 1) * block)
            key_rows = key_rows_of(pieces, key_dev, per_block, batch, index)
            grad_wk = grad_wk + mm_tn(key_rows, gks[batch][here])
            grad_wv = grad_wv + mm_tn(key_rows, gvs[batch][here])
    grad_queries = jnp.concatenate(grad_queries, axis=0)
    grad_wq = mm_tn(normed[...], grad_queries)
    attended = jnp.concatenate([part[...] for part in attended], axis=0)
    grad_wo = mm_tn(attended, middle[...].astype(bf16))
    is_low = lax.axis_index("sp") % 2 == 0
    for owner in range(n_fs):
        part = slice(owner * shard, (owner + 1) * shard)
        low = jnp.concatenate([grad_wq[part], grad_wk[part]], axis=0).astype(bf16)
        high = jnp.concatenate([grad_wv[part], grad_wo[part]], axis=0).astype(bf16)
        keep_ref[owner] = jnp.where(is_low, low, high)
        send_ref[owner] = jnp.where(is_low, high, low)
    gnormed_ref[...] = mm_nt(grad_queries, wq[...])
    gvec_ref[...] = jnp.zeros_like(gvec_ref)
    gvec_ref[QUERY_B : QUERY_B + 1] = jnp.sum(grad_queries.astype(f32), axis=0, keepdims=True)
    bias_value = gvecs[0][0:1]
    for gvec in gvecs[1:]:
        bias_value = bias_value + gvec[0:1]
    gvec_ref[VALUE_B : VALUE_B + 1] = bias_value


def sum_parts(parts):
    if len(parts) == 1:
        total = parts[0][0].astype(f32)
        for index in range(1, parts[0].shape[0]):
            total = total + parts[0][index].astype(f32)
        return total
    total = parts[0][...].astype(f32)
    for part in parts[1:]:
        total = total + part[...].astype(f32)
    return total


def reduction_kernel(n_parts, batches, reduced, vec_ref, *refs):
    parts, gvec_ref, outs = refs[:n_parts], refs[-1], refs[-1 - batches : -1]
    grad_key = sum_parts(parts)
    normal, rstd = normalize(reduced[...])
    grad_low = normalize_back(grad_key, normal, rstd, vec_ref[KEYS_G : KEYS_G + 1]).astype(bf16)
    rows = outs[0].shape[0]
    for batch, out in enumerate(outs):
        out[...] = grad_low[batch * rows : (batch + 1) * rows]
    gvec_ref[...] = jnp.zeros_like(gvec_ref)
    for index, value in (
        (REDUCE_B, grad_low.astype(f32)),
        (KEYS_G, grad_key * normal),
        (KEYS_B, grad_key),
    ):
        gvec_ref[index : index + 1] = jnp.sum(value, axis=0, keepdims=True)


def weight_kernel(batches, *refs):
    (own_cols, other_cols), own, other, (vectors, *outs) = take(refs, 2, batches, batches)
    fs = lax.axis_index("fs")
    own = jnp.concatenate([part[...] for part in own], axis=0)
    other = jnp.concatenate([part[...] for part in other], axis=0)
    rows = own_cols.shape[2]
    for step, out in enumerate(outs):
        place = lax.rem(fs + step, len(outs))
        out[:rows] = (mm_tn(own_cols[place], own) + mm_tn(other_cols[place], other)).astype(out.dtype)
        out[rows:] = vectors[...]


def normed_kernel(dims, gnormed, mask_ref, weight, normal_ref, vec_a, vec_b, vec_c, *refs):
    batches, row_dev, cols, dim = dims
    grads, (grad_ref, gvec_ref, wide) = take(refs, batches)
    tok = row_dev * cols
    half_cols = cols // 2
    gain_first = jnp.zeros((1, dim), f32)
    bias_first = jnp.zeros((1, dim), f32)
    for batch in range(batches):
        for offset in range(4):
            dr, dc = offset // 2, offset % 2
            back = mm_nt(grads[batch][...], weight[offset])
            for row in range(row_dev // 2):
                for part in range(dim // 128):
                    wide[part, pl.ds((2 * row + dr) * cols + dc, half_cols, stride=2), :] = back[
                        row * half_cols : (row + 1) * half_cols, part * 128 : (part + 1) * 128
                    ]
        rows = slice(batch * tok, (batch + 1) * tok)
        spread = jnp.concatenate([wide[part] for part in range(dim // 128)], axis=1)
        grad_normed = gnormed[rows] + spread * mask_ref[rows]
        grad_ref[rows] = grad_normed
        gain_first = gain_first + jnp.sum(grad_normed * normal_ref[rows], axis=0, keepdims=True)
        bias_first = bias_first + jnp.sum(grad_normed, axis=0, keepdims=True)
    index = lax.broadcasted_iota(jnp.int32, (VECS, dim), 0)
    vectors = vec_a[...] + vec_b[...] + vec_c[...]
    vectors = jnp.where(index == FIRST_G, gain_first, vectors)
    vectors = jnp.where(index == FIRST_B, bias_first, vectors)
    gvec_ref[...] = vectors.astype(bf16)


def input_kernel(dims, middle, grad_normed, normal_ref, rstd_ref, vec_ref, _, grad_ref, done_ref):
    batches, row_dev, cols, dim = dims
    tok = row_dev * cols
    rstd = jnp.concatenate([rstd_ref[...]] * (dim // rstd_ref.shape[1]), axis=1)
    back = normalize_back(grad_normed[...], normal_ref[...], rstd, vec_ref[FIRST_G : FIRST_G + 1])
    grad_x = middle[...] + back
    for batch in range(batches):
        grad_ref[batch, 0] = grad_x[batch * tok : (batch + 1) * tok].reshape(row_dev, cols, dim)
    done_ref[...] = jnp.zeros_like(done_ref)


def key_sum_kernel(batches, *refs):
    near, far, _, outs = take(refs, batches, batches, 2)
    for step, out in enumerate(outs):
        rows = near[0].shape[1]
        for batch in range(batches):
            total = near[batch][step].astype(f32) + far[batch][step].astype(f32)
            out[batch * rows : (batch + 1) * rows] = total.astype(out.dtype)


def owner_kernel(keep, arrived, *outs):
    fs = lax.axis_index("fs")
    for step, out in enumerate(outs):
        place = lax.rem(fs + step, len(outs))
        out[...] = (keep[place].astype(f32) + arrived[place].astype(f32)).astype(out.dtype)


def chip_kernel(keep, arrived, _, *outs):
    chip = lax.axis_index("sp") // 2
    rows = outs[0].shape[1]
    for step, out in enumerate(outs):
        here = shard_rows(chip ^ step, rows)
        out[...] = (keep[:, here, :].astype(f32) + arrived[:, here, :].astype(f32)).astype(out.dtype)


def chip_sum_kernel(*refs):
    refs[-1][...] = sum_parts(refs[:-1]).astype(refs[-1].dtype)


def owners_kernel(total, keep, arrived, *outs):
    fs = lax.axis_index("fs")
    rows = total.shape[1]
    for step, out in enumerate(outs):
        place = lax.rem(fs + step, len(outs))
        out[:rows] = total[place]
        out[rows:] = (keep[place].astype(f32) + arrived[place].astype(f32)).astype(out.dtype)


def join_kernel(n, *refs):
    refs[-1][...] = sum_parts(refs[:n]).astype(refs[-1].dtype)


def merge_kernel(rows, *refs):
    parts, out = refs[:4], refs[5]
    chip = lax.axis_index("sp") // 2
    if rows:
        for step, part in enumerate(parts):
            out[shard_rows(chip ^ step, rows), :] = part[:rows]
    rest = [part[rows:].astype(f32) for part in parts]
    out[4 * rows :] = ((rest[0] + rest[1]) + (rest[2] + rest[3])).astype(out.dtype)


def final_kernel(mine, other, query_w, keyval_w, output_w, hidden_w, return_w):
    shard, dim = query_w.shape
    low, high = both_halves(mine, other)
    low, high = low.astype(f32), high.astype(f32)
    for chunk in range(hidden_w.shape[1] // dim):
        hidden_w[:, chunk * dim : (chunk + 1) * dim] = low[chunk * shard : (chunk + 1) * shard]
    return_w[...] = high[:dim]
    low, high = low[dim:], high[dim:]
    query_w[...] = low[:shard]
    keyval_w[:, :dim] = low[shard : 2 * shard]
    keyval_w[:, dim:] = high[:shard]
    output_w[...] = high[shard : 2 * shard]


def final_small_kernel(n_fs, mine, other, reduce_w, *outs):
    smalls, hidden_b = outs[:-1], outs[-1]
    dim = reduce_w.shape[0]
    shard = dim // n_fs
    half = dim // 2
    fs = lax.axis_index("fs")
    low, high = both_halves(mine, other)
    low, high = low.astype(f32), high.astype(f32)
    reduce_w[:half] = low[:half]
    reduce_w[half:] = high[:half]
    vecs = low[half:] + high[half:]
    lane = lax.broadcasted_iota(jnp.int32, vecs.shape, 1)
    chosen = jnp.where(lane // shard == fs, vecs, 0.0)
    folded = chosen[:, :shard]
    for index in range(1, n_fs):
        folded = folded + chosen[:, index * shard : (index + 1) * shard]
    for index, small in enumerate(smalls):
        small[...] = folded[index : index + 1].reshape(shard)
    row = lax.broadcasted_iota(jnp.int32, vecs.shape, 0)
    hidden_b[...] = jnp.sum(jnp.where(row == HIDDEN_B + fs, vecs, 0.0), axis=0)


def rotate(value, n, step):
    return lax.ppermute(value, "fs", [(i, (i + step) % n) for i in range(n)])


def swap(value, n, bits):
    return lax.ppermute(value, "fs", [(i, i ^ bits) for i in range(n)])


def flip(value, n, bits):
    return lax.ppermute(value, "sp", [(i, i ^ bits) for i in range(n)])


def sum_over_rows(value, n_sp):
    bit = 2
    while bit < n_sp:
        if 2 * bit < n_sp:
            a, b, c = flip(value, n_sp, bit), flip(value, n_sp, 2 * bit), flip(value, n_sp, 3 * bit)
            value = (
                (value.astype(f32) + a.astype(f32)) + (b.astype(f32) + c.astype(f32))
            ).astype(value.dtype)
            bit = 4 * bit
        else:
            a = flip(value, n_sp, bit)
            value = (value.astype(f32) + a.astype(f32)).astype(value.dtype)
            bit = 2 * bit
    return value


def exchange(pieces, n_sp):
    return [pieces[0]] + [flip(pieces[step], n_sp, 2 * step) for step in range(1, n_sp // 2)]


def to_owners(pieces, n_fs):
    return [pieces[0]] + [rotate(pieces[step], n_fs, step) for step in range(1, n_fs)]


def call(kernel, out_shape, in_specs=None, scratch=(), limit=SMALL_VMEM, micros=0):
    specs = {} if in_specs is None else {"in_specs": in_specs}
    return pl.pallas_call(
        kernel,
        out_shape=out_shape,
        **specs,
        scratch_shapes=scratch,
        compiler_params=pltpu.CompilerParams(vmem_limit_bytes=limit),
        cost_estimate=pl.CostEstimate(flops=int(micros * 1e9), bytes_accessed=0, transcendentals=0),
    )


def on_device(
    n_fs,
    n_sp,
    tokens,
    cotangent,
    image_sizes,
    first_gain,
    first_bias,
    query_weight,
    query_bias,
    reduce_weight,
    reduce_bias,
    keys_gain,
    keys_bias,
    keyval_weight,
    value_bias,
    output_weight,
    output_bias,
    second_gain,
    second_bias,
    hidden_weight,
    hidden_bias,
    return_weight,
    return_bias,
):
    batches, _, row_dev, cols, dim = tokens.shape
    hid = hidden_weight.shape[1]
    tok = row_dev * cols
    key_dev = tok // 4
    keys = n_sp * key_dev
    shard = dim // n_fs
    half = dim // 2
    vmem = pl.BlockSpec(memory_space=pltpu.VMEM)
    smem = pl.BlockSpec(memory_space=pltpu.SMEM)
    single = keys <= KEY_BLOCK
    split = n_sp == 8
    block = keys if single else KEY_BLOCK
    limit = MAIN_VMEM if single else WHOLE_VMEM

    def shape(*dims, dtype=bf16):
        return jax.ShapeDtypeStruct(dims, dtype)

    smalls = (
        first_gain,
        first_bias,
        query_bias,
        reduce_bias,
        keys_gain,
        keys_bias,
        value_bias,
        output_bias,
        second_gain,
        second_bias,
        return_bias,
    )
    first_half = call(
        functools.partial(pack_first_kernel, n_fs),
        shape(half + VECS + 3 * shard // 2, dim),
        scratch=[pltpu.VMEM((VECS, dim), f32)],
        limit=WHOLE_VMEM,
    )(*smalls, hidden_bias, reduce_weight, query_weight, keyval_weight)
    mine_first = to_owners([first_half] * n_fs, n_fs)[1:]

    begun = call(
        functools.partial(begin_kernel, (n_sp, batches, row_dev, cols, dim)),
        [
            shape(batches * tok, dim, dtype=f32),
            shape(batches * tok, 128, dtype=f32),
            shape(batches * tok, dim, dtype=f32),
            shape(batches, keys, dim),
            shape(dim, dim),
            shape(shard, dim),
            shape(shard, 2 * dim),
            shape(VECS, dim, dtype=f32),
            shape(dim + shard // 2, dim),
        ],
        in_specs=[smem] + [vmem] * 8,
        limit=SMALL_VMEM if single else WHOLE_VMEM,
    )(
        image_sizes,
        tokens,
        reduce_weight,
        query_weight,
        keyval_weight,
        hidden_weight,
        return_weight,
        output_weight,
        first_half,
    )
    normal_first, rstd_first, mask, bias, own_r, own_q, own_kv, own_vec, second_half = begun
    mine_first = call(functools.partial(relay_kernel, n_fs - 1), [shape(*first_half.shape)] * (n_fs - 1))(
        *mine_first, own_vec
    )
    other_first = [flip(piece, n_sp, 1) for piece in mine_first]
    normed, patch_cols, patch_send, reduced, key_low, whole_reduce, wq, wkv, vec = call(
        functools.partial(reduce_kernel, (n_fs, batches, row_dev, cols, dim)),
        [
            shape(batches * tok, dim),
            shape(4, batches * key_dev, half),
            shape(4, batches * key_dev, half),
            shape(batches * key_dev, dim, dtype=f32),
            shape(batches * key_dev, dim),
            shape(n_fs, dim, dim),
            shape(dim, dim),
            shape(dim, 2 * dim),
            shape(VECS, dim, dtype=f32),
        ],
        scratch=[pltpu.VMEM((batches * key_dev, 4 * dim), bf16), pltpu.VMEM((dim // 128, tok, 128), f32)],
    )(normal_first, mask, own_r, own_q, own_kv, own_vec, *mine_first, *other_first)
    across = swap(second_half, n_fs, 2)
    passed = call(functools.partial(relay_kernel, 1), [shape(dim + shard // 2, dim)], micros=15)(across, own_vec)
    mine_second = [swap(second_half, n_fs, 1), across, swap(passed[0], n_fs, 1)]

    if split:
        same = exchange([key_low] * (n_sp // 2), n_sp)
        key_pieces = [piece for part in same for piece in (part, flip(part, n_sp, 1))]
    else:
        key_pieces = [lax.all_gather(key_low, "sp")]
    n_pieces = len(key_pieces)

    kept = [
        call(
            functools.partial(forward_kernel, (batch, tok, key_dev, keys, block, n_pieces)),
            [
                shape(tok, dim),
                shape(tok, dim),
                shape(keys, 2 * dim),
                shape(dim, tok, dtype=f32),
                shape(PAIRS, 8, 2 * tok, dtype=f32),
                shape(PAIRS, keys, 2 * tok) if single else shape(16, 128),
            ],
            scratch=[pltpu.VMEM((2, block, 2 * tok) if single else (8, 128), f32)],
            limit=limit,
        )(normed, vec, bias, wq, wkv, *key_pieces)
        for batch in range(batches)
    ]
    attended = [results[0] for results in kept]
    kept = [results[1:] for results in kept]
    mine_second = call(functools.partial(relay_kernel, n_fs - 1), [shape(dim + shard // 2, dim)] * (n_fs - 1))(
        *mine_second, kept[0][3]
    )
    patch_other = flip(patch_send, n_sp, 1)
    other_second = [flip(piece, n_sp, 1) for piece in mine_second]

    acts, middle, gatt, keep_a, send_a, gvec_a = call(
        functools.partial(mlp_kernel, (n_fs, batches, row_dev, cols, dim, hid)),
        [
            shape(batches, 1, row_dev, cols, dim, dtype=f32),
            shape(batches * tok, dim, dtype=f32),
            shape(batches * tok, dim),
            shape(n_fs, dim, dim),
            shape(n_fs, dim, dim),
            shape(VECS, dim, dtype=f32),
        ],
        scratch=[
            pltpu.VMEM((dim, hid), bf16),
            pltpu.VMEM((hid, dim), bf16),
            pltpu.VMEM((dim, dim), bf16),
            pltpu.VMEM((n_fs, dim, dim), bf16),
            pltpu.VMEM((n_fs, dim, dim), bf16),
        ],
        limit=limit,
    )(
        tokens,
        cotangent,
        mask,
        vec,
        *attended,
        hidden_weight,
        return_weight,
        output_weight,
        *mine_second,
        *other_second,
        patch_other,
    )
    arrived_a = flip(send_a, n_sp, 1)
    gkey_dims = (n_sp // 2, key_dev, dim) if split else (n_sp, key_dev, dim)
    back = []
    for batch in range(batches):
        queries, kvs, attf, stats, probs = kept[batch]
        order = vec
        if split and batch == batches - 1:
            pieces_a = call(chip_kernel, [shape(n_fs, dim // 4, dim)] * 4)(keep_a, arrived_a, back[0][5])
            total_a = call(chip_sum_kernel, shape(n_fs, dim // 4, dim), micros=5)(*exchange(pieces_a, n_sp))
            order = pieces_a[0]
        back.append(
            call(
                functools.partial(backward_kernel, (n_sp, batch, tok, key_dev, keys, block, n_pieces)),
                [
                    shape(*gkey_dims),
                    shape(*(gkey_dims if split else (16, 128))),
                    shape(PAIRS, keys, 2 * tok) if single else shape(dim, tok, dtype=f32),
                    shape(keys, dim),
                    shape(keys, dim),
                    shape(8, dim, dtype=f32),
                ],
                scratch=[pltpu.VMEM((2, keys, 2 * tok), f32)] if single else [pltpu.VMEM((keys, dim), f32)] * 2,
                limit=limit,
            )(gatt, queries, kvs, attf, stats, probs, bias, wkv, order)
        )
    near = [results[0] for results in back]
    keep_c, send_c, gnormed, gvec_c = call(
        functools.partial(query_kernel, (n_fs, batches, tok, key_dev, keys, block, n_pieces)),
        [
            shape(n_fs, half, dim),
            shape(n_fs, half, dim),
            shape(batches * tok, dim, dtype=f32),
            shape(VECS, dim, dtype=f32),
        ],
        scratch=[pltpu.VMEM((dim, tok), f32)],
        limit=limit,
    )(
        normed,
        wq,
        middle,
        *attended,
        *[kept[batch][1] for batch in range(batches)],
        *[results[2] for results in back],
        *[results[3] for results in back],
        *[results[4] for results in back],
        *[results[5] for results in back],
        *key_pieces,
    )
    arrived_c = flip(send_c, n_sp, 1)
    if split:
        far = [flip(results[1], n_sp, 1) for results in back]
        sums = call(functools.partial(key_sum_kernel, batches), [shape(batches * key_dev, dim)] * 4)(
            *near, *far, total_a, gvec_c
        )
        parts = exchange(sums, n_sp)
    else:
        parts = [lax.all_to_all(jnp.concatenate(near, axis=1), "sp", 0, 0)]
    *grad_reduced, gvec_b = call(
        functools.partial(reduction_kernel, len(parts), batches),
        [shape(key_dev, dim)] * batches + [shape(VECS, dim, dtype=f32)],
    )(reduced, vec, *parts)
    grad_other = [flip(part, n_sp, 1) for part in grad_reduced]
    grad_normed, vectors = call(
        functools.partial(normed_kernel, (batches, row_dev, cols, dim)),
        [shape(batches * tok, dim, dtype=f32), shape(VECS, dim)],
        scratch=[pltpu.VMEM((dim // 128, tok, 128), f32)],
    )(gnormed, mask, whole_reduce, normal_first, gvec_a, gvec_b, gvec_c, *grad_reduced)
    chunks_b = call(functools.partial(weight_kernel, batches), [shape(half + VECS, dim)] * n_fs)(
        patch_cols, patch_other, *grad_reduced, *grad_other, vectors
    )
    if split:
        rows = dim // 4
        chunks = call(owners_kernel, [shape(rows + half, dim)] * n_fs)(total_a, keep_c, arrived_c)
        join = functools.partial(join_kernel, n_fs)
        joined_a = call(join, shape(rows + half, dim), micros=5)(*to_owners(chunks, n_fs), vec)
        order = joined_a
    else:
        order = vec
    grads, done = call(
        functools.partial(input_kernel, (batches, row_dev, cols, dim)),
        [shape(batches, 1, row_dev, cols, dim, dtype=f32), shape(8, 128, dtype=f32)],
    )(middle, grad_normed, normal_first, rstd_first, vec, order)

    if split:
        joined_b = call(join, shape(half + VECS, dim), micros=1)(*to_owners(chunks_b, n_fs), done)
        mine = call(functools.partial(merge_kernel, rows), shape(4 * rows + half, dim))(
            *exchange([joined_a] * 4, n_sp), joined_b
        )
        mine_b = call(functools.partial(merge_kernel, 0), shape(half + VECS, dim))(
            *exchange([joined_b] * 4, n_sp), mine
        )
    else:
        groups = [to_owners(chunks_b, n_fs)]
        for keep, arrived in ((keep_c, arrived_c), (keep_a, arrived_a)):
            pieces = call(owner_kernel, [shape(*keep.shape[1:])] * n_fs)(keep, arrived)
            groups.insert(0, to_owners(pieces, n_fs))
        mine_a, mine_c, mine_b = (
            sum_over_rows(sum(piece.astype(f32) for piece in group).astype(bf16), n_sp) for group in groups
        )
        mine = jnp.concatenate([mine_a, mine_c], axis=0)

    gquery, gkeyval, goutput, ghidden, greturn = call(
        final_kernel,
        [
            shape(shard, dim, dtype=f32),
            shape(shard, 2 * dim, dtype=f32),
            shape(shard, dim, dtype=f32),
            shape(shard, hid, dtype=f32),
            shape(dim, dim, dtype=f32),
        ],
    )(mine, flip(mine, n_sp, 1))
    greduce, *vectors = call(
        functools.partial(final_small_kernel, n_fs),
        [shape(dim, dim, dtype=f32)] + [shape(shard, dtype=f32)] * HIDDEN_B + [shape(dim, dtype=f32)],
        micros=3,
    )(mine_b, flip(mine_b, n_sp, 1))
    return (
        acts,
        grads,
        vectors[FIRST_G],
        vectors[FIRST_B],
        gquery,
        vectors[QUERY_B],
        greduce,
        vectors[REDUCE_B],
        vectors[KEYS_G],
        vectors[KEYS_B],
        gkeyval,
        vectors[VALUE_B],
        goutput,
        vectors[OUTPUT_B],
        vectors[SECOND_G],
        vectors[SECOND_B],
        ghidden,
        vectors[HIDDEN_B],
        greturn,
        vectors[RETURN_B],
    )


def solution(mesh):
    vec, mat = P("fs"), P("fs", None)
    image = P(None, "fs", "sp", None, None)
    weights = (vec, vec, mat, vec, mat, vec, vec, vec, mat, vec, mat, vec, vec, vec, mat, vec, mat, vec)
    return jax.shard_map(
        functools.partial(on_device, mesh.shape["fs"], mesh.shape["sp"]),
        mesh=mesh,
        in_specs=(image, image, P(None, "fs", None)) + weights,
        out_specs=(image, image) + weights,
        check_vma=False,
    )
```

```python
import functools

import jax
import jax.numpy as jnp
from jax import lax
from jax.experimental import pallas as pl
from jax.experimental.pallas import tpu as pltpu
from jax.sharding import PartitionSpec as P

HEADS = 8
HDIM = 32
PAIRS = HEADS // 2
SCALE = HDIM ** (-0.5)
EXP_SCALE = SCALE * 1.4426950408889634
EPS = 1e-06
NEG = -1e30
KEY_BLOCK = 768
SMALL_VMEM = 12 * 2**20
MAIN_VMEM = 16 * 2**20
WHOLE_VMEM = 58 * 2**20

bf16 = jnp.bfloat16
f32 = jnp.float32

(
    FIRST_G,
    FIRST_B,
    QUERY_B,
    REDUCE_B,
    KEYS_G,
    KEYS_B,
    VALUE_B,
    OUTPUT_B,
    SECOND_G,
    SECOND_B,
    RETURN_B,
    HIDDEN_B,
) = range(12)
VECS = 16


def mm(left, right):
    return jnp.dot(left, right, preferred_element_type=f32)


def mm_tn(left, right):
    return lax.dot_general(left, right, (((0,), (0,)), ((), ())), preferred_element_type=f32)


def mm_nt(left, right):
    return lax.dot_general(left, right, (((1,), (1,)), ((), ())), preferred_element_type=f32)


def normalize(rows):
    mean = jnp.mean(rows, axis=-1, keepdims=True)
    centered = rows - mean
    var = jnp.mean(centered * centered, axis=-1, keepdims=True)
    rstd = lax.rsqrt(var + EPS)
    return centered * rstd, rstd


def normalize_back(grad, normal, rstd, gain):
    scaled = grad * gain
    mean_a = jnp.mean(scaled, axis=-1, keepdims=True)
    mean_b = jnp.mean(scaled * normal, axis=-1, keepdims=True)
    return (scaled - mean_a - normal * mean_b) * rstd


def token_mask(first_row, rows, cols, width, height, image_width):
    row_ids = lax.broadcasted_iota(jnp.int32, (rows, cols, width), 0) + first_row
    col_ids = lax.broadcasted_iota(jnp.int32, (rows, cols, width), 1)
    valid = (row_ids < height) & (col_ids < image_width)
    return jnp.where(valid, 1.0, 0.0).astype(f32).reshape(rows * cols, width)


def pack_first_kernel(n_fs, *refs):
    smalls, (hidden_b, reduce_w, query_w, keyval_w, first, wide) = take(refs, HIDDEN_B)
    dim = reduce_w.shape[1]
    shard = dim // n_fs
    half = dim // 2
    rest = half + VECS
    fs = lax.axis_index("fs")
    is_low = lax.axis_index("sp") % 2 == 0

    @pl.when(is_low)
    def _():
        first[:half] = reduce_w[:half]
        first[rest : rest + shard] = query_w[...]
        first[rest + shard :] = keyval_w[: shard // 2, :dim]

    @pl.when(jnp.logical_not(is_low))
    def _():
        first[:half] = reduce_w[half:]
        first[rest : rest + shard // 2] = keyval_w[shard // 2 :, :dim]
        first[rest + shard // 2 :] = keyval_w[:, dim:]

    wide[...] = jnp.zeros_like(wide)
    for index, small in enumerate(smalls):
        row = small[...].astype(f32).reshape(1, shard)
        wide[index : index + 1, :] = jnp.concatenate([row] * n_fs, axis=1)
    lane = lax.broadcasted_iota(jnp.int32, wide.shape, 1)
    row = lax.broadcasted_iota(jnp.int32, wide.shape, 0)
    vectors = jnp.where(lane // shard == fs, wide[...], 0.0)
    hidden_row = hidden_b[...].astype(f32).reshape(1, dim)
    first[half:rest] = jnp.where(row == HIDDEN_B + fs, hidden_row, vectors).astype(bf16)


def both_halves(mine, other):
    is_low = lax.axis_index("sp") % 2 == 0
    a, b = mine[...], other[...]
    return jnp.where(is_low, a, b), jnp.where(is_low, b, a)


def shard_rows(place, rows):
    return pl.ds(pl.multiple_of(place * rows, rows), rows)


def begin_kernel(dims, sizes, tokens, reduce_w, query_w, keyval_w, hidden_w, return_w, output_w, packed, *outs):
    n_sp, batches, row_dev, cols, dim = dims
    normal_ref, rstd_ref, mask_ref, bias_ref, own_r, own_q, own_kv, own_vec, second = outs
    tok = row_dev * cols
    half_cols = cols // 2
    rows_dev = row_dev // 2
    half = dim // 2
    shard = hidden_w.shape[0]
    sp = lax.axis_index("sp")
    own_r[...] = reduce_w[...]
    own_q[...] = query_w[...]
    own_kv[...] = keyval_w[...]
    own_vec[...] = packed[half : half + VECS].astype(f32)

    @pl.when(sp % 2 == 0)
    def _():
        for chunk in range(hidden_w.shape[1] // dim):
            second[chunk * shard : (chunk + 1) * shard] = hidden_w[:, chunk * dim : (chunk + 1) * dim]
        second[dim:] = output_w[: shard // 2]

    @pl.when(sp % 2 == 1)
    def _():
        second[:dim] = return_w[...]
        second[dim:] = output_w[shard // 2 :]

    for batch in range(batches):
        height, image_width = sizes[batch, 0, 0], sizes[batch, 0, 1]
        rows = slice(batch * tok, (batch + 1) * tok)
        normal, rstd = normalize(tokens[batch, 0].reshape(tok, dim).astype(f32))
        normal_ref[rows] = normal
        rstd_ref[rows] = jnp.broadcast_to(rstd, (tok, 128))
        mask_ref[rows] = token_mask(sp * row_dev, row_dev, cols, dim, height, image_width)
        col_ids = lax.broadcasted_iota(jnp.int32, (half_cols, dim), 0)

        def key_row_bias(index, _, batch=batch, height=height, image_width=image_width, col_ids=col_ids):
            key_row = index
            if n_sp == 8:
                key_row = (sp ^ (index // rows_dev)) * rows_dev + lax.rem(index, rows_dev)
            width = jnp.where(2 * key_row < height, image_width, 0)
            here = pl.ds(pl.multiple_of(index * half_cols, half_cols), half_cols)
            bias_ref[batch, here, :] = jnp.where(2 * col_ids < width, 0.0, NEG).astype(bf16)
            return 0

        lax.fori_loop(0, n_sp * rows_dev, key_row_bias, 0)


def reduce_kernel(dims, *refs):
    n_fs, batches, row_dev, cols, dim = dims
    ins, mine, other, outs = take(refs, 6, n_fs - 1, n_fs - 1)
    normal_in, mask_ref, own_w, own_q, own_kv, own_vec = ins
    normed_ref, cols_ref, send_ref, reduced_ref, key_ref, weight_ref, wq, wkv, vec_ref, patch_ref, wide = outs
    half = dim // 2
    shard = dim // n_fs
    rest = half + VECS
    tok = row_dev * cols
    half_cols = cols // 2
    key_dev = tok // 4
    fs = lax.axis_index("fs")
    weight_ref[fs] = own_w[...]
    here = shard_rows(fs, shard)
    wq[here, :] = own_q[...]
    wkv[here, :] = own_kv[...]
    vec = own_vec[...]
    for step in range(1, n_fs):
        low, high = both_halves(mine[step - 1], other[step - 1])
        place = lax.rem(fs + n_fs - step, n_fs)
        weight_ref[place, :half] = low[:half]
        weight_ref[place, half:] = high[:half]
        vec = vec + low[half:rest].astype(f32)
        here = shard_rows(place, shard)
        wq[here, :] = low[rest : rest + shard]
        wkv[here, :dim] = jnp.concatenate([low[rest + shard :], high[rest : rest + shard // 2]], axis=0)
        wkv[here, dim:] = high[rest + shard // 2 :]
    vec_ref[...] = vec
    for batch in range(batches):
        rows = slice(batch * tok, (batch + 1) * tok)
        low = (normal_in[rows] * vec[FIRST_G : FIRST_G + 1] + vec[FIRST_B : FIRST_B + 1]).astype(bf16)
        normed_ref[rows] = low
        masked = low.astype(f32) * mask_ref[rows]
        for part in range(dim // 128):
            wide[part] = masked[:, part * 128 : (part + 1) * 128]
        for row in range(row_dev // 2):
            start = batch * key_dev + row * half_cols
            for offset in range(4):
                dr, dc = offset // 2, offset % 2
                for part in range(dim // 128):
                    piece = wide[part, pl.ds((2 * row + dr) * cols + dc, half_cols, stride=2), :]
                    lanes = slice(offset * dim + part * 128, offset * dim + (part + 1) * 128)
                    patch_ref[start : start + half_cols, lanes] = piece.astype(bf16)
    is_low = lax.axis_index("sp") % 2 == 0
    for offset in range(4):
        low = patch_ref[:, offset * dim : offset * dim + half]
        high = patch_ref[:, offset * dim + half : (offset + 1) * dim]
        cols_ref[offset] = jnp.where(is_low, low, high)
        send_ref[offset] = jnp.where(is_low, high, low)
    reduced = mm(patch_ref[...], weight_ref[...].reshape(4 * dim, dim)) + vec[REDUCE_B : REDUCE_B + 1]
    reduced_ref[...] = reduced
    normal, _ = normalize(reduced)
    key_ref[...] = (normal * vec[KEYS_G : KEYS_G + 1] + vec[KEYS_B : KEYS_B + 1]).astype(bf16)


def relay_kernel(n, *refs):
    for source, target in zip(refs[:n], refs[n + 1 :]):
        target[...] = source[...]


def head_stack_t(values_t, pair, tok):
    both = jnp.concatenate([values_t, values_t], axis=1)
    head = lax.broadcasted_iota(jnp.int32, both.shape, 0) // HDIM
    want = 2 * pair + jnp.where(lax.broadcasted_iota(jnp.int32, both.shape, 1) >= tok, 1, 0)
    return jnp.where(head == want, both, jnp.zeros_like(both))


def head_stack(values, pair):
    head = lax.broadcasted_iota(jnp.int32, values.shape, 1) // HDIM
    zero = jnp.zeros_like(values)
    return jnp.concatenate(
        [jnp.where(head == 2 * pair, values, zero), jnp.where(head == 2 * pair + 1, values, zero)],
        axis=0,
    )


def split_pair(both, tok):
    return jnp.concatenate([both[:HDIM, :tok], both[HDIM:, tok:]], axis=0)


def key_rows_of(pieces, key_dev, per_block, batch, index):
    here = slice(batch * key_dev, (batch + 1) * key_dev)
    if len(pieces) > 1:
        return jnp.concatenate([part[here] for part in pieces], axis=0)
    dim = pieces[0].shape[2]
    devices = slice(index * per_block, (index + 1) * per_block)
    return pieces[0][devices, here, :].reshape(per_block * key_dev, dim)


def mask_lane(pair, dim):
    return 0 if pair == PAIRS - 1 else dim - 1


def with_bias(key_block, bias, lane_id):
    lane = lax.broadcasted_iota(jnp.int32, key_block.shape, 1)
    return jnp.where(lane == lane_id, bias.astype(f32), key_block.astype(f32)).astype(bf16)


def query_stack(queries_t, pair, lane_id, tok):
    stacked = head_stack_t(queries_t, pair, tok)
    row = lax.broadcasted_iota(jnp.int32, stacked.shape, 0)
    return jnp.where(row == lane_id, jnp.ones_like(stacked), stacked)


def take(refs, *counts):
    refs = list(refs)
    groups = []
    for count in counts:
        groups.append(refs[:count])
        refs = refs[count:]
    return groups + [refs]


def forward_kernel(dims, *refs):
    batch, tok, key_dev, keys, block, n_pieces = dims
    (normed, vec_ref, bias_ref, wq, wkv), pieces, outs = take(refs, 5, n_pieces)
    attended, queries_out, kvs, attf, stats, probs, wide = outs
    dim = wq.shape[0]
    blocks = keys // block
    per_block = block // key_dev
    queries = (mm(normed[batch * tok : (batch + 1) * tok], wq[...]) + vec_ref[QUERY_B : QUERY_B + 1]).astype(bf16)
    queries_out[...] = queries
    queries_t = queries.T
    for index in range(blocks):
        key_rows = key_rows_of(pieces, key_dev, per_block, batch, index)
        here = slice(index * block, (index + 1) * block)
        kvs[here, :dim] = mm(key_rows, wkv[:, :dim]).astype(bf16)
        value_rows = mm(key_rows, wkv[:, dim:]) + vec_ref[VALUE_B : VALUE_B + 1]
        kvs[here, dim:] = value_rows.astype(bf16)
    if blocks == 1:
        key_block = kvs[:, :dim]
        values_t = kvs[:, dim:].T
        masked = {lane_id: with_bias(key_block, bias_ref[batch], lane_id) for lane_id in (0, dim - 1)}

        def score(pair):
            lane_id = mask_lane(pair, dim)
            wide[pair % 2] = mm(masked[lane_id], query_stack(queries_t, pair, lane_id, tok))

        score(0)
        for pair in range(PAIRS):
            if pair + 1 < PAIRS:
                score(pair + 1)
            heads = slice(2 * HDIM * pair, 2 * HDIM * (pair + 1))
            scores = wide[pair % 2]
            top = jnp.max(scores, axis=0, keepdims=True)
            weights = jnp.exp2((scores - top) * EXP_SCALE)
            inverse = 1.0 / jnp.sum(weights, axis=0, keepdims=True)
            low = weights.astype(bf16)
            probs[pair] = low
            stats[pair, 0:1] = inverse
            mixed = mm(values_t[heads], low) * inverse
            attf[heads] = split_pair(mixed, tok)
    else:
        for pair in range(PAIRS):
            lane_id = mask_lane(pair, dim)
            heads = slice(2 * HDIM * pair, 2 * HDIM * (pair + 1))
            stacked = query_stack(queries_t, pair, lane_id, tok)

            def block_scores(index, stacked=stacked, lane_id=lane_id):
                here = pl.ds(pl.multiple_of(index * block, block), block)
                masked = with_bias(kvs[here, :dim], bias_ref[batch, here, :], lane_id)
                return here, mm(masked, stacked)

            def find_top(index, top, block_scores=block_scores):
                _, scores = block_scores(index)
                return jnp.maximum(top, jnp.max(scores, axis=0, keepdims=True))

            top = lax.fori_loop(0, blocks, find_top, jnp.full((1, 2 * tok), 4 * NEG, f32))

            def add_block(index, carry, block_scores=block_scores, top=top, heads=heads):
                total, mixed = carry
                here, scores = block_scores(index)
                weights = jnp.exp2((scores - top) * EXP_SCALE)
                values_t = kvs[here, dim:].T
                mixed = mixed + mm(values_t[heads], weights.astype(bf16))
                return total + jnp.sum(weights, axis=0, keepdims=True), mixed

            start = (jnp.zeros((1, 2 * tok), f32), jnp.zeros((2 * HDIM, 2 * tok), f32))
            total, mixed = lax.fori_loop(0, blocks, add_block, start)
            inverse = 1.0 / total
            stats[pair, 0:1] = inverse
            stats[pair, 1:2] = top
            attf[heads] = split_pair(mixed * inverse, tok)
    attended[...] = attf[...].T.astype(bf16)


def mlp_kernel(dims, *refs):
    n_fs, batches, row_dev, cols, dim, hid = dims
    ins, attended, own, mine, other, _, outs, scratch = take(refs, 4, batches, 3, n_fs - 1, n_fs - 1, 1, 6)
    tokens, cotangent, mask_ref, vec_ref = ins
    acts_ref, middle_ref, gatt, keep_ref, send_ref, gvec_ref = outs
    wh, wr, wo, lows, highs = scratch
    tok = row_dev * cols
    shard = dim // n_fs
    chunks = hid // dim
    fs = lax.axis_index("fs")
    is_low = lax.axis_index("sp") % 2 == 0
    wh[shard_rows(fs, shard), :] = own[0][...]
    wr[shard_rows(fs, dim), :] = own[1][...]
    wo[shard_rows(fs, shard), :] = own[2][...]
    for step in range(1, n_fs):
        low, high = both_halves(mine[step - 1], other[step - 1])
        place = fs ^ step
        here = shard_rows(place, shard)
        for chunk in range(chunks):
            wh[here, chunk * dim : (chunk + 1) * dim] = low[chunk * shard : (chunk + 1) * shard]
        wr[shard_rows(place, dim), :] = high[:dim]
        wo[here, :] = jnp.concatenate([low[dim:], high[dim:]], axis=0)

    def vec(index):
        return vec_ref[index : index + 1, :]

    x = jnp.concatenate([tokens[b, 0].reshape(tok, dim).astype(f32) for b in range(batches)], axis=0)
    mask = mask_ref[...]
    attended = jnp.concatenate([part[...] for part in attended], axis=0)
    middle = x + mm(attended, wo[...]) + vec(OUTPUT_B)
    normal, rstd = normalize(middle)
    second = (normal * vec(SECOND_G) + vec(SECOND_B)).astype(bf16)
    grad_out = jnp.concatenate([cotangent[b, 0].reshape(tok, dim) for b in range(batches)], axis=0) * mask
    grad_mlp = grad_out.astype(bf16)
    second_t, grad_mlp_t = second.T, grad_mlp.T
    total = middle + vec(RETURN_B)
    grad_second = jnp.zeros((batches * tok, dim), f32)
    gvec_ref[...] = jnp.zeros_like(gvec_ref)
    for chunk in range(chunks):
        lanes = slice(chunk * dim, (chunk + 1) * dim)
        hidden = mm(second, wh[:, lanes]) + vec(HIDDEN_B + chunk)
        phi = 0.5 + 0.5 * lax.erf(hidden * 0.7071067811865476)
        density = 0.3989422804014327 * jnp.exp2(hidden * hidden * (-0.5 * 1.4426950408889634))
        activated = (hidden * phi).astype(bf16)
        total = total + mm(activated, wr[lanes, :])
        grad_activated = mm_nt(grad_mlp, wr[lanes, :])
        grad_hidden = ((phi + hidden * density) * grad_activated).astype(bf16)
        gvec_ref[HIDDEN_B + chunk : HIDDEN_B + chunk + 1] = jnp.sum(
            grad_hidden.astype(f32), axis=0, keepdims=True
        )
        grad_second = grad_second + mm_nt(grad_hidden, wh[:, lanes])
        highs[chunk] = mm(grad_mlp_t, activated).T.astype(bf16)
        grad_wh = mm(second_t, grad_hidden).astype(bf16)
        for owner in range(n_fs):
            lows[owner, chunk * shard : (chunk + 1) * shard] = grad_wh[owner * shard : (owner + 1) * shard]
    low, high = lows[...], highs[...]
    keep_ref[...] = jnp.where(is_low, low, high)
    send_ref[...] = jnp.where(is_low, high, low)
    total = total * mask
    for batch in range(batches):
        acts_ref[batch, 0] = total[batch * tok : (batch + 1) * tok].reshape(row_dev, cols, dim)
    grad_middle = grad_out + normalize_back(grad_second, normal, rstd, vec(SECOND_G))
    middle_ref[...] = grad_middle
    grad_branch = grad_middle.astype(bf16)
    gatt[...] = mm_nt(grad_branch, wo[...]).astype(bf16)
    for index, value in (
        (OUTPUT_B, grad_branch.astype(f32)),
        (SECOND_G, grad_second * normal),
        (SECOND_B, grad_second),
        (RETURN_B, grad_mlp.astype(f32)),
    ):
        gvec_ref[index : index + 1] = jnp.sum(value, axis=0, keepdims=True)


def backward_kernel(dims, *refs):
    n_sp, batch, tok, key_dev, keys, block, n_pieces = dims
    gatt, queries_ref, kvs, attf, stats, probs, bias_ref, wkv, _ = refs[:9]
    near_ref, far_ref, scores_ref, gks, gvs, gvec_ref = refs[9:15]
    dim = wkv.shape[0]
    blocks = keys // block
    per_block = block // key_dev
    rows = slice(batch * tok, (batch + 1) * tok)
    queries = queries_ref[...]
    grad_att_t = gatt[rows].astype(f32).T
    product = grad_att_t * attf[...]

    def pair_terms(pair):
        inverse = stats[pair, 0:1]
        piece = product[2 * HDIM * pair : 2 * HDIM * (pair + 1)]
        delta = jnp.concatenate(
            [jnp.sum(piece[:HDIM], axis=0, keepdims=True), jnp.sum(piece[HDIM:], axis=0, keepdims=True)],
            axis=1,
        )
        stacked = head_stack_t(grad_att_t, pair, tok) * inverse
        return delta * inverse, stacked.astype(bf16)

    if blocks == 1:
        (wide,) = refs[15:]
        values = kvs[:, dim:]
        grad_k = jnp.zeros((keys, dim), f32)
        grad_v = jnp.zeros((keys, dim), f32)
        terms = []

        def grad_prob(pair):
            delta, stacked = pair_terms(pair)
            wide[pair % 2] = mm(values, stacked)
            terms.append((delta, stacked))

        grad_prob(0)
        for pair in range(PAIRS):
            if pair + 1 < PAIRS:
                grad_prob(pair + 1)
            delta, stacked = terms[pair]
            low = probs[pair]
            grad_scores = (low.astype(f32) * (wide[pair % 2] - delta)).astype(bf16)
            scores_ref[pair] = grad_scores
            grad_k = grad_k + mm(grad_scores, head_stack(queries, pair))
            grad_v = grad_v + mm(low, stacked.T)
    else:
        wide_k, wide_v = refs[15:]
        wide_k[...] = jnp.zeros_like(wide_k)
        wide_v[...] = jnp.zeros_like(wide_v)
        queries_t = queries.T
        for pair in range(PAIRS):
            heads = slice(2 * HDIM * pair, 2 * HDIM * (pair + 1))
            lane_id = mask_lane(pair, dim)
            delta, stacked = pair_terms(pair)
            stacked_n = stacked.T
            query_t = query_stack(queries_t, pair, lane_id, tok)
            query_n = head_stack(queries, pair)
            top = stats[pair, 1:2]

            def back_block(index, gq, heads=heads, lane_id=lane_id, delta=delta, stacked=stacked, stacked_n=stacked_n, query_t=query_t, query_n=query_n, top=top):
                here = pl.ds(pl.multiple_of(index * block, block), block)
                key_block = kvs[here, :dim]
                masked = with_bias(key_block, bias_ref[batch, here, :], lane_id)
                weights = jnp.exp2((mm(masked, query_t) - top) * EXP_SCALE)
                grad_probs = mm(kvs[here, dim:], stacked)
                grad_scores = (weights * (grad_probs - delta)).astype(bf16)
                wide_k[here, :] += mm(grad_scores, query_n)
                wide_v[here, :] += mm(weights.astype(bf16), stacked_n)
                return gq + mm(key_block.T[heads], grad_scores)

            gq = lax.fori_loop(0, blocks, back_block, jnp.zeros((2 * HDIM, 2 * tok), f32))
            scores_ref[heads] = split_pair(gq, tok)
    bias_value = jnp.zeros((1, dim), f32)
    for index in range(blocks):
        here = slice(index * block, (index + 1) * block)
        if blocks > 1:
            grad_k, grad_v = wide_k[here], wide_v[here]
        grad_k = (grad_k * SCALE).astype(bf16)
        bias_value = bias_value + jnp.sum(grad_v, axis=0, keepdims=True)
        grad_v = grad_v.astype(bf16)
        gks[here] = grad_k
        gvs[here] = grad_v
        grad_key = (mm_nt(grad_k, wkv[:, :dim]) + mm_nt(grad_v, wkv[:, dim:])).astype(bf16)
        if n_pieces > 1:
            pairs = grad_key.reshape(n_sp // 2, 2, key_dev, dim)
            near_ref[...] = pairs[:, 0]
            far_ref[...] = pairs[:, 1]
        else:
            near_ref[index * per_block : (index + 1) * per_block] = grad_key.reshape(per_block, key_dev, dim)
    gvec_ref[...] = jnp.broadcast_to(bias_value, gvec_ref.shape)


def query_kernel(dims, *refs):
    n_fs, batches, tok, key_dev, keys, block, n_pieces = dims
    ins, attended, kvs, scores, gks, gvs, gvecs, pieces, outs = take(refs, 3, *([batches] * 6), n_pieces)
    normed, wq, middle = ins
    keep_ref, send_ref, gnormed_ref, gvec_ref, wide = outs
    dim = wq.shape[0]
    shard = dim // n_fs
    blocks = keys // block
    per_block = block // key_dev
    grad_queries = []
    grad_wk = jnp.zeros((dim, dim), f32)
    grad_wv = jnp.zeros((dim, dim), f32)
    for batch in range(batches):
        if blocks == 1:
            keys_t = kvs[batch][:, :dim].T
            for pair in range(PAIRS):
                heads = slice(2 * HDIM * pair, 2 * HDIM * (pair + 1))
                wide[heads] = split_pair(mm(keys_t[heads], scores[batch][pair]), tok)
            grad_t = wide[...]
        else:
            grad_t = scores[batch][...]
        grad_queries.append((grad_t.T * SCALE).astype(bf16))
        for index in range(blocks):
            here = slice(index * block, (index + 1) * block)
            key_rows = key_rows_of(pieces, key_dev, per_block, batch, index)
            grad_wk = grad_wk + mm_tn(key_rows, gks[batch][here])
            grad_wv = grad_wv + mm_tn(key_rows, gvs[batch][here])
    grad_queries = jnp.concatenate(grad_queries, axis=0)
    grad_wq = mm_tn(normed[...], grad_queries)
    attended = jnp.concatenate([part[...] for part in attended], axis=0)
    grad_wo = mm_tn(attended, middle[...].astype(bf16))
    is_low = lax.axis_index("sp") % 2 == 0
    for owner in range(n_fs):
        part = slice(owner * shard, (owner + 1) * shard)
        low = jnp.concatenate([grad_wq[part], grad_wk[part]], axis=0).astype(bf16)
        high = jnp.concatenate([grad_wv[part], grad_wo[part]], axis=0).astype(bf16)
        keep_ref[owner] = jnp.where(is_low, low, high)
        send_ref[owner] = jnp.where(is_low, high, low)
    gnormed_ref[...] = mm_nt(grad_queries, wq[...])
    gvec_ref[...] = jnp.zeros_like(gvec_ref)
    gvec_ref[QUERY_B : QUERY_B + 1] = jnp.sum(grad_queries.astype(f32), axis=0, keepdims=True)
    bias_value = gvecs[0][0:1]
    for gvec in gvecs[1:]:
        bias_value = bias_value + gvec[0:1]
    gvec_ref[VALUE_B : VALUE_B + 1] = bias_value


def sum_parts(parts):
    if len(parts) == 1:
        total = parts[0][0].astype(f32)
        for index in range(1, parts[0].shape[0]):
            total = total + parts[0][index].astype(f32)
        return total
    total = parts[0][...].astype(f32)
    for part in parts[1:]:
        total = total + part[...].astype(f32)
    return total


def reduction_kernel(n_parts, batches, reduced, vec_ref, *refs):
    parts, gvec_ref, outs = refs[:n_parts], refs[-1], refs[-1 - batches : -1]
    grad_key = sum_parts(parts)
    normal, rstd = normalize(reduced[...])
    grad_low = normalize_back(grad_key, normal, rstd, vec_ref[KEYS_G : KEYS_G + 1]).astype(bf16)
    rows = outs[0].shape[0]
    for batch, out in enumerate(outs):
        out[...] = grad_low[batch * rows : (batch + 1) * rows]
    gvec_ref[...] = jnp.zeros_like(gvec_ref)
    for index, value in (
        (REDUCE_B, grad_low.astype(f32)),
        (KEYS_G, grad_key * normal),
        (KEYS_B, grad_key),
    ):
        gvec_ref[index : index + 1] = jnp.sum(value, axis=0, keepdims=True)


def weight_kernel(batches, *refs):
    (own_cols, other_cols), own, other, (vectors, *outs) = take(refs, 2, batches, batches)
    fs = lax.axis_index("fs")
    own = jnp.concatenate([part[...] for part in own], axis=0)
    other = jnp.concatenate([part[...] for part in other], axis=0)
    rows = own_cols.shape[2]
    for step, out in enumerate(outs):
        place = lax.rem(fs + step, len(outs))
        out[:rows] = (mm_tn(own_cols[place], own) + mm_tn(other_cols[place], other)).astype(out.dtype)
        out[rows:] = vectors[...]


def normed_kernel(dims, gnormed, mask_ref, weight, normal_ref, vec_a, vec_b, vec_c, *refs):
    batches, row_dev, cols, dim = dims
    grads, (grad_ref, gvec_ref, wide) = take(refs, batches)
    tok = row_dev * cols
    half_cols = cols // 2
    gain_first = jnp.zeros((1, dim), f32)
    bias_first = jnp.zeros((1, dim), f32)
    for batch in range(batches):
        for offset in range(4):
            dr, dc = offset // 2, offset % 2
            back = mm_nt(grads[batch][...], weight[offset])
            for row in range(row_dev // 2):
                for part in range(dim // 128):
                    wide[part, pl.ds((2 * row + dr) * cols + dc, half_cols, stride=2), :] = back[
                        row * half_cols : (row + 1) * half_cols, part * 128 : (part + 1) * 128
                    ]
        rows = slice(batch * tok, (batch + 1) * tok)
        spread = jnp.concatenate([wide[part] for part in range(dim // 128)], axis=1)
        grad_normed = gnormed[rows] + spread * mask_ref[rows]
        grad_ref[rows] = grad_normed
        gain_first = gain_first + jnp.sum(grad_normed * normal_ref[rows], axis=0, keepdims=True)
        bias_first = bias_first + jnp.sum(grad_normed, axis=0, keepdims=True)
    index = lax.broadcasted_iota(jnp.int32, (VECS, dim), 0)
    vectors = vec_a[...] + vec_b[...] + vec_c[...]
    vectors = jnp.where(index == FIRST_G, gain_first, vectors)
    vectors = jnp.where(index == FIRST_B, bias_first, vectors)
    gvec_ref[...] = vectors.astype(bf16)


def input_kernel(dims, middle, grad_normed, normal_ref, rstd_ref, vec_ref, _, grad_ref, done_ref):
    batches, row_dev, cols, dim = dims
    tok = row_dev * cols
    rstd = jnp.concatenate([rstd_ref[...]] * (dim // rstd_ref.shape[1]), axis=1)
    back = normalize_back(grad_normed[...], normal_ref[...], rstd, vec_ref[FIRST_G : FIRST_G + 1])
    grad_x = middle[...] + back
    for batch in range(batches):
        grad_ref[batch, 0] = grad_x[batch * tok : (batch + 1) * tok].reshape(row_dev, cols, dim)
    done_ref[...] = jnp.zeros_like(done_ref)


def key_sum_kernel(batches, *refs):
    near, far, _, outs = take(refs, batches, batches, 2)
    for step, out in enumerate(outs):
        rows = near[0].shape[1]
        for batch in range(batches):
            total = near[batch][step].astype(f32) + far[batch][step].astype(f32)
            out[batch * rows : (batch + 1) * rows] = total.astype(out.dtype)


def owner_kernel(keep, arrived, *outs):
    fs = lax.axis_index("fs")
    for step, out in enumerate(outs):
        place = lax.rem(fs + step, len(outs))
        out[...] = (keep[place].astype(f32) + arrived[place].astype(f32)).astype(out.dtype)


def chip_kernel(keep, arrived, _, *outs):
    chip = lax.axis_index("sp") // 2
    rows = outs[0].shape[1]
    for step, out in enumerate(outs):
        here = shard_rows(chip ^ step, rows)
        out[...] = (keep[:, here, :].astype(f32) + arrived[:, here, :].astype(f32)).astype(out.dtype)


def chip_sum_kernel(*refs):
    refs[-1][...] = sum_parts(refs[:-1]).astype(refs[-1].dtype)


def owners_kernel(total, keep, arrived, *outs):
    fs = lax.axis_index("fs")
    rows = total.shape[1]
    for step, out in enumerate(outs):
        place = lax.rem(fs + step, len(outs))
        out[:rows] = total[place]
        out[rows:] = (keep[place].astype(f32) + arrived[place].astype(f32)).astype(out.dtype)


def join_kernel(n, *refs):
    refs[-1][...] = sum_parts(refs[:n]).astype(refs[-1].dtype)


def merge_kernel(rows, *refs):
    parts, out = refs[:4], refs[5]
    chip = lax.axis_index("sp") // 2
    if rows:
        for step, part in enumerate(parts):
            out[shard_rows(chip ^ step, rows), :] = part[:rows]
    rest = [part[rows:].astype(f32) for part in parts]
    out[4 * rows :] = ((rest[0] + rest[1]) + (rest[2] + rest[3])).astype(out.dtype)


def final_kernel(mine, other, query_w, keyval_w, output_w, hidden_w, return_w):
    shard, dim = query_w.shape
    low, high = both_halves(mine, other)
    low, high = low.astype(f32), high.astype(f32)
    for chunk in range(hidden_w.shape[1] // dim):
        hidden_w[:, chunk * dim : (chunk + 1) * dim] = low[chunk * shard : (chunk + 1) * shard]
    return_w[...] = high[:dim]
    low, high = low[dim:], high[dim:]
    query_w[...] = low[:shard]
    keyval_w[:, :dim] = low[shard : 2 * shard]
    keyval_w[:, dim:] = high[:shard]
    output_w[...] = high[shard : 2 * shard]


def final_small_kernel(n_fs, mine, other, reduce_w, *outs):
    smalls, hidden_b = outs[:-1], outs[-1]
    dim = reduce_w.shape[0]
    shard = dim // n_fs
    half = dim // 2
    fs = lax.axis_index("fs")
    low, high = both_halves(mine, other)
    low, high = low.astype(f32), high.astype(f32)
    reduce_w[:half] = low[:half]
    reduce_w[half:] = high[:half]
    vecs = low[half:] + high[half:]
    lane = lax.broadcasted_iota(jnp.int32, vecs.shape, 1)
    chosen = jnp.where(lane // shard == fs, vecs, 0.0)
    folded = chosen[:, :shard]
    for index in range(1, n_fs):
        folded = folded + chosen[:, index * shard : (index + 1) * shard]
    for index, small in enumerate(smalls):
        small[...] = folded[index : index + 1].reshape(shard)
    row = lax.broadcasted_iota(jnp.int32, vecs.shape, 0)
    hidden_b[...] = jnp.sum(jnp.where(row == HIDDEN_B + fs, vecs, 0.0), axis=0)


def rotate(value, n, step):
    return lax.ppermute(value, "fs", [(i, (i + step) % n) for i in range(n)])


def swap(value, n, bits):
    return lax.ppermute(value, "fs", [(i, i ^ bits) for i in range(n)])


def flip(value, n, bits):
    return lax.ppermute(value, "sp", [(i, i ^ bits) for i in range(n)])


def sum_over_rows(value, n_sp):
    bit = 2
    while bit < n_sp:
        if 2 * bit < n_sp:
            a, b, c = flip(value, n_sp, bit), flip(value, n_sp, 2 * bit), flip(value, n_sp, 3 * bit)
            value = (
                (value.astype(f32) + a.astype(f32)) + (b.astype(f32) + c.astype(f32))
            ).astype(value.dtype)
            bit = 4 * bit
        else:
            a = flip(value, n_sp, bit)
            value = (value.astype(f32) + a.astype(f32)).astype(value.dtype)
            bit = 2 * bit
    return value


def exchange(pieces, n_sp):
    return [pieces[0]] + [flip(pieces[step], n_sp, 2 * step) for step in range(1, n_sp // 2)]


def to_owners(pieces, n_fs):
    return [pieces[0]] + [rotate(pieces[step], n_fs, step) for step in range(1, n_fs)]


def call(kernel, out_shape, in_specs=None, scratch=(), limit=SMALL_VMEM, micros=0):
    specs = {} if in_specs is None else {"in_specs": in_specs}
    return pl.pallas_call(
        kernel,
        out_shape=out_shape,
        **specs,
        scratch_shapes=scratch,
        compiler_params=pltpu.CompilerParams(vmem_limit_bytes=limit),
        cost_estimate=pl.CostEstimate(flops=int(micros * 1e9), bytes_accessed=0, transcendentals=0),
    )


def on_device(
    n_fs,
    n_sp,
    tokens,
    cotangent,
    image_sizes,
    first_gain,
    first_bias,
    query_weight,
    query_bias,
    reduce_weight,
    reduce_bias,
    keys_gain,
    keys_bias,
    keyval_weight,
    value_bias,
    output_weight,
    output_bias,
    second_gain,
    second_bias,
    hidden_weight,
    hidden_bias,
    return_weight,
    return_bias,
):
    batches, _, row_dev, cols, dim = tokens.shape
    hid = hidden_weight.shape[1]
    tok = row_dev * cols
    key_dev = tok // 4
    keys = n_sp * key_dev
    shard = dim // n_fs
    half = dim // 2
    vmem = pl.BlockSpec(memory_space=pltpu.VMEM)
    smem = pl.BlockSpec(memory_space=pltpu.SMEM)
    single = keys <= KEY_BLOCK
    split = n_sp == 8
    block = keys if single else KEY_BLOCK
    limit = MAIN_VMEM if single else WHOLE_VMEM

    def shape(*dims, dtype=bf16):
        return jax.ShapeDtypeStruct(dims, dtype)

    smalls = (
        first_gain,
        first_bias,
        query_bias,
        reduce_bias,
        keys_gain,
        keys_bias,
        value_bias,
        output_bias,
        second_gain,
        second_bias,
        return_bias,
    )
    first_half = call(
        functools.partial(pack_first_kernel, n_fs),
        shape(half + VECS + 3 * shard // 2, dim),
        scratch=[pltpu.VMEM((VECS, dim), f32)],
        limit=WHOLE_VMEM,
    )(*smalls, hidden_bias, reduce_weight, query_weight, keyval_weight)
    mine_first = to_owners([first_half] * n_fs, n_fs)[1:]

    begun = call(
        functools.partial(begin_kernel, (n_sp, batches, row_dev, cols, dim)),
        [
            shape(batches * tok, dim, dtype=f32),
            shape(batches * tok, 128, dtype=f32),
            shape(batches * tok, dim, dtype=f32),
            shape(batches, keys, dim),
            shape(dim, dim),
            shape(shard, dim),
            shape(shard, 2 * dim),
            shape(VECS, dim, dtype=f32),
            shape(dim + shard // 2, dim),
        ],
        in_specs=[smem] + [vmem] * 8,
        limit=SMALL_VMEM if single else WHOLE_VMEM,
    )(
        image_sizes,
        tokens,
        reduce_weight,
        query_weight,
        keyval_weight,
        hidden_weight,
        return_weight,
        output_weight,
        first_half,
    )
    normal_first, rstd_first, mask, bias, own_r, own_q, own_kv, own_vec, second_half = begun
    mine_first = call(functools.partial(relay_kernel, n_fs - 1), [shape(*first_half.shape)] * (n_fs - 1))(
        *mine_first, own_vec
    )
    other_first = [flip(piece, n_sp, 1) for piece in mine_first]
    normed, patch_cols, patch_send, reduced, key_low, whole_reduce, wq, wkv, vec = call(
        functools.partial(reduce_kernel, (n_fs, batches, row_dev, cols, dim)),
        [
            shape(batches * tok, dim),
            shape(4, batches * key_dev, half),
            shape(4, batches * key_dev, half),
            shape(batches * key_dev, dim, dtype=f32),
            shape(batches * key_dev, dim),
            shape(n_fs, dim, dim),
            shape(dim, dim),
            shape(dim, 2 * dim),
            shape(VECS, dim, dtype=f32),
        ],
        scratch=[pltpu.VMEM((batches * key_dev, 4 * dim), bf16), pltpu.VMEM((dim // 128, tok, 128), f32)],
    )(normal_first, mask, own_r, own_q, own_kv, own_vec, *mine_first, *other_first)
    across = swap(second_half, n_fs, 2)
    passed = call(functools.partial(relay_kernel, 1), [shape(dim + shard // 2, dim)], micros=15)(across, own_vec)
    mine_second = [swap(second_half, n_fs, 1), across, swap(passed[0], n_fs, 1)]

    if split:
        same = exchange([key_low] * (n_sp // 2), n_sp)
        key_pieces = [piece for part in same for piece in (part, flip(part, n_sp, 1))]
    else:
        key_pieces = [lax.all_gather(key_low, "sp")]
    n_pieces = len(key_pieces)

    kept = [
        call(
            functools.partial(forward_kernel, (batch, tok, key_dev, keys, block, n_pieces)),
            [
                shape(tok, dim),
                shape(tok, dim),
                shape(keys, 2 * dim),
                shape(dim, tok, dtype=f32),
                shape(PAIRS, 8, 2 * tok, dtype=f32),
                shape(PAIRS, keys, 2 * tok) if single else shape(16, 128),
            ],
            scratch=[pltpu.VMEM((2, block, 2 * tok) if single else (8, 128), f32)],
            limit=limit,
        )(normed, vec, bias, wq, wkv, *key_pieces)
        for batch in range(batches)
    ]
    attended = [results[0] for results in kept]
    kept = [results[1:] for results in kept]
    mine_second = call(functools.partial(relay_kernel, n_fs - 1), [shape(dim + shard // 2, dim)] * (n_fs - 1))(
        *mine_second, kept[0][3]
    )
    patch_other = flip(patch_send, n_sp, 1)
    other_second = [flip(piece, n_sp, 1) for piece in mine_second]

    acts, middle, gatt, keep_a, send_a, gvec_a = call(
        functools.partial(mlp_kernel, (n_fs, batches, row_dev, cols, dim, hid)),
        [
            shape(batches, 1, row_dev, cols, dim, dtype=f32),
            shape(batches * tok, dim, dtype=f32),
            shape(batches * tok, dim),
            shape(n_fs, dim, dim),
            shape(n_fs, dim, dim),
            shape(VECS, dim, dtype=f32),
        ],
        scratch=[
            pltpu.VMEM((dim, hid), bf16),
            pltpu.VMEM((hid, dim), bf16),
            pltpu.VMEM((dim, dim), bf16),
            pltpu.VMEM((n_fs, dim, dim), bf16),
            pltpu.VMEM((n_fs, dim, dim), bf16),
        ],
        limit=limit,
    )(
        tokens,
        cotangent,
        mask,
        vec,
        *attended,
        hidden_weight,
        return_weight,
        output_weight,
        *mine_second,
        *other_second,
        patch_other,
    )
    arrived_a = flip(send_a, n_sp, 1)
    gkey_dims = (n_sp // 2, key_dev, dim) if split else (n_sp, key_dev, dim)
    back = []
    for batch in range(batches):
        queries, kvs, attf, stats, probs = kept[batch]
        order = vec
        if split and batch == batches - 1:
            pieces_a = call(chip_kernel, [shape(n_fs, dim // 4, dim)] * 4)(keep_a, arrived_a, back[0][5])
            total_a = call(chip_sum_kernel, shape(n_fs, dim // 4, dim), micros=5)(*exchange(pieces_a, n_sp))
            order = pieces_a[0]
        back.append(
            call(
                functools.partial(backward_kernel, (n_sp, batch, tok, key_dev, keys, block, n_pieces)),
                [
                    shape(*gkey_dims),
                    shape(*(gkey_dims if split else (16, 128))),
                    shape(PAIRS, keys, 2 * tok) if single else shape(dim, tok, dtype=f32),
                    shape(keys, dim),
                    shape(keys, dim),
                    shape(8, dim, dtype=f32),
                ],
                scratch=[pltpu.VMEM((2, keys, 2 * tok), f32)] if single else [pltpu.VMEM((keys, dim), f32)] * 2,
                limit=limit,
            )(gatt, queries, kvs, attf, stats, probs, bias, wkv, order)
        )
    near = [results[0] for results in back]
    keep_c, send_c, gnormed, gvec_c = call(
        functools.partial(query_kernel, (n_fs, batches, tok, key_dev, keys, block, n_pieces)),
        [
            shape(n_fs, half, dim),
            shape(n_fs, half, dim),
            shape(batches * tok, dim, dtype=f32),
            shape(VECS, dim, dtype=f32),
        ],
        scratch=[pltpu.VMEM((dim, tok), f32)],
        limit=limit,
    )(
        normed,
        wq,
        middle,
        *attended,
        *[kept[batch][1] for batch in range(batches)],
        *[results[2] for results in back],
        *[results[3] for results in back],
        *[results[4] for results in back],
        *[results[5] for results in back],
        *key_pieces,
    )
    arrived_c = flip(send_c, n_sp, 1)
    if split:
        far = [flip(results[1], n_sp, 1) for results in back]
        sums = call(functools.partial(key_sum_kernel, batches), [shape(batches * key_dev, dim)] * 4)(
            *near, *far, total_a, gvec_c
        )
        parts = exchange(sums, n_sp)
    else:
        parts = [lax.all_to_all(jnp.concatenate(near, axis=1), "sp", 0, 0)]
    *grad_reduced, gvec_b = call(
        functools.partial(reduction_kernel, len(parts), batches),
        [shape(key_dev, dim)] * batches + [shape(VECS, dim, dtype=f32)],
    )(reduced, vec, *parts)
    grad_other = [flip(part, n_sp, 1) for part in grad_reduced]
    grad_normed, vectors = call(
        functools.partial(normed_kernel, (batches, row_dev, cols, dim)),
        [shape(batches * tok, dim, dtype=f32), shape(VECS, dim)],
        scratch=[pltpu.VMEM((dim // 128, tok, 128), f32)],
    )(gnormed, mask, whole_reduce, normal_first, gvec_a, gvec_b, gvec_c, *grad_reduced)
    chunks_b = call(functools.partial(weight_kernel, batches), [shape(half + VECS, dim)] * n_fs)(
        patch_cols, patch_other, *grad_reduced, *grad_other, vectors
    )
    if split:
        rows = dim // 4
        chunks = call(owners_kernel, [shape(rows + half, dim)] * n_fs)(total_a, keep_c, arrived_c)
        join = functools.partial(join_kernel, n_fs)
        *first_a, last_a = to_owners(chunks, n_fs)
        joined_a = call(functools.partial(join_kernel, n_fs - 1), shape(rows + half, dim), micros=5)(*first_a, vec)
        joined_a = call(functools.partial(join_kernel, 2), shape(rows + half, dim))(joined_a, last_a, vec)
        order = joined_a
    else:
        order = vec
    grads, done = call(
        functools.partial(input_kernel, (batches, row_dev, cols, dim)),
        [shape(batches, 1, row_dev, cols, dim, dtype=f32), shape(8, 128, dtype=f32)],
    )(middle, grad_normed, normal_first, rstd_first, vec, order)

    if split:
        joined_b = call(join, shape(half + VECS, dim), micros=1)(*to_owners(chunks_b, n_fs), done)
        mine = call(functools.partial(merge_kernel, rows), shape(4 * rows + half, dim))(
            *exchange([joined_a] * 4, n_sp), joined_b
        )
        mine_b = call(functools.partial(merge_kernel, 0), shape(half + VECS, dim))(
            *exchange([joined_b] * 4, n_sp), mine
        )
    else:
        groups = [to_owners(chunks_b, n_fs)]
        for keep, arrived in ((keep_c, arrived_c), (keep_a, arrived_a)):
            pieces = call(owner_kernel, [shape(*keep.shape[1:])] * n_fs)(keep, arrived)
            groups.insert(0, to_owners(pieces, n_fs))
        mine_a, mine_c, mine_b = (
            sum_over_rows(sum(piece.astype(f32) for piece in group).astype(bf16), n_sp) for group in groups
        )
        mine = jnp.concatenate([mine_a, mine_c], axis=0)

    gquery, gkeyval, goutput, ghidden, greturn = call(
        final_kernel,
        [
            shape(shard, dim, dtype=f32),
            shape(shard, 2 * dim, dtype=f32),
            shape(shard, dim, dtype=f32),
            shape(shard, hid, dtype=f32),
            shape(dim, dim, dtype=f32),
        ],
    )(mine, flip(mine, n_sp, 1))
    greduce, *vectors = call(
        functools.partial(final_small_kernel, n_fs),
        [shape(dim, dim, dtype=f32)] + [shape(shard, dtype=f32)] * HIDDEN_B + [shape(dim, dtype=f32)],
        micros=1,
    )(mine_b, flip(mine_b, n_sp, 1))
    return (
        acts,
        grads,
        vectors[FIRST_G],
        vectors[FIRST_B],
        gquery,
        vectors[QUERY_B],
        greduce,
        vectors[REDUCE_B],
        vectors[KEYS_G],
        vectors[KEYS_B],
        gkeyval,
        vectors[VALUE_B],
        goutput,
        vectors[OUTPUT_B],
        vectors[SECOND_G],
        vectors[SECOND_B],
        ghidden,
        vectors[HIDDEN_B],
        greturn,
        vectors[RETURN_B],
    )


def solution(mesh):
    vec, mat = P("fs"), P("fs", None)
    image = P(None, "fs", "sp", None, None)
    weights = (vec, vec, mat, vec, mat, vec, vec, vec, mat, vec, mat, vec, vec, vec, mat, vec, mat, vec)
    return jax.shard_map(
        functools.partial(on_device, mesh.shape["fs"], mesh.shape["sp"]),
        mesh=mesh,
        in_specs=(image, image, P(None, "fs", None)) + weights,
        out_specs=(image, image) + weights,
        check_vma=False,
    )
```

```python
import functools

import jax
import jax.numpy as jnp
from jax import lax
from jax.experimental import pallas as pl
from jax.experimental.pallas import tpu as pltpu
from jax.sharding import PartitionSpec as P

HEADS = 8
HDIM = 32
PAIRS = HEADS // 2
SCALE = HDIM ** (-0.5)
EXP_SCALE = SCALE * 1.4426950408889634
EPS = 1e-06
NEG = -1e30
KEY_BLOCK = 768
SMALL_VMEM = 12 * 2**20
MAIN_VMEM = 16 * 2**20
WHOLE_VMEM = 58 * 2**20

bf16 = jnp.bfloat16
f32 = jnp.float32

(
    FIRST_G,
    FIRST_B,
    QUERY_B,
    REDUCE_B,
    KEYS_G,
    KEYS_B,
    VALUE_B,
    OUTPUT_B,
    SECOND_G,
    SECOND_B,
    RETURN_B,
    HIDDEN_B,
) = range(12)
VECS = 16


def mm(left, right):
    return jnp.dot(left, right, preferred_element_type=f32)


def mm_tn(left, right):
    return lax.dot_general(left, right, (((0,), (0,)), ((), ())), preferred_element_type=f32)


def mm_nt(left, right):
    return lax.dot_general(left, right, (((1,), (1,)), ((), ())), preferred_element_type=f32)


def normalize(rows):
    mean = jnp.mean(rows, axis=-1, keepdims=True)
    centered = rows - mean
    var = jnp.mean(centered * centered, axis=-1, keepdims=True)
    rstd = lax.rsqrt(var + EPS)
    return centered * rstd, rstd


def normalize_back(grad, normal, rstd, gain):
    scaled = grad * gain
    mean_a = jnp.mean(scaled, axis=-1, keepdims=True)
    mean_b = jnp.mean(scaled * normal, axis=-1, keepdims=True)
    return (scaled - mean_a - normal * mean_b) * rstd


def token_mask(first_row, rows, cols, width, height, image_width):
    row_ids = lax.broadcasted_iota(jnp.int32, (rows, cols, width), 0) + first_row
    col_ids = lax.broadcasted_iota(jnp.int32, (rows, cols, width), 1)
    valid = (row_ids < height) & (col_ids < image_width)
    return jnp.where(valid, 1.0, 0.0).astype(f32).reshape(rows * cols, width)


def pack_first_kernel(n_fs, *refs):
    smalls, (hidden_b, reduce_w, query_w, keyval_w, first, wide) = take(refs, HIDDEN_B)
    dim = reduce_w.shape[1]
    shard = dim // n_fs
    half = dim // 2
    rest = half + VECS
    fs = lax.axis_index("fs")
    is_low = lax.axis_index("sp") % 2 == 0

    @pl.when(is_low)
    def _():
        first[:half] = reduce_w[:half]
        first[rest : rest + shard] = query_w[...]
        first[rest + shard :] = keyval_w[: shard // 2, :dim]

    @pl.when(jnp.logical_not(is_low))
    def _():
        first[:half] = reduce_w[half:]
        first[rest : rest + shard // 2] = keyval_w[shard // 2 :, :dim]
        first[rest + shard // 2 :] = keyval_w[:, dim:]

    wide[...] = jnp.zeros_like(wide)
    for index, small in enumerate(smalls):
        row = small[...].astype(f32).reshape(1, shard)
        wide[index : index + 1, :] = jnp.concatenate([row] * n_fs, axis=1)
    lane = lax.broadcasted_iota(jnp.int32, wide.shape, 1)
    row = lax.broadcasted_iota(jnp.int32, wide.shape, 0)
    vectors = jnp.where(lane // shard == fs, wide[...], 0.0)
    hidden_row = hidden_b[...].astype(f32).reshape(1, dim)
    first[half:rest] = jnp.where(row == HIDDEN_B + fs, hidden_row, vectors).astype(bf16)


def both_halves(mine, other):
    is_low = lax.axis_index("sp") % 2 == 0
    a, b = mine[...], other[...]
    return jnp.where(is_low, a, b), jnp.where(is_low, b, a)


def shard_rows(place, rows):
    return pl.ds(pl.multiple_of(place * rows, rows), rows)


def begin_kernel(dims, sizes, tokens, reduce_w, query_w, keyval_w, hidden_w, return_w, output_w, packed, *outs):
    n_sp, batches, row_dev, cols, dim = dims
    normal_ref, rstd_ref, mask_ref, bias_ref, own_r, own_q, own_kv, own_vec, second = outs
    tok = row_dev * cols
    half_cols = cols // 2
    rows_dev = row_dev // 2
    half = dim // 2
    shard = hidden_w.shape[0]
    sp = lax.axis_index("sp")
    own_r[...] = reduce_w[...]
    own_q[...] = query_w[...]
    own_kv[...] = keyval_w[...]
    own_vec[...] = packed[half : half + VECS].astype(f32)

    @pl.when(sp % 2 == 0)
    def _():
        for chunk in range(hidden_w.shape[1] // dim):
            second[chunk * shard : (chunk + 1) * shard] = hidden_w[:, chunk * dim : (chunk + 1) * dim]
        second[dim:] = output_w[: shard // 2]

    @pl.when(sp % 2 == 1)
    def _():
        second[:dim] = return_w[...]
        second[dim:] = output_w[shard // 2 :]

    for batch in range(batches):
        height, image_width = sizes[batch, 0, 0], sizes[batch, 0, 1]
        rows = slice(batch * tok, (batch + 1) * tok)
        normal, rstd = normalize(tokens[batch, 0].reshape(tok, dim).astype(f32))
        normal_ref[rows] = normal
        rstd_ref[rows] = jnp.broadcast_to(rstd, (tok, 128))
        mask_ref[rows] = token_mask(sp * row_dev, row_dev, cols, dim, height, image_width)
        col_ids = lax.broadcasted_iota(jnp.int32, (half_cols, dim), 0)

        def key_row_bias(index, _, batch=batch, height=height, image_width=image_width, col_ids=col_ids):
            key_row = index
            if n_sp == 8:
                key_row = (sp ^ (index // rows_dev)) * rows_dev + lax.rem(index, rows_dev)
            width = jnp.where(2 * key_row < height, image_width, 0)
            here = pl.ds(pl.multiple_of(index * half_cols, half_cols), half_cols)
            bias_ref[batch, here, :] = jnp.where(2 * col_ids < width, 0.0, NEG).astype(bf16)
            return 0

        lax.fori_loop(0, n_sp * rows_dev, key_row_bias, 0)


def reduce_kernel(dims, *refs):
    n_fs, batches, row_dev, cols, dim = dims
    ins, mine, other, outs = take(refs, 6, n_fs - 1, n_fs - 1)
    normal_in, mask_ref, own_w, own_q, own_kv, own_vec = ins
    normed_ref, cols_ref, send_ref, reduced_ref, key_ref, weight_ref, wq, wkv, vec_ref, patch_ref, wide = outs
    half = dim // 2
    shard = dim // n_fs
    rest = half + VECS
    tok = row_dev * cols
    half_cols = cols // 2
    key_dev = tok // 4
    fs = lax.axis_index("fs")
    weight_ref[fs] = own_w[...]
    here = shard_rows(fs, shard)
    wq[here, :] = own_q[...]
    wkv[here, :] = own_kv[...]
    vec = own_vec[...]
    for step in range(1, n_fs):
        low, high = both_halves(mine[step - 1], other[step - 1])
        place = lax.rem(fs + n_fs - step, n_fs)
        weight_ref[place, :half] = low[:half]
        weight_ref[place, half:] = high[:half]
        vec = vec + low[half:rest].astype(f32)
        here = shard_rows(place, shard)
        wq[here, :] = low[rest : rest + shard]
        wkv[here, :dim] = jnp.concatenate([low[rest + shard :], high[rest : rest + shard // 2]], axis=0)
        wkv[here, dim:] = high[rest + shard // 2 :]
    vec_ref[...] = vec
    for batch in range(batches):
        rows = slice(batch * tok, (batch + 1) * tok)
        low = (normal_in[rows] * vec[FIRST_G : FIRST_G + 1] + vec[FIRST_B : FIRST_B + 1]).astype(bf16)
        normed_ref[rows] = low
        masked = low.astype(f32) * mask_ref[rows]
        for part in range(dim // 128):
            wide[part] = masked[:, part * 128 : (part + 1) * 128]
        for row in range(row_dev // 2):
            start = batch * key_dev + row * half_cols
            for offset in range(4):
                dr, dc = offset // 2, offset % 2
                for part in range(dim // 128):
                    piece = wide[part, pl.ds((2 * row + dr) * cols + dc, half_cols, stride=2), :]
                    lanes = slice(offset * dim + part * 128, offset * dim + (part + 1) * 128)
                    patch_ref[start : start + half_cols, lanes] = piece.astype(bf16)
    is_low = lax.axis_index("sp") % 2 == 0
    for offset in range(4):
        low = patch_ref[:, offset * dim : offset * dim + half]
        high = patch_ref[:, offset * dim + half : (offset + 1) * dim]
        cols_ref[offset] = jnp.where(is_low, low, high)
        send_ref[offset] = jnp.where(is_low, high, low)
    reduced = mm(patch_ref[...], weight_ref[...].reshape(4 * dim, dim)) + vec[REDUCE_B : REDUCE_B + 1]
    reduced_ref[...] = reduced
    normal, _ = normalize(reduced)
    key_ref[...] = (normal * vec[KEYS_G : KEYS_G + 1] + vec[KEYS_B : KEYS_B + 1]).astype(bf16)


def relay_kernel(n, *refs):
    for source, target in zip(refs[:n], refs[n + 1 :]):
        target[...] = source[...]


def head_stack_t(values_t, pair, tok):
    both = jnp.concatenate([values_t, values_t], axis=1)
    head = lax.broadcasted_iota(jnp.int32, both.shape, 0) // HDIM
    want = 2 * pair + jnp.where(lax.broadcasted_iota(jnp.int32, both.shape, 1) >= tok, 1, 0)
    return jnp.where(head == want, both, jnp.zeros_like(both))


def head_stack(values, pair):
    head = lax.broadcasted_iota(jnp.int32, values.shape, 1) // HDIM
    zero = jnp.zeros_like(values)
    return jnp.concatenate(
        [jnp.where(head == 2 * pair, values, zero), jnp.where(head == 2 * pair + 1, values, zero)],
        axis=0,
    )


def split_pair(both, tok):
    return jnp.concatenate([both[:HDIM, :tok], both[HDIM:, tok:]], axis=0)


def key_rows_of(pieces, key_dev, per_block, batch, index):
    here = slice(batch * key_dev, (batch + 1) * key_dev)
    if len(pieces) > 1:
        return jnp.concatenate([part[here] for part in pieces], axis=0)
    dim = pieces[0].shape[2]
    devices = slice(index * per_block, (index + 1) * per_block)
    return pieces[0][devices, here, :].reshape(per_block * key_dev, dim)


def mask_lane(pair, dim):
    return 0 if pair == PAIRS - 1 else dim - 1


def with_bias(key_block, bias, lane_id):
    lane = lax.broadcasted_iota(jnp.int32, key_block.shape, 1)
    return jnp.where(lane == lane_id, bias.astype(f32), key_block.astype(f32)).astype(bf16)


def query_stack(queries_t, pair, lane_id, tok):
    stacked = head_stack_t(queries_t, pair, tok)
    row = lax.broadcasted_iota(jnp.int32, stacked.shape, 0)
    return jnp.where(row == lane_id, jnp.ones_like(stacked), stacked)


def take(refs, *counts):
    refs = list(refs)
    groups = []
    for count in counts:
        groups.append(refs[:count])
        refs = refs[count:]
    return groups + [refs]


def forward_kernel(dims, *refs):
    batch, tok, key_dev, keys, block, n_pieces = dims
    (normed, vec_ref, bias_ref, wq, wkv), pieces, outs = take(refs, 5, n_pieces)
    attended, queries_out, kvs, attf, stats, probs, wide = outs
    dim = wq.shape[0]
    blocks = keys // block
    per_block = block // key_dev
    queries = (mm(normed[batch * tok : (batch + 1) * tok], wq[...]) + vec_ref[QUERY_B : QUERY_B + 1]).astype(bf16)
    queries_out[...] = queries
    queries_t = queries.T
    for index in range(blocks):
        key_rows = key_rows_of(pieces, key_dev, per_block, batch, index)
        here = slice(index * block, (index + 1) * block)
        kvs[here, :dim] = mm(key_rows, wkv[:, :dim]).astype(bf16)
        value_rows = mm(key_rows, wkv[:, dim:]) + vec_ref[VALUE_B : VALUE_B + 1]
        kvs[here, dim:] = value_rows.astype(bf16)
    if blocks == 1:
        key_block = kvs[:, :dim]
        values_t = kvs[:, dim:].T
        masked = {lane_id: with_bias(key_block, bias_ref[batch], lane_id) for lane_id in (0, dim - 1)}

        def score(pair):
            lane_id = mask_lane(pair, dim)
            wide[pair % 2] = mm(masked[lane_id], query_stack(queries_t, pair, lane_id, tok))

        score(0)
        for pair in range(PAIRS):
            if pair + 1 < PAIRS:
                score(pair + 1)
            heads = slice(2 * HDIM * pair, 2 * HDIM * (pair + 1))
            scores = wide[pair % 2]
            top = jnp.max(scores, axis=0, keepdims=True)
            weights = jnp.exp2((scores - top) * EXP_SCALE)
            inverse = 1.0 / jnp.sum(weights, axis=0, keepdims=True)
            low = weights.astype(bf16)
            probs[pair] = low
            stats[pair, 0:1] = inverse
            mixed = mm(values_t[heads], low) * inverse
            attf[heads] = split_pair(mixed, tok)
    else:
        for pair in range(PAIRS):
            lane_id = mask_lane(pair, dim)
            heads = slice(2 * HDIM * pair, 2 * HDIM * (pair + 1))
            stacked = query_stack(queries_t, pair, lane_id, tok)

            def block_scores(index, stacked=stacked, lane_id=lane_id):
                here = pl.ds(pl.multiple_of(index * block, block), block)
                masked = with_bias(kvs[here, :dim], bias_ref[batch, here, :], lane_id)
                return here, mm(masked, stacked)

            def find_top(index, top, block_scores=block_scores):
                _, scores = block_scores(index)
                return jnp.maximum(top, jnp.max(scores, axis=0, keepdims=True))

            top = lax.fori_loop(0, blocks, find_top, jnp.full((1, 2 * tok), 4 * NEG, f32))

            def add_block(index, carry, block_scores=block_scores, top=top, heads=heads):
                total, mixed = carry
                here, scores = block_scores(index)
                weights = jnp.exp2((scores - top) * EXP_SCALE)
                values_t = kvs[here, dim:].T
                mixed = mixed + mm(values_t[heads], weights.astype(bf16))
                return total + jnp.sum(weights, axis=0, keepdims=True), mixed

            start = (jnp.zeros((1, 2 * tok), f32), jnp.zeros((2 * HDIM, 2 * tok), f32))
            total, mixed = lax.fori_loop(0, blocks, add_block, start)
            inverse = 1.0 / total
            stats[pair, 0:1] = inverse
            stats[pair, 1:2] = top
            attf[heads] = split_pair(mixed * inverse, tok)
    attended[...] = attf[...].T.astype(bf16)


def mlp_kernel(dims, *refs):
    n_fs, batches, row_dev, cols, dim, hid = dims
    ins, attended, own, mine, other, _, outs, scratch = take(refs, 4, batches, 3, n_fs - 1, n_fs - 1, 1, 6)
    tokens, cotangent, mask_ref, vec_ref = ins
    acts_ref, middle_ref, gatt, keep_ref, send_ref, gvec_ref = outs
    wh, wr, wo, lows, highs = scratch
    tok = row_dev * cols
    shard = dim // n_fs
    chunks = hid // dim
    fs = lax.axis_index("fs")
    is_low = lax.axis_index("sp") % 2 == 0
    wh[shard_rows(fs, shard), :] = own[0][...]
    wr[shard_rows(fs, dim), :] = own[1][...]
    wo[shard_rows(fs, shard), :] = own[2][...]
    for step in range(1, n_fs):
        low, high = both_halves(mine[step - 1], other[step - 1])
        place = fs ^ step
        here = shard_rows(place, shard)
        for chunk in range(chunks):
            wh[here, chunk * dim : (chunk + 1) * dim] = low[chunk * shard : (chunk + 1) * shard]
        wr[shard_rows(place, dim), :] = high[:dim]
        wo[here, :] = jnp.concatenate([low[dim:], high[dim:]], axis=0)

    def vec(index):
        return vec_ref[index : index + 1, :]

    x = jnp.concatenate([tokens[b, 0].reshape(tok, dim).astype(f32) for b in range(batches)], axis=0)
    mask = mask_ref[...]
    attended = jnp.concatenate([part[...] for part in attended], axis=0)
    middle = x + mm(attended, wo[...]) + vec(OUTPUT_B)
    normal, rstd = normalize(middle)
    second = (normal * vec(SECOND_G) + vec(SECOND_B)).astype(bf16)
    grad_out = jnp.concatenate([cotangent[b, 0].reshape(tok, dim) for b in range(batches)], axis=0) * mask
    grad_mlp = grad_out.astype(bf16)
    second_t, grad_mlp_t = second.T, grad_mlp.T
    total = middle + vec(RETURN_B)
    grad_second = jnp.zeros((batches * tok, dim), f32)
    gvec_ref[...] = jnp.zeros_like(gvec_ref)
    for chunk in range(chunks):
        lanes = slice(chunk * dim, (chunk + 1) * dim)
        hidden = mm(second, wh[:, lanes]) + vec(HIDDEN_B + chunk)
        phi = 0.5 + 0.5 * lax.erf(hidden * 0.7071067811865476)
        density = 0.3989422804014327 * jnp.exp2(hidden * hidden * (-0.5 * 1.4426950408889634))
        activated = (hidden * phi).astype(bf16)
        total = total + mm(activated, wr[lanes, :])
        grad_activated = mm_nt(grad_mlp, wr[lanes, :])
        grad_hidden = ((phi + hidden * density) * grad_activated).astype(bf16)
        gvec_ref[HIDDEN_B + chunk : HIDDEN_B + chunk + 1] = jnp.sum(
            grad_hidden.astype(f32), axis=0, keepdims=True
        )
        grad_second = grad_second + mm_nt(grad_hidden, wh[:, lanes])
        highs[chunk] = mm(grad_mlp_t, activated).T.astype(bf16)
        grad_wh = mm(second_t, grad_hidden).astype(bf16)
        for owner in range(n_fs):
            lows[owner, chunk * shard : (chunk + 1) * shard] = grad_wh[owner * shard : (owner + 1) * shard]
    low, high = lows[...], highs[...]
    keep_ref[...] = jnp.where(is_low, low, high)
    send_ref[...] = jnp.where(is_low, high, low)
    total = total * mask
    for batch in range(batches):
        acts_ref[batch, 0] = total[batch * tok : (batch + 1) * tok].reshape(row_dev, cols, dim)
    grad_middle = grad_out + normalize_back(grad_second, normal, rstd, vec(SECOND_G))
    middle_ref[...] = grad_middle
    grad_branch = grad_middle.astype(bf16)
    gatt[...] = mm_nt(grad_branch, wo[...]).astype(bf16)
    for index, value in (
        (OUTPUT_B, grad_branch.astype(f32)),
        (SECOND_G, grad_second * normal),
        (SECOND_B, grad_second),
        (RETURN_B, grad_mlp.astype(f32)),
    ):
        gvec_ref[index : index + 1] = jnp.sum(value, axis=0, keepdims=True)


def backward_kernel(dims, *refs):
    n_sp, batch, tok, key_dev, keys, block, n_pieces = dims
    gatt, queries_ref, kvs, attf, stats, probs, bias_ref, wkv, _ = refs[:9]
    near_ref, far_ref, scores_ref, gks, gvs, gvec_ref = refs[9:15]
    dim = wkv.shape[0]
    blocks = keys // block
    per_block = block // key_dev
    rows = slice(batch * tok, (batch + 1) * tok)
    queries = queries_ref[...]
    grad_att_t = gatt[rows].astype(f32).T
    product = grad_att_t * attf[...]

    def pair_terms(pair):
        inverse = stats[pair, 0:1]
        piece = product[2 * HDIM * pair : 2 * HDIM * (pair + 1)]
        delta = jnp.concatenate(
            [jnp.sum(piece[:HDIM], axis=0, keepdims=True), jnp.sum(piece[HDIM:], axis=0, keepdims=True)],
            axis=1,
        )
        stacked = head_stack_t(grad_att_t, pair, tok) * inverse
        return delta * inverse, stacked.astype(bf16)

    if blocks == 1:
        (wide,) = refs[15:]
        values = kvs[:, dim:]
        grad_k = jnp.zeros((keys, dim), f32)
        grad_v = jnp.zeros((keys, dim), f32)
        terms = []

        def grad_prob(pair):
            delta, stacked = pair_terms(pair)
            wide[pair % 2] = mm(values, stacked)
            terms.append((delta, stacked))

        grad_prob(0)
        for pair in range(PAIRS):
            if pair + 1 < PAIRS:
                grad_prob(pair + 1)
            delta, stacked = terms[pair]
            low = probs[pair]
            grad_scores = (low.astype(f32) * (wide[pair % 2] - delta)).astype(bf16)
            scores_ref[pair] = grad_scores
            grad_k = grad_k + mm(grad_scores, head_stack(queries, pair))
            grad_v = grad_v + mm(low, stacked.T)
    else:
        wide_k, wide_v = refs[15:]
        wide_k[...] = jnp.zeros_like(wide_k)
        wide_v[...] = jnp.zeros_like(wide_v)
        queries_t = queries.T
        for pair in range(PAIRS):
            heads = slice(2 * HDIM * pair, 2 * HDIM * (pair + 1))
            lane_id = mask_lane(pair, dim)
            delta, stacked = pair_terms(pair)
            stacked_n = stacked.T
            query_t = query_stack(queries_t, pair, lane_id, tok)
            query_n = head_stack(queries, pair)
            top = stats[pair, 1:2]

            def back_block(index, gq, heads=heads, lane_id=lane_id, delta=delta, stacked=stacked, stacked_n=stacked_n, query_t=query_t, query_n=query_n, top=top):
                here = pl.ds(pl.multiple_of(index * block, block), block)
                key_block = kvs[here, :dim]
                masked = with_bias(key_block, bias_ref[batch, here, :], lane_id)
                weights = jnp.exp2((mm(masked, query_t) - top) * EXP_SCALE)
                grad_probs = mm(kvs[here, dim:], stacked)
                grad_scores = (weights * (grad_probs - delta)).astype(bf16)
                wide_k[here, :] += mm(grad_scores, query_n)
                wide_v[here, :] += mm(weights.astype(bf16), stacked_n)
                return gq + mm(key_block.T[heads], grad_scores)

            gq = lax.fori_loop(0, blocks, back_block, jnp.zeros((2 * HDIM, 2 * tok), f32))
            scores_ref[heads] = split_pair(gq, tok)
    bias_value = jnp.zeros((1, dim), f32)
    for index in range(blocks):
        here = slice(index * block, (index + 1) * block)
        if blocks > 1:
            grad_k, grad_v = wide_k[here], wide_v[here]
        grad_k = (grad_k * SCALE).astype(bf16)
        bias_value = bias_value + jnp.sum(grad_v, axis=0, keepdims=True)
        grad_v = grad_v.astype(bf16)
        gks[here] = grad_k
        gvs[here] = grad_v
        grad_key = (mm_nt(grad_k, wkv[:, :dim]) + mm_nt(grad_v, wkv[:, dim:])).astype(bf16)
        if n_pieces > 1:
            pairs = grad_key.reshape(n_sp // 2, 2, key_dev, dim)
            near_ref[...] = pairs[:, 0]
            far_ref[...] = pairs[:, 1]
        else:
            near_ref[index * per_block : (index + 1) * per_block] = grad_key.reshape(per_block, key_dev, dim)
    gvec_ref[...] = jnp.broadcast_to(bias_value, gvec_ref.shape)


def query_kernel(dims, *refs):
    n_fs, batches, tok, key_dev, keys, block, n_pieces = dims
    ins, attended, kvs, scores, gks, gvs, gvecs, pieces, outs = take(refs, 3, *([batches] * 6), n_pieces)
    normed, wq, middle = ins
    keep_ref, send_ref, gnormed_ref, gvec_ref, wide = outs
    dim = wq.shape[0]
    shard = dim // n_fs
    blocks = keys // block
    per_block = block // key_dev
    grad_queries = []
    grad_wk = jnp.zeros((dim, dim), f32)
    grad_wv = jnp.zeros((dim, dim), f32)
    for batch in range(batches):
        if blocks == 1:
            keys_t = kvs[batch][:, :dim].T
            for pair in range(PAIRS):
                heads = slice(2 * HDIM * pair, 2 * HDIM * (pair + 1))
                wide[heads] = split_pair(mm(keys_t[heads], scores[batch][pair]), tok)
            grad_t = wide[...]
        else:
            grad_t = scores[batch][...]
        grad_queries.append((grad_t.T * SCALE).astype(bf16))
        for index in range(blocks):
            here = slice(index * block, (index + 1) * block)
            key_rows = key_rows_of(pieces, key_dev, per_block, batch, index)
            grad_wk = grad_wk + mm_tn(key_rows, gks[batch][here])
            grad_wv = grad_wv + mm_tn(key_rows, gvs[batch][here])
    grad_queries = jnp.concatenate(grad_queries, axis=0)
    grad_wq = mm_tn(normed[...], grad_queries)
    attended = jnp.concatenate([part[...] for part in attended], axis=0)
    grad_wo = mm_tn(attended, middle[...].astype(bf16))
    is_low = lax.axis_index("sp") % 2 == 0
    for owner in range(n_fs):
        part = slice(owner * shard, (owner + 1) * shard)
        low = jnp.concatenate([grad_wq[part], grad_wk[part]], axis=0).astype(bf16)
        high = jnp.concatenate([grad_wv[part], grad_wo[part]], axis=0).astype(bf16)
        keep_ref[owner] = jnp.where(is_low, low, high)
        send_ref[owner] = jnp.where(is_low, high, low)
    gnormed_ref[...] = mm_nt(grad_queries, wq[...])
    gvec_ref[...] = jnp.zeros_like(gvec_ref)
    gvec_ref[QUERY_B : QUERY_B + 1] = jnp.sum(grad_queries.astype(f32), axis=0, keepdims=True)
    bias_value = gvecs[0][0:1]
    for gvec in gvecs[1:]:
        bias_value = bias_value + gvec[0:1]
    gvec_ref[VALUE_B : VALUE_B + 1] = bias_value


def sum_parts(parts):
    if len(parts) == 1:
        total = parts[0][0].astype(f32)
        for index in range(1, parts[0].shape[0]):
            total = total + parts[0][index].astype(f32)
        return total
    total = parts[0][...].astype(f32)
    for part in parts[1:]:
        total = total + part[...].astype(f32)
    return total


def reduction_kernel(n_parts, batches, reduced, vec_ref, *refs):
    parts, gvec_ref, outs = refs[:n_parts], refs[-1], refs[-1 - batches : -1]
    grad_key = sum_parts(parts)
    normal, rstd = normalize(reduced[...])
    grad_low = normalize_back(grad_key, normal, rstd, vec_ref[KEYS_G : KEYS_G + 1]).astype(bf16)
    rows = outs[0].shape[0]
    for batch, out in enumerate(outs):
        out[...] = grad_low[batch * rows : (batch + 1) * rows]
    gvec_ref[...] = jnp.zeros_like(gvec_ref)
    for index, value in (
        (REDUCE_B, grad_low.astype(f32)),
        (KEYS_G, grad_key * normal),
        (KEYS_B, grad_key),
    ):
        gvec_ref[index : index + 1] = jnp.sum(value, axis=0, keepdims=True)


def weight_kernel(batches, *refs):
    (own_cols, other_cols), own, other, (vectors, *outs) = take(refs, 2, batches, batches)
    fs = lax.axis_index("fs")
    own = jnp.concatenate([part[...] for part in own], axis=0)
    other = jnp.concatenate([part[...] for part in other], axis=0)
    rows = own_cols.shape[2]
    for step, out in enumerate(outs):
        place = lax.rem(fs + step, len(outs))
        out[:rows] = (mm_tn(own_cols[place], own) + mm_tn(other_cols[place], other)).astype(out.dtype)
        out[rows:] = vectors[...]


def normed_kernel(dims, gnormed, mask_ref, weight, normal_ref, vec_a, vec_b, vec_c, *refs):
    batches, row_dev, cols, dim = dims
    grads, (grad_ref, gvec_ref, wide) = take(refs, batches)
    tok = row_dev * cols
    half_cols = cols // 2
    gain_first = jnp.zeros((1, dim), f32)
    bias_first = jnp.zeros((1, dim), f32)
    for batch in range(batches):
        for offset in range(4):
            dr, dc = offset // 2, offset % 2
            back = mm_nt(grads[batch][...], weight[offset])
            for row in range(row_dev // 2):
                for part in range(dim // 128):
                    wide[part, pl.ds((2 * row + dr) * cols + dc, half_cols, stride=2), :] = back[
                        row * half_cols : (row + 1) * half_cols, part * 128 : (part + 1) * 128
                    ]
        rows = slice(batch * tok, (batch + 1) * tok)
        spread = jnp.concatenate([wide[part] for part in range(dim // 128)], axis=1)
        grad_normed = gnormed[rows] + spread * mask_ref[rows]
        grad_ref[rows] = grad_normed
        gain_first = gain_first + jnp.sum(grad_normed * normal_ref[rows], axis=0, keepdims=True)
        bias_first = bias_first + jnp.sum(grad_normed, axis=0, keepdims=True)
    index = lax.broadcasted_iota(jnp.int32, (VECS, dim), 0)
    vectors = vec_a[...] + vec_b[...] + vec_c[...]
    vectors = jnp.where(index == FIRST_G, gain_first, vectors)
    vectors = jnp.where(index == FIRST_B, bias_first, vectors)
    gvec_ref[...] = vectors.astype(bf16)


def input_kernel(dims, middle, grad_normed, normal_ref, rstd_ref, vec_ref, _, grad_ref, done_ref):
    batches, row_dev, cols, dim = dims
    tok = row_dev * cols
    rstd = jnp.concatenate([rstd_ref[...]] * (dim // rstd_ref.shape[1]), axis=1)
    back = normalize_back(grad_normed[...], normal_ref[...], rstd, vec_ref[FIRST_G : FIRST_G + 1])
    grad_x = middle[...] + back
    for batch in range(batches):
        grad_ref[batch, 0] = grad_x[batch * tok : (batch + 1) * tok].reshape(row_dev, cols, dim)
    done_ref[...] = jnp.zeros_like(done_ref)


def key_sum_kernel(batches, *refs):
    near, far, _, outs = take(refs, batches, batches, 2)
    for step, out in enumerate(outs):
        rows = near[0].shape[1]
        for batch in range(batches):
            total = near[batch][step].astype(f32) + far[batch][step].astype(f32)
            out[batch * rows : (batch + 1) * rows] = total.astype(out.dtype)


def owner_kernel(keep, arrived, *outs):
    fs = lax.axis_index("fs")
    for step, out in enumerate(outs):
        place = lax.rem(fs + step, len(outs))
        out[...] = (keep[place].astype(f32) + arrived[place].astype(f32)).astype(out.dtype)


def chip_kernel(keep, arrived, _, *outs):
    chip = lax.axis_index("sp") // 2
    rows = outs[0].shape[1]
    for step, out in enumerate(outs):
        here = shard_rows(chip ^ step, rows)
        out[...] = (keep[:, here, :].astype(f32) + arrived[:, here, :].astype(f32)).astype(out.dtype)


def chip_sum_kernel(*refs):
    refs[-1][...] = sum_parts(refs[:-1]).astype(refs[-1].dtype)


def owners_kernel(total, keep, arrived, *outs):
    fs = lax.axis_index("fs")
    rows = total.shape[1]
    for step, out in enumerate(outs):
        place = lax.rem(fs + step, len(outs))
        out[:rows] = total[place]
        out[rows:] = (keep[place].astype(f32) + arrived[place].astype(f32)).astype(out.dtype)


def join_kernel(n, *refs):
    refs[-1][...] = sum_parts(refs[:n]).astype(refs[-1].dtype)


def merge_kernel(rows, *refs):
    parts, out = refs[:4], refs[5]
    chip = lax.axis_index("sp") // 2
    if rows:
        for step, part in enumerate(parts):
            out[shard_rows(chip ^ step, rows), :] = part[:rows]
    rest = [part[rows:].astype(f32) for part in parts]
    out[4 * rows :] = ((rest[0] + rest[1]) + (rest[2] + rest[3])).astype(out.dtype)


def final_kernel(n_fs, mine, other, mine_b, other_b, *outs):
    query_w, keyval_w, output_w, hidden_w, return_w, reduce_w = outs[:6]
    smalls, hidden_b = outs[6:-1], outs[-1]
    shard, dim = query_w.shape
    half = dim // 2
    fs = lax.axis_index("fs")
    low, high = both_halves(mine, other)
    low, high = low.astype(f32), high.astype(f32)
    for chunk in range(hidden_w.shape[1] // dim):
        hidden_w[:, chunk * dim : (chunk + 1) * dim] = low[chunk * shard : (chunk + 1) * shard]
    return_w[...] = high[:dim]
    low, high = low[dim:], high[dim:]
    query_w[...] = low[:shard]
    keyval_w[:, :dim] = low[shard : 2 * shard]
    keyval_w[:, dim:] = high[:shard]
    output_w[...] = high[shard : 2 * shard]
    low, high = both_halves(mine_b, other_b)
    low, high = low.astype(f32), high.astype(f32)
    reduce_w[:half] = low[:half]
    reduce_w[half:] = high[:half]
    vecs = low[half:] + high[half:]
    lane = lax.broadcasted_iota(jnp.int32, vecs.shape, 1)
    chosen = jnp.where(lane // shard == fs, vecs, 0.0)
    folded = chosen[:, :shard]
    for index in range(1, n_fs):
        folded = folded + chosen[:, index * shard : (index + 1) * shard]
    for index, small in enumerate(smalls):
        small[...] = folded[index : index + 1].reshape(shard)
    row = lax.broadcasted_iota(jnp.int32, vecs.shape, 0)
    hidden_b[...] = jnp.sum(jnp.where(row == HIDDEN_B + fs, vecs, 0.0), axis=0)


def rotate(value, n, step):
    return lax.ppermute(value, "fs", [(i, (i + step) % n) for i in range(n)])


def swap(value, n, bits):
    return lax.ppermute(value, "fs", [(i, i ^ bits) for i in range(n)])


def flip(value, n, bits):
    return lax.ppermute(value, "sp", [(i, i ^ bits) for i in range(n)])


def sum_over_rows(value, n_sp):
    bit = 2
    while bit < n_sp:
        if 2 * bit < n_sp:
            a, b, c = flip(value, n_sp, bit), flip(value, n_sp, 2 * bit), flip(value, n_sp, 3 * bit)
            value = (
                (value.astype(f32) + a.astype(f32)) + (b.astype(f32) + c.astype(f32))
            ).astype(value.dtype)
            bit = 4 * bit
        else:
            a = flip(value, n_sp, bit)
            value = (value.astype(f32) + a.astype(f32)).astype(value.dtype)
            bit = 2 * bit
    return value


def exchange(pieces, n_sp):
    return [pieces[0]] + [flip(pieces[step], n_sp, 2 * step) for step in range(1, n_sp // 2)]


def to_owners(pieces, n_fs):
    return [pieces[0]] + [rotate(pieces[step], n_fs, step) for step in range(1, n_fs)]


def call(kernel, out_shape, in_specs=None, scratch=(), limit=SMALL_VMEM, micros=0):
    specs = {} if in_specs is None else {"in_specs": in_specs}
    return pl.pallas_call(
        kernel,
        out_shape=out_shape,
        **specs,
        scratch_shapes=scratch,
        compiler_params=pltpu.CompilerParams(vmem_limit_bytes=limit),
        cost_estimate=pl.CostEstimate(flops=int(micros * 1e9), bytes_accessed=0, transcendentals=0),
    )


def on_device(
    n_fs,
    n_sp,
    tokens,
    cotangent,
    image_sizes,
    first_gain,
    first_bias,
    query_weight,
    query_bias,
    reduce_weight,
    reduce_bias,
    keys_gain,
    keys_bias,
    keyval_weight,
    value_bias,
    output_weight,
    output_bias,
    second_gain,
    second_bias,
    hidden_weight,
    hidden_bias,
    return_weight,
    return_bias,
):
    batches, _, row_dev, cols, dim = tokens.shape
    hid = hidden_weight.shape[1]
    tok = row_dev * cols
    key_dev = tok // 4
    keys = n_sp * key_dev
    shard = dim // n_fs
    half = dim // 2
    vmem = pl.BlockSpec(memory_space=pltpu.VMEM)
    smem = pl.BlockSpec(memory_space=pltpu.SMEM)
    single = keys <= KEY_BLOCK
    split = n_sp == 8
    block = keys if single else KEY_BLOCK
    limit = MAIN_VMEM if single else WHOLE_VMEM

    def shape(*dims, dtype=bf16):
        return jax.ShapeDtypeStruct(dims, dtype)

    smalls = (
        first_gain,
        first_bias,
        query_bias,
        reduce_bias,
        keys_gain,
        keys_bias,
        value_bias,
        output_bias,
        second_gain,
        second_bias,
        return_bias,
    )
    first_half = call(
        functools.partial(pack_first_kernel, n_fs),
        shape(half + VECS + 3 * shard // 2, dim),
        scratch=[pltpu.VMEM((VECS, dim), f32)],
        limit=WHOLE_VMEM,
    )(*smalls, hidden_bias, reduce_weight, query_weight, keyval_weight)
    mine_first = to_owners([first_half] * n_fs, n_fs)[1:]

    begun = call(
        functools.partial(begin_kernel, (n_sp, batches, row_dev, cols, dim)),
        [
            shape(batches * tok, dim, dtype=f32),
            shape(batches * tok, 128, dtype=f32),
            shape(batches * tok, dim, dtype=f32),
            shape(batches, keys, dim),
            shape(dim, dim),
            shape(shard, dim),
            shape(shard, 2 * dim),
            shape(VECS, dim, dtype=f32),
            shape(dim + shard // 2, dim),
        ],
        in_specs=[smem] + [vmem] * 8,
        limit=SMALL_VMEM if single else WHOLE_VMEM,
    )(
        image_sizes,
        tokens,
        reduce_weight,
        query_weight,
        keyval_weight,
        hidden_weight,
        return_weight,
        output_weight,
        first_half,
    )
    normal_first, rstd_first, mask, bias, own_r, own_q, own_kv, own_vec, second_half = begun
    mine_first = call(functools.partial(relay_kernel, n_fs - 1), [shape(*first_half.shape)] * (n_fs - 1))(
        *mine_first, own_vec
    )
    other_first = [flip(piece, n_sp, 1) for piece in mine_first]
    normed, patch_cols, patch_send, reduced, key_low, whole_reduce, wq, wkv, vec = call(
        functools.partial(reduce_kernel, (n_fs, batches, row_dev, cols, dim)),
        [
            shape(batches * tok, dim),
            shape(4, batches * key_dev, half),
            shape(4, batches * key_dev, half),
            shape(batches * key_dev, dim, dtype=f32),
            shape(batches * key_dev, dim),
            shape(n_fs, dim, dim),
            shape(dim, dim),
            shape(dim, 2 * dim),
            shape(VECS, dim, dtype=f32),
        ],
        scratch=[pltpu.VMEM((batches * key_dev, 4 * dim), bf16), pltpu.VMEM((dim // 128, tok, 128), f32)],
    )(normal_first, mask, own_r, own_q, own_kv, own_vec, *mine_first, *other_first)
    across = swap(second_half, n_fs, 2)
    passed = call(functools.partial(relay_kernel, 1), [shape(dim + shard // 2, dim)], micros=15)(across, own_vec)
    mine_second = [swap(second_half, n_fs, 1), across, swap(passed[0], n_fs, 1)]

    if split:
        same = exchange([key_low] * (n_sp // 2), n_sp)
        key_pieces = [piece for part in same for piece in (part, flip(part, n_sp, 1))]
    else:
        key_pieces = [lax.all_gather(key_low, "sp")]
    n_pieces = len(key_pieces)

    kept = [
        call(
            functools.partial(forward_kernel, (batch, tok, key_dev, keys, block, n_pieces)),
            [
                shape(tok, dim),
                shape(tok, dim),
                shape(keys, 2 * dim),
                shape(dim, tok, dtype=f32),
                shape(PAIRS, 8, 2 * tok, dtype=f32),
                shape(PAIRS, keys, 2 * tok) if single else shape(16, 128),
            ],
            scratch=[pltpu.VMEM((2, block, 2 * tok) if single else (8, 128), f32)],
            limit=limit,
        )(normed, vec, bias, wq, wkv, *key_pieces)
        for batch in range(batches)
    ]
    attended = [results[0] for results in kept]
    kept = [results[1:] for results in kept]
    mine_second = call(functools.partial(relay_kernel, n_fs - 1), [shape(dim + shard // 2, dim)] * (n_fs - 1))(
        *mine_second, kept[0][3]
    )
    patch_other = flip(patch_send, n_sp, 1)
    other_second = [flip(piece, n_sp, 1) for piece in mine_second]

    acts, middle, gatt, keep_a, send_a, gvec_a = call(
        functools.partial(mlp_kernel, (n_fs, batches, row_dev, cols, dim, hid)),
        [
            shape(batches, 1, row_dev, cols, dim, dtype=f32),
            shape(batches * tok, dim, dtype=f32),
            shape(batches * tok, dim),
            shape(n_fs, dim, dim),
            shape(n_fs, dim, dim),
            shape(VECS, dim, dtype=f32),
        ],
        scratch=[
            pltpu.VMEM((dim, hid), bf16),
            pltpu.VMEM((hid, dim), bf16),
            pltpu.VMEM((dim, dim), bf16),
            pltpu.VMEM((n_fs, dim, dim), bf16),
            pltpu.VMEM((n_fs, dim, dim), bf16),
        ],
        limit=limit,
    )(
        tokens,
        cotangent,
        mask,
        vec,
        *attended,
        hidden_weight,
        return_weight,
        output_weight,
        *mine_second,
        *other_second,
        patch_other,
    )
    arrived_a = flip(send_a, n_sp, 1)
    gkey_dims = (n_sp // 2, key_dev, dim) if split else (n_sp, key_dev, dim)
    back = []
    for batch in range(batches):
        queries, kvs, attf, stats, probs = kept[batch]
        order = vec
        if split and batch == batches - 1:
            pieces_a = call(chip_kernel, [shape(n_fs, dim // 4, dim)] * 4)(keep_a, arrived_a, back[0][5])
            total_a = call(chip_sum_kernel, shape(n_fs, dim // 4, dim), micros=5)(*exchange(pieces_a, n_sp))
            order = pieces_a[0]
        back.append(
            call(
                functools.partial(backward_kernel, (n_sp, batch, tok, key_dev, keys, block, n_pieces)),
                [
                    shape(*gkey_dims),
                    shape(*(gkey_dims if split else (16, 128))),
                    shape(PAIRS, keys, 2 * tok) if single else shape(dim, tok, dtype=f32),
                    shape(keys, dim),
                    shape(keys, dim),
                    shape(8, dim, dtype=f32),
                ],
                scratch=[pltpu.VMEM((2, keys, 2 * tok), f32)] if single else [pltpu.VMEM((keys, dim), f32)] * 2,
                limit=limit,
            )(gatt, queries, kvs, attf, stats, probs, bias, wkv, order)
        )
    near = [results[0] for results in back]
    keep_c, send_c, gnormed, gvec_c = call(
        functools.partial(query_kernel, (n_fs, batches, tok, key_dev, keys, block, n_pieces)),
        [
            shape(n_fs, half, dim),
            shape(n_fs, half, dim),
            shape(batches * tok, dim, dtype=f32),
            shape(VECS, dim, dtype=f32),
        ],
        scratch=[pltpu.VMEM((dim, tok), f32)],
        limit=limit,
    )(
        normed,
        wq,
        middle,
        *attended,
        *[kept[batch][1] for batch in range(batches)],
        *[results[2] for results in back],
        *[results[3] for results in back],
        *[results[4] for results in back],
        *[results[5] for results in back],
        *key_pieces,
    )
    arrived_c = flip(send_c, n_sp, 1)
    if split:
        far = [flip(results[1], n_sp, 1) for results in back]
        sums = call(functools.partial(key_sum_kernel, batches), [shape(batches * key_dev, dim)] * 4)(
            *near, *far, total_a, gvec_c
        )
        parts = exchange(sums, n_sp)
    else:
        parts = [lax.all_to_all(jnp.concatenate(near, axis=1), "sp", 0, 0)]
    *grad_reduced, gvec_b = call(
        functools.partial(reduction_kernel, len(parts), batches),
        [shape(key_dev, dim)] * batches + [shape(VECS, dim, dtype=f32)],
    )(reduced, vec, *parts)
    grad_other = [flip(part, n_sp, 1) for part in grad_reduced]
    grad_normed, vectors = call(
        functools.partial(normed_kernel, (batches, row_dev, cols, dim)),
        [shape(batches * tok, dim, dtype=f32), shape(VECS, dim)],
        scratch=[pltpu.VMEM((dim // 128, tok, 128), f32)],
    )(gnormed, mask, whole_reduce, normal_first, gvec_a, gvec_b, gvec_c, *grad_reduced)
    chunks_b = call(functools.partial(weight_kernel, batches), [shape(half + VECS, dim)] * n_fs)(
        patch_cols, patch_other, *grad_reduced, *grad_other, vectors
    )
    if split:
        rows = dim // 4
        chunks = call(owners_kernel, [shape(rows + half, dim)] * n_fs)(total_a, keep_c, arrived_c)
        join = functools.partial(join_kernel, n_fs)
        first_a = to_owners(chunks, n_fs)
        last_a = first_a.pop(1)
        joined_a = call(functools.partial(join_kernel, n_fs - 1), shape(rows + half, dim), micros=5)(*first_a, vec)
        joined_a = call(functools.partial(join_kernel, 2), shape(rows + half, dim))(joined_a, last_a, vec)
        joined_b = call(join, shape(half + VECS, dim), micros=1)(*to_owners(chunks_b, n_fs), vec)
        mine = call(functools.partial(merge_kernel, rows), shape(4 * rows + half, dim))(
            *exchange([joined_a] * 4, n_sp), joined_b
        )
        order = mine
    else:
        order = vec
        groups = [to_owners(chunks_b, n_fs)]
        for keep, arrived in ((keep_c, arrived_c), (keep_a, arrived_a)):
            pieces = call(owner_kernel, [shape(*keep.shape[1:])] * n_fs)(keep, arrived)
            groups.insert(0, to_owners(pieces, n_fs))
        mine_a, mine_c, mine_b = (
            sum_over_rows(sum(piece.astype(f32) for piece in group).astype(bf16), n_sp) for group in groups
        )
        mine = jnp.concatenate([mine_a, mine_c], axis=0)

    grads, done = call(
        functools.partial(input_kernel, (batches, row_dev, cols, dim)),
        [shape(batches, 1, row_dev, cols, dim, dtype=f32), shape(8, 128, dtype=f32)],
    )(middle, grad_normed, normal_first, rstd_first, vec, order)

    if split:
        mine_b = call(functools.partial(merge_kernel, 0), shape(half + VECS, dim))(
            *exchange([joined_b] * 4, n_sp), done
        )
    (other_b,) = call(functools.partial(relay_kernel, 1), [shape(half + VECS, dim)], micros=1)(
        flip(mine_b, n_sp, 1), vec
    )
    gquery, gkeyval, goutput, ghidden, greturn, greduce, *vectors = call(
        functools.partial(final_kernel, n_fs),
        [
            shape(shard, dim, dtype=f32),
            shape(shard, 2 * dim, dtype=f32),
            shape(shard, dim, dtype=f32),
            shape(shard, hid, dtype=f32),
            shape(dim, dim, dtype=f32),
            shape(dim, dim, dtype=f32),
        ]
        + [shape(shard, dtype=f32)] * HIDDEN_B
        + [shape(dim, dtype=f32)],
    )(mine, flip(mine, n_sp, 1), mine_b, other_b)
    return (
        acts,
        grads,
        vectors[FIRST_G],
        vectors[FIRST_B],
        gquery,
        vectors[QUERY_B],
        greduce,
        vectors[REDUCE_B],
        vectors[KEYS_G],
        vectors[KEYS_B],
        gkeyval,
        vectors[VALUE_B],
        goutput,
        vectors[OUTPUT_B],
        vectors[SECOND_G],
        vectors[SECOND_B],
        ghidden,
        vectors[HIDDEN_B],
        greturn,
        vectors[RETURN_B],
    )


def solution(mesh):
    vec, mat = P("fs"), P("fs", None)
    image = P(None, "fs", "sp", None, None)
    weights = (vec, vec, mat, vec, mat, vec, vec, vec, mat, vec, mat, vec, vec, vec, mat, vec, mat, vec)
    return jax.shard_map(
        functools.partial(on_device, mesh.shape["fs"], mesh.shape["sp"]),
        mesh=mesh,
        in_specs=(image, image, P(None, "fs", None)) + weights,
        out_specs=(image, image) + weights,
        check_vma=False,
    )
```

```python
import functools

import jax
import jax.numpy as jnp
from jax import lax
from jax.experimental import pallas as pl
from jax.experimental.pallas import tpu as pltpu
from jax.sharding import PartitionSpec as P

HEADS = 8
HDIM = 32
PAIRS = HEADS // 2
SCALE = HDIM ** (-0.5)
EXP_SCALE = SCALE * 1.4426950408889634
EPS = 1e-06
NEG = -1e30
KEY_BLOCK = 768
SMALL_VMEM = 12 * 2**20
MAIN_VMEM = 16 * 2**20
WHOLE_VMEM = 58 * 2**20

bf16 = jnp.bfloat16
f32 = jnp.float32

(
    FIRST_G,
    FIRST_B,
    QUERY_B,
    REDUCE_B,
    KEYS_G,
    KEYS_B,
    VALUE_B,
    OUTPUT_B,
    SECOND_G,
    SECOND_B,
    RETURN_B,
    HIDDEN_B,
) = range(12)
VECS = 16


def mm(left, right):
    return jnp.dot(left, right, preferred_element_type=f32)


def mm_tn(left, right):
    return lax.dot_general(left, right, (((0,), (0,)), ((), ())), preferred_element_type=f32)


def mm_nt(left, right):
    return lax.dot_general(left, right, (((1,), (1,)), ((), ())), preferred_element_type=f32)


def normalize(rows):
    mean = jnp.mean(rows, axis=-1, keepdims=True)
    centered = rows - mean
    var = jnp.mean(centered * centered, axis=-1, keepdims=True)
    rstd = lax.rsqrt(var + EPS)
    return centered * rstd, rstd


def normalize_back(grad, normal, rstd, gain):
    scaled = grad * gain
    mean_a = jnp.mean(scaled, axis=-1, keepdims=True)
    mean_b = jnp.mean(scaled * normal, axis=-1, keepdims=True)
    return (scaled - mean_a - normal * mean_b) * rstd


def token_mask(first_row, rows, cols, width, height, image_width):
    row_ids = lax.broadcasted_iota(jnp.int32, (rows, cols, width), 0) + first_row
    col_ids = lax.broadcasted_iota(jnp.int32, (rows, cols, width), 1)
    valid = (row_ids < height) & (col_ids < image_width)
    return jnp.where(valid, 1.0, 0.0).astype(f32).reshape(rows * cols, width)


def pack_first_kernel(n_fs, *refs):
    smalls, (hidden_b, reduce_w, query_w, keyval_w, first, wide) = take(refs, HIDDEN_B)
    dim = reduce_w.shape[1]
    shard = dim // n_fs
    half = dim // 2
    rest = half + VECS
    fs = lax.axis_index("fs")
    is_low = lax.axis_index("sp") % 2 == 0

    @pl.when(is_low)
    def _():
        first[:half] = reduce_w[:half]
        first[rest : rest + shard] = query_w[...]
        first[rest + shard :] = keyval_w[: shard // 2, :dim]

    @pl.when(jnp.logical_not(is_low))
    def _():
        first[:half] = reduce_w[half:]
        first[rest : rest + shard // 2] = keyval_w[shard // 2 :, :dim]
        first[rest + shard // 2 :] = keyval_w[:, dim:]

    wide[...] = jnp.zeros_like(wide)
    for index, small in enumerate(smalls):
        row = small[...].astype(f32).reshape(1, shard)
        wide[index : index + 1, :] = jnp.concatenate([row] * n_fs, axis=1)
    lane = lax.broadcasted_iota(jnp.int32, wide.shape, 1)
    row = lax.broadcasted_iota(jnp.int32, wide.shape, 0)
    vectors = jnp.where(lane // shard == fs, wide[...], 0.0)
    hidden_row = hidden_b[...].astype(f32).reshape(1, dim)
    first[half:rest] = jnp.where(row == HIDDEN_B + fs, hidden_row, vectors).astype(bf16)


def both_halves(mine, other):
    is_low = lax.axis_index("sp") % 2 == 0
    a, b = mine[...], other[...]
    return jnp.where(is_low, a, b), jnp.where(is_low, b, a)


def shard_rows(place, rows):
    return pl.ds(pl.multiple_of(place * rows, rows), rows)


def begin_kernel(dims, sizes, tokens, reduce_w, query_w, keyval_w, hidden_w, return_w, output_w, packed, *outs):
    n_sp, batches, row_dev, cols, dim = dims
    normal_ref, rstd_ref, mask_ref, bias_ref, own_r, own_q, own_kv, own_vec, second = outs
    tok = row_dev * cols
    half_cols = cols // 2
    rows_dev = row_dev // 2
    half = dim // 2
    shard = hidden_w.shape[0]
    sp = lax.axis_index("sp")
    own_r[...] = reduce_w[...]
    own_q[...] = query_w[...]
    own_kv[...] = keyval_w[...]
    own_vec[...] = packed[half : half + VECS].astype(f32)

    @pl.when(sp % 2 == 0)
    def _():
        for chunk in range(hidden_w.shape[1] // dim):
            second[chunk * shard : (chunk + 1) * shard] = hidden_w[:, chunk * dim : (chunk + 1) * dim]
        second[dim:] = output_w[: shard // 2]

    @pl.when(sp % 2 == 1)
    def _():
        second[:dim] = return_w[...]
        second[dim:] = output_w[shard // 2 :]

    for batch in range(batches):
        height, image_width = sizes[batch, 0, 0], sizes[batch, 0, 1]
        rows = slice(batch * tok, (batch + 1) * tok)
        normal, rstd = normalize(tokens[batch, 0].reshape(tok, dim).astype(f32))
        normal_ref[rows] = normal
        rstd_ref[rows] = jnp.broadcast_to(rstd, (tok, 128))
        mask_ref[rows] = token_mask(sp * row_dev, row_dev, cols, dim, height, image_width)
        col_ids = lax.broadcasted_iota(jnp.int32, (half_cols, dim), 0)

        def key_row_bias(index, _, batch=batch, height=height, image_width=image_width, col_ids=col_ids):
            key_row = index
            if n_sp == 8:
                key_row = (sp ^ (index // rows_dev)) * rows_dev + lax.rem(index, rows_dev)
            width = jnp.where(2 * key_row < height, image_width, 0)
            here = pl.ds(pl.multiple_of(index * half_cols, half_cols), half_cols)
            bias_ref[batch, here, :] = jnp.where(2 * col_ids < width, 0.0, NEG).astype(bf16)
            return 0

        lax.fori_loop(0, n_sp * rows_dev, key_row_bias, 0)


def reduce_kernel(dims, *refs):
    n_fs, batches, row_dev, cols, dim = dims
    ins, mine, other, outs = take(refs, 6, n_fs - 1, n_fs - 1)
    normal_in, mask_ref, own_w, own_q, own_kv, own_vec = ins
    normed_ref, cols_ref, send_ref, reduced_ref, key_ref, weight_ref, wq, wkv, vec_ref, patch_ref, wide = outs
    half = dim // 2
    shard = dim // n_fs
    rest = half + VECS
    tok = row_dev * cols
    half_cols = cols // 2
    key_dev = tok // 4
    fs = lax.axis_index("fs")
    weight_ref[fs] = own_w[...]
    here = shard_rows(fs, shard)
    wq[here, :] = own_q[...]
    wkv[here, :] = own_kv[...]
    vec = own_vec[...]
    for step in range(1, n_fs):
        low, high = both_halves(mine[step - 1], other[step - 1])
        place = lax.rem(fs + n_fs - step, n_fs)
        weight_ref[place, :half] = low[:half]
        weight_ref[place, half:] = high[:half]
        vec = vec + low[half:rest].astype(f32)
        here = shard_rows(place, shard)
        wq[here, :] = low[rest : rest + shard]
        wkv[here, :dim] = jnp.concatenate([low[rest + shard :], high[rest : rest + shard // 2]], axis=0)
        wkv[here, dim:] = high[rest + shard // 2 :]
    vec_ref[...] = vec
    for batch in range(batches):
        rows = slice(batch * tok, (batch + 1) * tok)
        low = (normal_in[rows] * vec[FIRST_G : FIRST_G + 1] + vec[FIRST_B : FIRST_B + 1]).astype(bf16)
        normed_ref[rows] = low
        masked = low.astype(f32) * mask_ref[rows]
        for part in range(dim // 128):
            wide[part, :tok] = masked[:, part * 128 : (part + 1) * 128]
        for row in range(row_dev // 2):
            start = batch * key_dev + row * half_cols
            for offset in range(4):
                dr, dc = offset // 2, offset % 2
                for part in range(dim // 128):
                    piece = wide[part, pl.ds((2 * row + dr) * cols + dc, half_cols, stride=2), :]
                    lanes = slice(offset * dim + part * 128, offset * dim + (part + 1) * 128)
                    patch_ref[start : start + half_cols, lanes] = piece.astype(bf16)
    is_low = lax.axis_index("sp") % 2 == 0
    for offset in range(4):
        low = patch_ref[:, offset * dim : offset * dim + half]
        high = patch_ref[:, offset * dim + half : (offset + 1) * dim]
        cols_ref[offset] = jnp.where(is_low, low, high)
        send_ref[offset] = jnp.where(is_low, high, low)
    reduced = mm(patch_ref[...], weight_ref[...].reshape(4 * dim, dim)) + vec[REDUCE_B : REDUCE_B + 1]
    reduced_ref[...] = reduced
    normal, _ = normalize(reduced)
    key_ref[...] = (normal * vec[KEYS_G : KEYS_G + 1] + vec[KEYS_B : KEYS_B + 1]).astype(bf16)


def relay_kernel(n, *refs):
    for source, target in zip(refs[:n], refs[n + 1 :]):
        target[...] = source[...]


def head_stack_t(values_t, pair, tok):
    both = jnp.concatenate([values_t, values_t], axis=1)
    head = lax.broadcasted_iota(jnp.int32, both.shape, 0) // HDIM
    want = 2 * pair + jnp.where(lax.broadcasted_iota(jnp.int32, both.shape, 1) >= tok, 1, 0)
    return jnp.where(head == want, both, jnp.zeros_like(both))


def head_stack(values, pair):
    head = lax.broadcasted_iota(jnp.int32, values.shape, 1) // HDIM
    zero = jnp.zeros_like(values)
    return jnp.concatenate(
        [jnp.where(head == 2 * pair, values, zero), jnp.where(head == 2 * pair + 1, values, zero)],
        axis=0,
    )


def split_pair(both, tok):
    return jnp.concatenate([both[:HDIM, :tok], both[HDIM:, tok:]], axis=0)


def key_rows_of(pieces, key_dev, per_block, batch, index):
    here = slice(batch * key_dev, (batch + 1) * key_dev)
    if len(pieces) > 1:
        return jnp.concatenate([part[here] for part in pieces], axis=0)
    dim = pieces[0].shape[2]
    devices = slice(index * per_block, (index + 1) * per_block)
    return pieces[0][devices, here, :].reshape(per_block * key_dev, dim)


def mask_lane(pair, dim):
    return 0 if pair == PAIRS - 1 else dim - 1


def with_bias(key_block, bias, lane_id):
    lane = lax.broadcasted_iota(jnp.int32, key_block.shape, 1)
    return jnp.where(lane == lane_id, bias.astype(f32), key_block.astype(f32)).astype(bf16)


def query_stack(queries_t, pair, lane_id, tok):
    stacked = head_stack_t(queries_t, pair, tok)
    row = lax.broadcasted_iota(jnp.int32, stacked.shape, 0)
    return jnp.where(row == lane_id, jnp.ones_like(stacked), stacked)


def take(refs, *counts):
    refs = list(refs)
    groups = []
    for count in counts:
        groups.append(refs[:count])
        refs = refs[count:]
    return groups + [refs]


def forward_kernel(dims, *refs):
    batch, tok, key_dev, keys, block, n_pieces = dims
    (normed, vec_ref, bias_ref, wq, wkv), pieces, outs = take(refs, 5, n_pieces)
    attended, queries_out, kvs, attf, stats, probs, wide = outs
    dim = wq.shape[0]
    blocks = keys // block
    per_block = block // key_dev
    queries = (mm(normed[batch * tok : (batch + 1) * tok], wq[...]) + vec_ref[QUERY_B : QUERY_B + 1]).astype(bf16)
    queries_out[...] = queries
    queries_t = queries.T
    for index in range(blocks):
        key_rows = key_rows_of(pieces, key_dev, per_block, batch, index)
        here = slice(index * block, (index + 1) * block)
        kvs[here, :dim] = mm(key_rows, wkv[:, :dim]).astype(bf16)
        value_rows = mm(key_rows, wkv[:, dim:]) + vec_ref[VALUE_B : VALUE_B + 1]
        kvs[here, dim:] = value_rows.astype(bf16)
    if blocks == 1:
        key_block = kvs[:, :dim]
        values_t = kvs[:, dim:].T
        masked = {lane_id: with_bias(key_block, bias_ref[batch], lane_id) for lane_id in (0, dim - 1)}

        def score(pair):
            lane_id = mask_lane(pair, dim)
            wide[pair % 2] = mm(masked[lane_id], query_stack(queries_t, pair, lane_id, tok))

        score(0)
        for pair in range(PAIRS):
            if pair + 1 < PAIRS:
                score(pair + 1)
            heads = slice(2 * HDIM * pair, 2 * HDIM * (pair + 1))
            scores = wide[pair % 2]
            top = jnp.max(scores, axis=0, keepdims=True)
            weights = jnp.exp2((scores - top) * EXP_SCALE)
            inverse = 1.0 / jnp.sum(weights, axis=0, keepdims=True)
            low = weights.astype(bf16)
            probs[pair] = low
            stats[pair, 0:1] = inverse
            mixed = mm(values_t[heads], low) * inverse
            attf[heads] = split_pair(mixed, tok)
    else:
        for pair in range(PAIRS):
            lane_id = mask_lane(pair, dim)
            heads = slice(2 * HDIM * pair, 2 * HDIM * (pair + 1))
            stacked = query_stack(queries_t, pair, lane_id, tok)

            def block_scores(index, stacked=stacked, lane_id=lane_id):
                here = pl.ds(pl.multiple_of(index * block, block), block)
                masked = with_bias(kvs[here, :dim], bias_ref[batch, here, :], lane_id)
                return here, mm(masked, stacked)

            def find_top(index, top, block_scores=block_scores):
                _, scores = block_scores(index)
                return jnp.maximum(top, jnp.max(scores, axis=0, keepdims=True))

            top = lax.fori_loop(0, blocks, find_top, jnp.full((1, 2 * tok), 4 * NEG, f32))

            def add_block(index, carry, block_scores=block_scores, top=top, heads=heads):
                total, mixed = carry
                here, scores = block_scores(index)
                weights = jnp.exp2((scores - top) * EXP_SCALE)
                values_t = kvs[here, dim:].T
                mixed = mixed + mm(values_t[heads], weights.astype(bf16))
                return total + jnp.sum(weights, axis=0, keepdims=True), mixed

            start = (jnp.zeros((1, 2 * tok), f32), jnp.zeros((2 * HDIM, 2 * tok), f32))
            total, mixed = lax.fori_loop(0, blocks, add_block, start)
            inverse = 1.0 / total
            stats[pair, 0:1] = inverse
            stats[pair, 1:2] = top
            attf[heads] = split_pair(mixed * inverse, tok)
    attended[...] = attf[...].T.astype(bf16)


def mlp_kernel(dims, *refs):
    n_fs, batches, row_dev, cols, dim, hid = dims
    ins, attended, own, mine, other, _, outs, scratch = take(refs, 4, batches, 3, n_fs - 1, n_fs - 1, 1, 6)
    tokens, cotangent, mask_ref, vec_ref = ins
    acts_ref, middle_ref, gatt, keep_ref, send_ref, gvec_ref = outs
    wh, wr, wo, lows, highs = scratch
    tok = row_dev * cols
    shard = dim // n_fs
    chunks = hid // dim
    fs = lax.axis_index("fs")
    is_low = lax.axis_index("sp") % 2 == 0
    wh[shard_rows(fs, shard), :] = own[0][...]
    wr[shard_rows(fs, dim), :] = own[1][...]
    wo[shard_rows(fs, shard), :] = own[2][...]
    for step in range(1, n_fs):
        low, high = both_halves(mine[step - 1], other[step - 1])
        place = fs ^ step
        here = shard_rows(place, shard)
        for chunk in range(chunks):
            wh[here, chunk * dim : (chunk + 1) * dim] = low[chunk * shard : (chunk + 1) * shard]
        wr[shard_rows(place, dim), :] = high[:dim]
        wo[here, :] = jnp.concatenate([low[dim:], high[dim:]], axis=0)

    def vec(index):
        return vec_ref[index : index + 1, :]

    x = jnp.concatenate([tokens[b, 0].reshape(tok, dim).astype(f32) for b in range(batches)], axis=0)
    mask = mask_ref[...]
    attended = jnp.concatenate([part[...] for part in attended], axis=0)
    middle = x + mm(attended, wo[...]) + vec(OUTPUT_B)
    normal, rstd = normalize(middle)
    second = (normal * vec(SECOND_G) + vec(SECOND_B)).astype(bf16)
    grad_out = jnp.concatenate([cotangent[b, 0].reshape(tok, dim) for b in range(batches)], axis=0) * mask
    grad_mlp = grad_out.astype(bf16)
    second_t, grad_mlp_t = second.T, grad_mlp.T
    total = middle + vec(RETURN_B)
    grad_second = jnp.zeros((batches * tok, dim), f32)
    gvec_ref[...] = jnp.zeros_like(gvec_ref)
    for chunk in range(chunks):
        lanes = slice(chunk * dim, (chunk + 1) * dim)
        hidden = mm(second, wh[:, lanes]) + vec(HIDDEN_B + chunk)
        phi = 0.5 + 0.5 * lax.erf(hidden * 0.7071067811865476)
        density = 0.3989422804014327 * jnp.exp2(hidden * hidden * (-0.5 * 1.4426950408889634))
        activated = (hidden * phi).astype(bf16)
        total = total + mm(activated, wr[lanes, :])
        grad_activated = mm_nt(grad_mlp, wr[lanes, :])
        grad_hidden = ((phi + hidden * density) * grad_activated).astype(bf16)
        gvec_ref[HIDDEN_B + chunk : HIDDEN_B + chunk + 1] = jnp.sum(
            grad_hidden.astype(f32), axis=0, keepdims=True
        )
        grad_second = grad_second + mm_nt(grad_hidden, wh[:, lanes])
        highs[chunk] = mm(grad_mlp_t, activated).T.astype(bf16)
        grad_wh = mm(second_t, grad_hidden).astype(bf16)
        for owner in range(n_fs):
            lows[owner, chunk * shard : (chunk + 1) * shard] = grad_wh[owner * shard : (owner + 1) * shard]
    low, high = lows[...], highs[...]
    keep_ref[...] = jnp.where(is_low, low, high)
    send_ref[...] = jnp.where(is_low, high, low)
    total = total * mask
    for batch in range(batches):
        acts_ref[batch, 0] = total[batch * tok : (batch + 1) * tok].reshape(row_dev, cols, dim)
    grad_middle = grad_out + normalize_back(grad_second, normal, rstd, vec(SECOND_G))
    middle_ref[...] = grad_middle
    grad_branch = grad_middle.astype(bf16)
    gatt[...] = mm_nt(grad_branch, wo[...]).astype(bf16)
    for index, value in (
        (OUTPUT_B, grad_branch.astype(f32)),
        (SECOND_G, grad_second * normal),
        (SECOND_B, grad_second),
        (RETURN_B, grad_mlp.astype(f32)),
    ):
        gvec_ref[index : index + 1] = jnp.sum(value, axis=0, keepdims=True)


def backward_kernel(dims, *refs):
    n_sp, batch, tok, key_dev, keys, block, n_pieces = dims
    gatt, queries_ref, kvs, attf, stats, probs, bias_ref, wkv, _ = refs[:9]
    near_ref, far_ref, scores_ref, gks, gvs, gvec_ref = refs[9:15]
    dim = wkv.shape[0]
    blocks = keys // block
    per_block = block // key_dev
    rows = slice(batch * tok, (batch + 1) * tok)
    queries = queries_ref[...]
    grad_att_t = gatt[rows].astype(f32).T
    product = grad_att_t * attf[...]

    def pair_terms(pair):
        inverse = stats[pair, 0:1]
        piece = product[2 * HDIM * pair : 2 * HDIM * (pair + 1)]
        delta = jnp.concatenate(
            [jnp.sum(piece[:HDIM], axis=0, keepdims=True), jnp.sum(piece[HDIM:], axis=0, keepdims=True)],
            axis=1,
        )
        stacked = head_stack_t(grad_att_t, pair, tok) * inverse
        return delta * inverse, stacked.astype(bf16)

    if blocks == 1:
        (wide,) = refs[15:]
        values = kvs[:, dim:]
        grad_k = jnp.zeros((keys, dim), f32)
        grad_v = jnp.zeros((keys, dim), f32)
        terms = []

        def grad_prob(pair):
            delta, stacked = pair_terms(pair)
            wide[pair % 2] = mm(values, stacked)
            terms.append((delta, stacked))

        grad_prob(0)
        for pair in range(PAIRS):
            if pair + 1 < PAIRS:
                grad_prob(pair + 1)
            delta, stacked = terms[pair]
            low = probs[pair]
            grad_scores = (low.astype(f32) * (wide[pair % 2] - delta)).astype(bf16)
            scores_ref[pair] = grad_scores
            grad_k = grad_k + mm(grad_scores, head_stack(queries, pair))
            grad_v = grad_v + mm(low, stacked.T)
    else:
        wide_k, wide_v = refs[15:]
        wide_k[...] = jnp.zeros_like(wide_k)
        wide_v[...] = jnp.zeros_like(wide_v)
        queries_t = queries.T
        for pair in range(PAIRS):
            heads = slice(2 * HDIM * pair, 2 * HDIM * (pair + 1))
            lane_id = mask_lane(pair, dim)
            delta, stacked = pair_terms(pair)
            stacked_n = stacked.T
            query_t = query_stack(queries_t, pair, lane_id, tok)
            query_n = head_stack(queries, pair)
            top = stats[pair, 1:2]

            def back_block(index, gq, heads=heads, lane_id=lane_id, delta=delta, stacked=stacked, stacked_n=stacked_n, query_t=query_t, query_n=query_n, top=top):
                here = pl.ds(pl.multiple_of(index * block, block), block)
                key_block = kvs[here, :dim]
                masked = with_bias(key_block, bias_ref[batch, here, :], lane_id)
                weights = jnp.exp2((mm(masked, query_t) - top) * EXP_SCALE)
                grad_probs = mm(kvs[here, dim:], stacked)
                grad_scores = (weights * (grad_probs - delta)).astype(bf16)
                wide_k[here, :] += mm(grad_scores, query_n)
                wide_v[here, :] += mm(weights.astype(bf16), stacked_n)
                return gq + mm(key_block.T[heads], grad_scores)

            gq = lax.fori_loop(0, blocks, back_block, jnp.zeros((2 * HDIM, 2 * tok), f32))
            scores_ref[heads] = split_pair(gq, tok)
    bias_value = jnp.zeros((1, dim), f32)
    for index in range(blocks):
        here = slice(index * block, (index + 1) * block)
        if blocks > 1:
            grad_k, grad_v = wide_k[here], wide_v[here]
        grad_k = (grad_k * SCALE).astype(bf16)
        bias_value = bias_value + jnp.sum(grad_v, axis=0, keepdims=True)
        grad_v = grad_v.astype(bf16)
        gks[here] = grad_k
        gvs[here] = grad_v
        grad_key = (mm_nt(grad_k, wkv[:, :dim]) + mm_nt(grad_v, wkv[:, dim:])).astype(bf16)
        if n_pieces > 1:
            pairs = grad_key.reshape(n_sp // 2, 2, key_dev, dim)
            near_ref[...] = pairs[:, 0]
            far_ref[...] = pairs[:, 1]
        else:
            near_ref[index * per_block : (index + 1) * per_block] = grad_key.reshape(per_block, key_dev, dim)
    gvec_ref[...] = jnp.broadcast_to(bias_value, gvec_ref.shape)


def query_kernel(dims, *refs):
    n_fs, batches, tok, key_dev, keys, block, n_pieces = dims
    ins, attended, kvs, scores, gks, gvs, gvecs, pieces, outs = take(refs, 3, *([batches] * 6), n_pieces)
    normed, wq, middle = ins
    keep_ref, send_ref, gnormed_ref, gvec_ref, wide = outs
    dim = wq.shape[0]
    shard = dim // n_fs
    blocks = keys // block
    per_block = block // key_dev
    grad_queries = []
    grad_wk = jnp.zeros((dim, dim), f32)
    grad_wv = jnp.zeros((dim, dim), f32)
    for batch in range(batches):
        if blocks == 1:
            keys_t = kvs[batch][:, :dim].T
            for pair in range(PAIRS):
                heads = slice(2 * HDIM * pair, 2 * HDIM * (pair + 1))
                wide[heads] = split_pair(mm(keys_t[heads], scores[batch][pair]), tok)
            grad_t = wide[...]
        else:
            grad_t = scores[batch][...]
        grad_queries.append((grad_t.T * SCALE).astype(bf16))
        for index in range(blocks):
            here = slice(index * block, (index + 1) * block)
            key_rows = key_rows_of(pieces, key_dev, per_block, batch, index)
            grad_wk = grad_wk + mm_tn(key_rows, gks[batch][here])
            grad_wv = grad_wv + mm_tn(key_rows, gvs[batch][here])
    grad_queries = jnp.concatenate(grad_queries, axis=0)
    grad_wq = mm_tn(normed[...], grad_queries)
    attended = jnp.concatenate([part[...] for part in attended], axis=0)
    grad_wo = mm_tn(attended, middle[...].astype(bf16))
    is_low = lax.axis_index("sp") % 2 == 0
    for owner in range(n_fs):
        part = slice(owner * shard, (owner + 1) * shard)
        low = jnp.concatenate([grad_wq[part], grad_wk[part]], axis=0).astype(bf16)
        high = jnp.concatenate([grad_wv[part], grad_wo[part]], axis=0).astype(bf16)
        keep_ref[owner] = jnp.where(is_low, low, high)
        send_ref[owner] = jnp.where(is_low, high, low)
    gnormed_ref[...] = mm_nt(grad_queries, wq[...])
    gvec_ref[...] = jnp.zeros_like(gvec_ref)
    gvec_ref[QUERY_B : QUERY_B + 1] = jnp.sum(grad_queries.astype(f32), axis=0, keepdims=True)
    bias_value = gvecs[0][0:1]
    for gvec in gvecs[1:]:
        bias_value = bias_value + gvec[0:1]
    gvec_ref[VALUE_B : VALUE_B + 1] = bias_value


def sum_parts(parts):
    if len(parts) == 1:
        total = parts[0][0].astype(f32)
        for index in range(1, parts[0].shape[0]):
            total = total + parts[0][index].astype(f32)
        return total
    total = parts[0][...].astype(f32)
    for part in parts[1:]:
        total = total + part[...].astype(f32)
    return total


def reduction_kernel(n_parts, batches, reduced, vec_ref, *refs):
    parts, gvec_ref, outs = refs[:n_parts], refs[-1], refs[-1 - batches : -1]
    grad_key = sum_parts(parts)
    normal, rstd = normalize(reduced[...])
    grad_low = normalize_back(grad_key, normal, rstd, vec_ref[KEYS_G : KEYS_G + 1]).astype(bf16)
    rows = outs[0].shape[0]
    for batch, out in enumerate(outs):
        out[...] = grad_low[batch * rows : (batch + 1) * rows]
    gvec_ref[...] = jnp.zeros_like(gvec_ref)
    for index, value in (
        (REDUCE_B, grad_low.astype(f32)),
        (KEYS_G, grad_key * normal),
        (KEYS_B, grad_key),
    ):
        gvec_ref[index : index + 1] = jnp.sum(value, axis=0, keepdims=True)


def weight_kernel(batches, *refs):
    (own_cols, other_cols), own, other, (vectors, *outs) = take(refs, 2, batches, batches)
    fs = lax.axis_index("fs")
    own = jnp.concatenate([part[...] for part in own], axis=0)
    other = jnp.concatenate([part[...] for part in other], axis=0)
    rows = own_cols.shape[2]
    for step, out in enumerate(outs):
        place = lax.rem(fs + step, len(outs))
        out[:rows] = (mm_tn(own_cols[place], own) + mm_tn(other_cols[place], other)).astype(out.dtype)
        out[rows:] = vectors[...]


def normed_kernel(dims, gnormed, mask_ref, weight, normal_ref, vec_a, vec_b, vec_c, *refs):
    batches, row_dev, cols, dim = dims
    grads, (grad_ref, gvec_ref, wide) = take(refs, batches)
    tok = row_dev * cols
    half_cols = cols // 2
    gain_first = jnp.zeros((1, dim), f32)
    bias_first = jnp.zeros((1, dim), f32)
    for batch in range(batches):
        for offset in range(4):
            dr, dc = offset // 2, offset % 2
            back = mm_nt(grads[batch][...], weight[offset])
            for row in range(row_dev // 2):
                for part in range(dim // 128):
                    wide[part, pl.ds((2 * row + dr) * cols + dc, half_cols, stride=2), :] = back[
                        row * half_cols : (row + 1) * half_cols, part * 128 : (part + 1) * 128
                    ]
        rows = slice(batch * tok, (batch + 1) * tok)
        spread = jnp.concatenate([wide[part, :tok] for part in range(dim // 128)], axis=1)
        grad_normed = gnormed[rows] + spread * mask_ref[rows]
        grad_ref[rows] = grad_normed
        gain_first = gain_first + jnp.sum(grad_normed * normal_ref[rows], axis=0, keepdims=True)
        bias_first = bias_first + jnp.sum(grad_normed, axis=0, keepdims=True)
    index = lax.broadcasted_iota(jnp.int32, (VECS, dim), 0)
    vectors = vec_a[...] + vec_b[...] + vec_c[...]
    vectors = jnp.where(index == FIRST_G, gain_first, vectors)
    vectors = jnp.where(index == FIRST_B, bias_first, vectors)
    gvec_ref[...] = vectors.astype(bf16)


def input_kernel(dims, middle, grad_normed, normal_ref, rstd_ref, vec_ref, _, grad_ref, done_ref):
    batches, row_dev, cols, dim = dims
    tok = row_dev * cols
    rstd = jnp.concatenate([rstd_ref[...]] * (dim // rstd_ref.shape[1]), axis=1)
    back = normalize_back(grad_normed[...], normal_ref[...], rstd, vec_ref[FIRST_G : FIRST_G + 1])
    grad_x = middle[...] + back
    for batch in range(batches):
        grad_ref[batch, 0] = grad_x[batch * tok : (batch + 1) * tok].reshape(row_dev, cols, dim)
    done_ref[...] = jnp.zeros_like(done_ref)


def key_sum_kernel(batches, *refs):
    near, far, _, outs = take(refs, batches, batches, 2)
    for step, out in enumerate(outs):
        rows = near[0].shape[1]
        for batch in range(batches):
            total = near[batch][step].astype(f32) + far[batch][step].astype(f32)
            out[batch * rows : (batch + 1) * rows] = total.astype(out.dtype)


def owner_kernel(keep, arrived, *outs):
    fs = lax.axis_index("fs")
    for step, out in enumerate(outs):
        place = lax.rem(fs + step, len(outs))
        out[...] = (keep[place].astype(f32) + arrived[place].astype(f32)).astype(out.dtype)


def chip_kernel(keep, arrived, _, *outs):
    chip = lax.axis_index("sp") // 2
    rows = outs[0].shape[1]
    for step, out in enumerate(outs):
        here = shard_rows(chip ^ step, rows)
        out[...] = (keep[:, here, :].astype(f32) + arrived[:, here, :].astype(f32)).astype(out.dtype)


def chip_sum_kernel(*refs):
    refs[-1][...] = sum_parts(refs[:-1]).astype(refs[-1].dtype)


def owners_kernel(total, keep, arrived, *outs):
    fs = lax.axis_index("fs")
    rows = total.shape[1]
    for step, out in enumerate(outs):
        place = lax.rem(fs + step, len(outs))
        out[:rows] = total[place]
        out[rows:] = (keep[place].astype(f32) + arrived[place].astype(f32)).astype(out.dtype)


def join_kernel(n, *refs):
    refs[-1][...] = sum_parts(refs[:n]).astype(refs[-1].dtype)


def merge_kernel(rows, *refs):
    parts, out = refs[:4], refs[5]
    chip = lax.axis_index("sp") // 2
    if rows:
        for step, part in enumerate(parts):
            out[shard_rows(chip ^ step, rows), :] = part[:rows]
    rest = [part[rows:].astype(f32) for part in parts]
    out[4 * rows :] = ((rest[0] + rest[1]) + (rest[2] + rest[3])).astype(out.dtype)


def final_kernel(n_fs, mine, other, mine_b, other_b, *outs):
    query_w, keyval_w, output_w, hidden_w, return_w, reduce_w = outs[:6]
    smalls, hidden_b = outs[6:-1], outs[-1]
    shard, dim = query_w.shape
    half = dim // 2
    fs = lax.axis_index("fs")
    low, high = both_halves(mine, other)
    low, high = low.astype(f32), high.astype(f32)
    for chunk in range(hidden_w.shape[1] // dim):
        hidden_w[:, chunk * dim : (chunk + 1) * dim] = low[chunk * shard : (chunk + 1) * shard]
    return_w[...] = high[:dim]
    low, high = low[dim:], high[dim:]
    query_w[...] = low[:shard]
    keyval_w[:, :dim] = low[shard : 2 * shard]
    keyval_w[:, dim:] = high[:shard]
    output_w[...] = high[shard : 2 * shard]
    low, high = both_halves(mine_b, other_b)
    low, high = low.astype(f32), high.astype(f32)
    reduce_w[:half] = low[:half]
    reduce_w[half:] = high[:half]
    vecs = low[half:] + high[half:]
    lane = lax.broadcasted_iota(jnp.int32, vecs.shape, 1)
    chosen = jnp.where(lane // shard == fs, vecs, 0.0)
    folded = chosen[:, :shard]
    for index in range(1, n_fs):
        folded = folded + chosen[:, index * shard : (index + 1) * shard]
    for index, small in enumerate(smalls):
        small[...] = folded[index : index + 1].reshape(shard)
    row = lax.broadcasted_iota(jnp.int32, vecs.shape, 0)
    hidden_b[...] = jnp.sum(jnp.where(row == HIDDEN_B + fs, vecs, 0.0), axis=0)


def rotate(value, n, step):
    return lax.ppermute(value, "fs", [(i, (i + step) % n) for i in range(n)])


def swap(value, n, bits):
    return lax.ppermute(value, "fs", [(i, i ^ bits) for i in range(n)])


def flip(value, n, bits):
    return lax.ppermute(value, "sp", [(i, i ^ bits) for i in range(n)])


def sum_over_rows(value, n_sp):
    bit = 2
    while bit < n_sp:
        if 2 * bit < n_sp:
            a, b, c = flip(value, n_sp, bit), flip(value, n_sp, 2 * bit), flip(value, n_sp, 3 * bit)
            value = (
                (value.astype(f32) + a.astype(f32)) + (b.astype(f32) + c.astype(f32))
            ).astype(value.dtype)
            bit = 4 * bit
        else:
            a = flip(value, n_sp, bit)
            value = (value.astype(f32) + a.astype(f32)).astype(value.dtype)
            bit = 2 * bit
    return value


def exchange(pieces, n_sp):
    return [pieces[0]] + [flip(pieces[step], n_sp, 2 * step) for step in range(1, n_sp // 2)]


def to_owners(pieces, n_fs):
    return [pieces[0]] + [rotate(pieces[step], n_fs, step) for step in range(1, n_fs)]


def call(kernel, out_shape, in_specs=None, scratch=(), limit=SMALL_VMEM, micros=0):
    specs = {} if in_specs is None else {"in_specs": in_specs}
    return pl.pallas_call(
        kernel,
        out_shape=out_shape,
        **specs,
        scratch_shapes=scratch,
        compiler_params=pltpu.CompilerParams(vmem_limit_bytes=limit),
        cost_estimate=pl.CostEstimate(flops=int(micros * 1e9), bytes_accessed=0, transcendentals=0),
    )


def on_device(
    n_fs,
    n_sp,
    tokens,
    cotangent,
    image_sizes,
    first_gain,
    first_bias,
    query_weight,
    query_bias,
    reduce_weight,
    reduce_bias,
    keys_gain,
    keys_bias,
    keyval_weight,
    value_bias,
    output_weight,
    output_bias,
    second_gain,
    second_bias,
    hidden_weight,
    hidden_bias,
    return_weight,
    return_bias,
):
    batches, _, row_dev, cols, dim = tokens.shape
    hid = hidden_weight.shape[1]
    tok = row_dev * cols
    key_dev = tok // 4
    keys = n_sp * key_dev
    shard = dim // n_fs
    half = dim // 2
    vmem = pl.BlockSpec(memory_space=pltpu.VMEM)
    smem = pl.BlockSpec(memory_space=pltpu.SMEM)
    single = keys <= KEY_BLOCK
    split = n_sp == 8
    block = keys if single else KEY_BLOCK
    limit = MAIN_VMEM if single else WHOLE_VMEM

    def shape(*dims, dtype=bf16):
        return jax.ShapeDtypeStruct(dims, dtype)

    smalls = (
        first_gain,
        first_bias,
        query_bias,
        reduce_bias,
        keys_gain,
        keys_bias,
        value_bias,
        output_bias,
        second_gain,
        second_bias,
        return_bias,
    )
    first_half = call(
        functools.partial(pack_first_kernel, n_fs),
        shape(half + VECS + 3 * shard // 2, dim),
        scratch=[pltpu.VMEM((VECS, dim), f32)],
        limit=WHOLE_VMEM,
    )(*smalls, hidden_bias, reduce_weight, query_weight, keyval_weight)
    mine_first = to_owners([first_half] * n_fs, n_fs)[1:]

    begun = call(
        functools.partial(begin_kernel, (n_sp, batches, row_dev, cols, dim)),
        [
            shape(batches * tok, dim, dtype=f32),
            shape(batches * tok, 128, dtype=f32),
            shape(batches * tok, dim, dtype=f32),
            shape(batches, keys, dim),
            shape(dim, dim),
            shape(shard, dim),
            shape(shard, 2 * dim),
            shape(VECS, dim, dtype=f32),
            shape(dim + shard // 2, dim),
        ],
        in_specs=[smem] + [vmem] * 8,
        limit=SMALL_VMEM if single else WHOLE_VMEM,
    )(
        image_sizes,
        tokens,
        reduce_weight,
        query_weight,
        keyval_weight,
        hidden_weight,
        return_weight,
        output_weight,
        first_half,
    )
    normal_first, rstd_first, mask, bias, own_r, own_q, own_kv, own_vec, second_half = begun
    mine_first = call(functools.partial(relay_kernel, n_fs - 1), [shape(*first_half.shape)] * (n_fs - 1))(
        *mine_first, own_vec
    )
    other_first = [flip(piece, n_sp, 1) for piece in mine_first]
    normed, patch_cols, patch_send, reduced, key_low, whole_reduce, wq, wkv, vec = call(
        functools.partial(reduce_kernel, (n_fs, batches, row_dev, cols, dim)),
        [
            shape(batches * tok, dim),
            shape(4, batches * key_dev, half),
            shape(4, batches * key_dev, half),
            shape(batches * key_dev, dim, dtype=f32),
            shape(batches * key_dev, dim),
            shape(n_fs, dim, dim),
            shape(dim, dim),
            shape(dim, 2 * dim),
            shape(VECS, dim, dtype=f32),
        ],
        scratch=[pltpu.VMEM((batches * key_dev, 4 * dim), bf16), pltpu.VMEM((dim // 128, tok + 8, 128), f32)],
    )(normal_first, mask, own_r, own_q, own_kv, own_vec, *mine_first, *other_first)
    across = swap(second_half, n_fs, 2)
    passed = call(functools.partial(relay_kernel, 1), [shape(dim + shard // 2, dim)], micros=15)(across, own_vec)
    mine_second = [swap(second_half, n_fs, 1), across, swap(passed[0], n_fs, 1)]

    if split:
        same = exchange([key_low] * (n_sp // 2), n_sp)
        key_pieces = [piece for part in same for piece in (part, flip(part, n_sp, 1))]
    else:
        key_pieces = [lax.all_gather(key_low, "sp")]
    n_pieces = len(key_pieces)

    kept = [
        call(
            functools.partial(forward_kernel, (batch, tok, key_dev, keys, block, n_pieces)),
            [
                shape(tok, dim),
                shape(tok, dim),
                shape(keys, 2 * dim),
                shape(dim, tok, dtype=f32),
                shape(PAIRS, 8, 2 * tok, dtype=f32),
                shape(PAIRS, keys, 2 * tok) if single else shape(16, 128),
            ],
            scratch=[pltpu.VMEM((2, block, 2 * tok) if single else (8, 128), f32)],
            limit=limit,
        )(normed, vec, bias, wq, wkv, *key_pieces)
        for batch in range(batches)
    ]
    attended = [results[0] for results in kept]
    kept = [results[1:] for results in kept]
    mine_second = call(functools.partial(relay_kernel, n_fs - 1), [shape(dim + shard // 2, dim)] * (n_fs - 1))(
        *mine_second, kept[0][3]
    )
    patch_other = flip(patch_send, n_sp, 1)
    other_second = [flip(piece, n_sp, 1) for piece in mine_second]

    acts, middle, gatt, keep_a, send_a, gvec_a = call(
        functools.partial(mlp_kernel, (n_fs, batches, row_dev, cols, dim, hid)),
        [
            shape(batches, 1, row_dev, cols, dim, dtype=f32),
            shape(batches * tok, dim, dtype=f32),
            shape(batches * tok, dim),
            shape(n_fs, dim, dim),
            shape(n_fs, dim, dim),
            shape(VECS, dim, dtype=f32),
        ],
        scratch=[
            pltpu.VMEM((dim, hid), bf16),
            pltpu.VMEM((hid, dim), bf16),
            pltpu.VMEM((dim, dim), bf16),
            pltpu.VMEM((n_fs, dim, dim), bf16),
            pltpu.VMEM((n_fs, dim, dim), bf16),
        ],
        limit=limit,
    )(
        tokens,
        cotangent,
        mask,
        vec,
        *attended,
        hidden_weight,
        return_weight,
        output_weight,
        *mine_second,
        *other_second,
        patch_other,
    )
    arrived_a = flip(send_a, n_sp, 1)
    gkey_dims = (n_sp // 2, key_dev, dim) if split else (n_sp, key_dev, dim)
    back = []
    for batch in range(batches):
        queries, kvs, attf, stats, probs = kept[batch]
        order = vec
        if split and batch == batches - 1:
            pieces_a = call(chip_kernel, [shape(n_fs, dim // 4, dim)] * 4)(keep_a, arrived_a, back[0][5])
            total_a = call(chip_sum_kernel, shape(n_fs, dim // 4, dim), micros=5)(*exchange(pieces_a, n_sp))
            order = pieces_a[0]
        back.append(
            call(
                functools.partial(backward_kernel, (n_sp, batch, tok, key_dev, keys, block, n_pieces)),
                [
                    shape(*gkey_dims),
                    shape(*(gkey_dims if split else (16, 128))),
                    shape(PAIRS, keys, 2 * tok) if single else shape(dim, tok, dtype=f32),
                    shape(keys, dim),
                    shape(keys, dim),
                    shape(8, dim, dtype=f32),
                ],
                scratch=[pltpu.VMEM((2, keys, 2 * tok), f32)] if single else [pltpu.VMEM((keys, dim), f32)] * 2,
                limit=limit,
            )(gatt, queries, kvs, attf, stats, probs, bias, wkv, order)
        )
    near = [results[0] for results in back]
    keep_c, send_c, gnormed, gvec_c = call(
        functools.partial(query_kernel, (n_fs, batches, tok, key_dev, keys, block, n_pieces)),
        [
            shape(n_fs, half, dim),
            shape(n_fs, half, dim),
            shape(batches * tok, dim, dtype=f32),
            shape(VECS, dim, dtype=f32),
        ],
        scratch=[pltpu.VMEM((dim, tok), f32)],
        limit=limit,
    )(
        normed,
        wq,
        middle,
        *attended,
        *[kept[batch][1] for batch in range(batches)],
        *[results[2] for results in back],
        *[results[3] for results in back],
        *[results[4] for results in back],
        *[results[5] for results in back],
        *key_pieces,
    )
    arrived_c = flip(send_c, n_sp, 1)
    if split:
        far = [flip(results[1], n_sp, 1) for results in back]
        sums = call(functools.partial(key_sum_kernel, batches), [shape(batches * key_dev, dim)] * 4)(
            *near, *far, total_a, gvec_c
        )
        parts = exchange(sums, n_sp)
    else:
        parts = [lax.all_to_all(jnp.concatenate(near, axis=1), "sp", 0, 0)]
    *grad_reduced, gvec_b = call(
        functools.partial(reduction_kernel, len(parts), batches),
        [shape(key_dev, dim)] * batches + [shape(VECS, dim, dtype=f32)],
    )(reduced, vec, *parts)
    grad_other = [flip(part, n_sp, 1) for part in grad_reduced]
    grad_normed, vectors = call(
        functools.partial(normed_kernel, (batches, row_dev, cols, dim)),
        [shape(batches * tok, dim, dtype=f32), shape(VECS, dim)],
        scratch=[pltpu.VMEM((dim // 128, tok + 8, 128), f32)],
    )(gnormed, mask, whole_reduce, normal_first, gvec_a, gvec_b, gvec_c, *grad_reduced)
    chunks_b = call(functools.partial(weight_kernel, batches), [shape(half + VECS, dim)] * n_fs)(
        patch_cols, patch_other, *grad_reduced, *grad_other, vectors
    )
    if split:
        rows = dim // 4
        chunks = call(owners_kernel, [shape(rows + half, dim)] * n_fs)(total_a, keep_c, arrived_c)
        join = functools.partial(join_kernel, n_fs)
        first_a = to_owners(chunks, n_fs)
        last_a = first_a.pop(1)
        joined_a = call(functools.partial(join_kernel, n_fs - 1), shape(rows + half, dim), micros=5)(*first_a, vec)
        joined_a = call(functools.partial(join_kernel, 2), shape(rows + half, dim))(joined_a, last_a, vec)
        joined_b = call(join, shape(half + VECS, dim), micros=1)(*to_owners(chunks_b, n_fs), vec)
        mine = call(functools.partial(merge_kernel, rows), shape(4 * rows + half, dim))(
            *exchange([joined_a] * 4, n_sp), joined_b
        )
        order = mine
    else:
        order = vec
        groups = [to_owners(chunks_b, n_fs)]
        for keep, arrived in ((keep_c, arrived_c), (keep_a, arrived_a)):
            pieces = call(owner_kernel, [shape(*keep.shape[1:])] * n_fs)(keep, arrived)
            groups.insert(0, to_owners(pieces, n_fs))
        mine_a, mine_c, mine_b = (
            sum_over_rows(sum(piece.astype(f32) for piece in group).astype(bf16), n_sp) for group in groups
        )
        mine = jnp.concatenate([mine_a, mine_c], axis=0)

    grads, done = call(
        functools.partial(input_kernel, (batches, row_dev, cols, dim)),
        [shape(batches, 1, row_dev, cols, dim, dtype=f32), shape(8, 128, dtype=f32)],
    )(middle, grad_normed, normal_first, rstd_first, vec, order)

    if split:
        mine_b = call(functools.partial(merge_kernel, 0), shape(half + VECS, dim))(
            *exchange([joined_b] * 4, n_sp), done
        )
    (other_b,) = call(functools.partial(relay_kernel, 1), [shape(half + VECS, dim)], micros=1)(
        flip(mine_b, n_sp, 1), vec
    )
    gquery, gkeyval, goutput, ghidden, greturn, greduce, *vectors = call(
        functools.partial(final_kernel, n_fs),
        [
            shape(shard, dim, dtype=f32),
            shape(shard, 2 * dim, dtype=f32),
            shape(shard, dim, dtype=f32),
            shape(shard, hid, dtype=f32),
            shape(dim, dim, dtype=f32),
            shape(dim, dim, dtype=f32),
        ]
        + [shape(shard, dtype=f32)] * HIDDEN_B
        + [shape(dim, dtype=f32)],
    )(mine, flip(mine, n_sp, 1), mine_b, other_b)
    return (
        acts,
        grads,
        vectors[FIRST_G],
        vectors[FIRST_B],
        gquery,
        vectors[QUERY_B],
        greduce,
        vectors[REDUCE_B],
        vectors[KEYS_G],
        vectors[KEYS_B],
        gkeyval,
        vectors[VALUE_B],
        goutput,
        vectors[OUTPUT_B],
        vectors[SECOND_G],
        vectors[SECOND_B],
        ghidden,
        vectors[HIDDEN_B],
        greturn,
        vectors[RETURN_B],
    )


def solution(mesh):
    vec, mat = P("fs"), P("fs", None)
    image = P(None, "fs", "sp", None, None)
    weights = (vec, vec, mat, vec, mat, vec, vec, vec, mat, vec, mat, vec, vec, vec, mat, vec, mat, vec)
    return jax.shard_map(
        functools.partial(on_device, mesh.shape["fs"], mesh.shape["sp"]),
        mesh=mesh,
        in_specs=(image, image, P(None, "fs", None)) + weights,
        out_specs=(image, image) + weights,
        check_vma=False,
    )
```

```python
import functools

import jax
import jax.numpy as jnp
from jax import lax
from jax.experimental import pallas as pl
from jax.experimental.pallas import tpu as pltpu
from jax.sharding import PartitionSpec as P

HEADS = 8
HDIM = 32
PAIRS = HEADS // 2
SCALE = HDIM ** (-0.5)
EXP_SCALE = SCALE * 1.4426950408889634
EPS = 1e-06
NEG = -1e30
KEY_BLOCK = 768
SMALL_VMEM = 12 * 2**20
MAIN_VMEM = 16 * 2**20
WHOLE_VMEM = 58 * 2**20

bf16 = jnp.bfloat16
f32 = jnp.float32

(
    FIRST_G,
    FIRST_B,
    QUERY_B,
    REDUCE_B,
    KEYS_G,
    KEYS_B,
    VALUE_B,
    OUTPUT_B,
    SECOND_G,
    SECOND_B,
    RETURN_B,
    HIDDEN_B,
) = range(12)
VECS = 16


def mm(left, right):
    return jnp.dot(left, right, preferred_element_type=f32)


def mm_tn(left, right):
    return lax.dot_general(left, right, (((0,), (0,)), ((), ())), preferred_element_type=f32)


def mm_nt(left, right):
    return lax.dot_general(left, right, (((1,), (1,)), ((), ())), preferred_element_type=f32)


def normalize(rows):
    mean = jnp.mean(rows, axis=-1, keepdims=True)
    centered = rows - mean
    var = jnp.mean(centered * centered, axis=-1, keepdims=True)
    rstd = lax.rsqrt(var + EPS)
    return centered * rstd, rstd


def normalize_back(grad, normal, rstd, gain):
    scaled = grad * gain
    mean_a = jnp.mean(scaled, axis=-1, keepdims=True)
    mean_b = jnp.mean(scaled * normal, axis=-1, keepdims=True)
    return (scaled - mean_a - normal * mean_b) * rstd


def token_mask(first_row, rows, cols, width, height, image_width):
    row_ids = lax.broadcasted_iota(jnp.int32, (rows, cols, width), 0) + first_row
    col_ids = lax.broadcasted_iota(jnp.int32, (rows, cols, width), 1)
    valid = (row_ids < height) & (col_ids < image_width)
    return jnp.where(valid, 1.0, 0.0).astype(f32).reshape(rows * cols, width)


def pack_first_kernel(n_fs, *refs):
    smalls, (hidden_b, reduce_w, query_w, keyval_w, first, wide) = take(refs, HIDDEN_B)
    dim = reduce_w.shape[1]
    shard = dim // n_fs
    half = dim // 2
    rest = half + VECS
    fs = lax.axis_index("fs")
    is_low = lax.axis_index("sp") % 2 == 0

    @pl.when(is_low)
    def _():
        first[:half] = reduce_w[:half]
        first[rest : rest + shard] = query_w[...]
        first[rest + shard :] = keyval_w[: shard // 2, :dim]

    @pl.when(jnp.logical_not(is_low))
    def _():
        first[:half] = reduce_w[half:]
        first[rest : rest + shard // 2] = keyval_w[shard // 2 :, :dim]
        first[rest + shard // 2 :] = keyval_w[:, dim:]

    wide[...] = jnp.zeros_like(wide)
    for index, small in enumerate(smalls):
        row = small[...].astype(f32).reshape(1, shard)
        wide[index : index + 1, :] = jnp.concatenate([row] * n_fs, axis=1)
    lane = lax.broadcasted_iota(jnp.int32, wide.shape, 1)
    row = lax.broadcasted_iota(jnp.int32, wide.shape, 0)
    vectors = jnp.where(lane // shard == fs, wide[...], 0.0)
    hidden_row = hidden_b[...].astype(f32).reshape(1, dim)
    first[half:rest] = jnp.where(row == HIDDEN_B + fs, hidden_row, vectors).astype(bf16)


def both_halves(mine, other):
    is_low = lax.axis_index("sp") % 2 == 0
    a, b = mine[...], other[...]
    return jnp.where(is_low, a, b), jnp.where(is_low, b, a)


def shard_rows(place, rows):
    return pl.ds(pl.multiple_of(place * rows, rows), rows)


def begin_kernel(dims, sizes, tokens, hidden_w, return_w, output_w, packed, *refs):
    outs = refs[2:]
    n_sp, batches, row_dev, cols, dim = dims
    normal_ref, rstd_ref, mask_ref, bias_ref, own_half, begun_ref, second = outs
    tok = row_dev * cols
    half_cols = cols // 2
    rows_dev = row_dev // 2
    shard = hidden_w.shape[0]
    sp = lax.axis_index("sp")
    own_half[...] = packed[...]
    begun_ref[...] = jnp.zeros_like(begun_ref)

    @pl.when(sp % 2 == 0)
    def _():
        for chunk in range(hidden_w.shape[1] // dim):
            second[chunk * shard : (chunk + 1) * shard] = hidden_w[:, chunk * dim : (chunk + 1) * dim]
        second[dim:] = output_w[: shard // 2]

    @pl.when(sp % 2 == 1)
    def _():
        second[:dim] = return_w[...]
        second[dim:] = output_w[shard // 2 :]

    for batch in range(batches):
        height, image_width = sizes[batch, 0, 0], sizes[batch, 0, 1]
        rows = slice(batch * tok, (batch + 1) * tok)
        normal, rstd = normalize(tokens[batch, 0].reshape(tok, dim).astype(f32))
        normal_ref[rows] = normal
        rstd_ref[rows] = jnp.broadcast_to(rstd, (tok, 128))
        mask_ref[rows] = token_mask(sp * row_dev, row_dev, cols, dim, height, image_width)
        col_ids = lax.broadcasted_iota(jnp.int32, (half_cols, dim), 0)

        def key_row_bias(index, _, batch=batch, height=height, image_width=image_width, col_ids=col_ids):
            key_row = index
            if n_sp == 8:
                key_row = (sp ^ (index // rows_dev)) * rows_dev + lax.rem(index, rows_dev)
            width = jnp.where(2 * key_row < height, image_width, 0)
            here = pl.ds(pl.multiple_of(index * half_cols, half_cols), half_cols)
            bias_ref[batch, here, :] = jnp.where(2 * col_ids < width, 0.0, NEG).astype(bf16)
            return 0

        lax.fori_loop(0, n_sp * rows_dev, key_row_bias, 0)


def reduce_kernel(dims, *refs):
    n_fs, batches, row_dev, cols, dim = dims
    (normal_in, mask_ref), mine, other, outs = take(refs, 2, n_fs, n_fs)
    normed_ref, cols_ref, send_ref, reduced_ref, key_ref, weight_ref, wq, wkv, vec_ref, patch_ref, wide = outs
    half = dim // 2
    shard = dim // n_fs
    rest = half + VECS
    tok = row_dev * cols
    half_cols = cols // 2
    key_dev = tok // 4
    fs = lax.axis_index("fs")
    vec = jnp.zeros((VECS, dim), f32)
    for step in range(n_fs):
        low, high = both_halves(mine[step], other[step])
        place = lax.rem(fs + n_fs - step, n_fs)
        weight_ref[place, :half] = low[:half]
        weight_ref[place, half:] = high[:half]
        vec = vec + low[half:rest].astype(f32)
        here = shard_rows(place, shard)
        wq[here, :] = low[rest : rest + shard]
        wkv[here, :dim] = jnp.concatenate([low[rest + shard :], high[rest : rest + shard // 2]], axis=0)
        wkv[here, dim:] = high[rest + shard // 2 :]
    vec_ref[...] = vec
    for batch in range(batches):
        rows = slice(batch * tok, (batch + 1) * tok)
        low = (normal_in[rows] * vec[FIRST_G : FIRST_G + 1] + vec[FIRST_B : FIRST_B + 1]).astype(bf16)
        normed_ref[rows] = low
        masked = low.astype(f32) * mask_ref[rows]
        for part in range(dim // 128):
            wide[part, :tok] = masked[:, part * 128 : (part + 1) * 128]
        for row in range(row_dev // 2):
            start = batch * key_dev + row * half_cols
            for offset in range(4):
                dr, dc = offset // 2, offset % 2
                for part in range(dim // 128):
                    piece = wide[part, pl.ds((2 * row + dr) * cols + dc, half_cols, stride=2), :]
                    lanes = slice(offset * dim + part * 128, offset * dim + (part + 1) * 128)
                    patch_ref[start : start + half_cols, lanes] = piece.astype(bf16)
    is_low = lax.axis_index("sp") % 2 == 0
    for offset in range(4):
        low = patch_ref[:, offset * dim : offset * dim + half]
        high = patch_ref[:, offset * dim + half : (offset + 1) * dim]
        cols_ref[offset] = jnp.where(is_low, low, high)
        send_ref[offset] = jnp.where(is_low, high, low)
    reduced = mm(patch_ref[...], weight_ref[...].reshape(4 * dim, dim)) + vec[REDUCE_B : REDUCE_B + 1]
    reduced_ref[...] = reduced
    normal, _ = normalize(reduced)
    key_ref[...] = (normal * vec[KEYS_G : KEYS_G + 1] + vec[KEYS_B : KEYS_B + 1]).astype(bf16)


def relay_kernel(n, *refs):
    for source, target in zip(refs[:n], refs[n + 1 :]):
        target[...] = source[...]


def head_stack_t(values_t, pair, tok):
    both = jnp.concatenate([values_t, values_t], axis=1)
    head = lax.broadcasted_iota(jnp.int32, both.shape, 0) // HDIM
    want = 2 * pair + jnp.where(lax.broadcasted_iota(jnp.int32, both.shape, 1) >= tok, 1, 0)
    return jnp.where(head == want, both, jnp.zeros_like(both))


def head_stack(values, pair):
    head = lax.broadcasted_iota(jnp.int32, values.shape, 1) // HDIM
    zero = jnp.zeros_like(values)
    return jnp.concatenate(
        [jnp.where(head == 2 * pair, values, zero), jnp.where(head == 2 * pair + 1, values, zero)],
        axis=0,
    )


def split_pair(both, tok):
    return jnp.concatenate([both[:HDIM, :tok], both[HDIM:, tok:]], axis=0)


def key_rows_of(pieces, key_dev, per_block, batch, index):
    here = slice(batch * key_dev, (batch + 1) * key_dev)
    if len(pieces) > 1:
        return jnp.concatenate([part[here] for part in pieces], axis=0)
    dim = pieces[0].shape[2]
    devices = slice(index * per_block, (index + 1) * per_block)
    return pieces[0][devices, here, :].reshape(per_block * key_dev, dim)


def mask_lane(pair, dim):
    return 0 if pair == PAIRS - 1 else dim - 1


def with_bias(key_block, bias, lane_id):
    lane = lax.broadcasted_iota(jnp.int32, key_block.shape, 1)
    return jnp.where(lane == lane_id, bias.astype(f32), key_block.astype(f32)).astype(bf16)


def query_stack(queries_t, pair, lane_id, tok):
    stacked = head_stack_t(queries_t, pair, tok)
    row = lax.broadcasted_iota(jnp.int32, stacked.shape, 0)
    return jnp.where(row == lane_id, jnp.ones_like(stacked), stacked)


def take(refs, *counts):
    refs = list(refs)
    groups = []
    for count in counts:
        groups.append(refs[:count])
        refs = refs[count:]
    return groups + [refs]


def forward_kernel(dims, *refs):
    batch, tok, key_dev, keys, block, n_pieces = dims
    (normed, vec_ref, bias_ref, wq, wkv), pieces, outs = take(refs, 5, n_pieces)
    attended, queries_out, kvs, attf, stats, probs, wide = outs
    dim = wq.shape[0]
    blocks = keys // block
    per_block = block // key_dev
    queries = (mm(normed[batch * tok : (batch + 1) * tok], wq[...]) + vec_ref[QUERY_B : QUERY_B + 1]).astype(bf16)
    queries_out[...] = queries
    queries_t = queries.T
    for index in range(blocks):
        key_rows = key_rows_of(pieces, key_dev, per_block, batch, index)
        here = slice(index * block, (index + 1) * block)
        kvs[here, :dim] = mm(key_rows, wkv[:, :dim]).astype(bf16)
        value_rows = mm(key_rows, wkv[:, dim:]) + vec_ref[VALUE_B : VALUE_B + 1]
        kvs[here, dim:] = value_rows.astype(bf16)
    if blocks == 1:
        key_block = kvs[:, :dim]
        values_t = kvs[:, dim:].T
        masked = {lane_id: with_bias(key_block, bias_ref[batch], lane_id) for lane_id in (0, dim - 1)}

        def score(pair):
            lane_id = mask_lane(pair, dim)
            wide[pair % 2] = mm(masked[lane_id], query_stack(queries_t, pair, lane_id, tok))

        score(0)
        for pair in range(PAIRS):
            if pair + 1 < PAIRS:
                score(pair + 1)
            heads = slice(2 * HDIM * pair, 2 * HDIM * (pair + 1))
            scores = wide[pair % 2]
            top = jnp.max(scores, axis=0, keepdims=True)
            weights = jnp.exp2((scores - top) * EXP_SCALE)
            inverse = 1.0 / jnp.sum(weights, axis=0, keepdims=True)
            low = weights.astype(bf16)
            probs[pair] = low
            stats[pair, 0:1] = inverse
            mixed = mm(values_t[heads], low) * inverse
            attf[heads] = split_pair(mixed, tok)
    else:
        for pair in range(PAIRS):
            lane_id = mask_lane(pair, dim)
            heads = slice(2 * HDIM * pair, 2 * HDIM * (pair + 1))
            stacked = query_stack(queries_t, pair, lane_id, tok)

            def block_scores(index, stacked=stacked, lane_id=lane_id):
                here = pl.ds(pl.multiple_of(index * block, block), block)
                masked = with_bias(kvs[here, :dim], bias_ref[batch, here, :], lane_id)
                return here, mm(masked, stacked)

            def find_top(index, top, block_scores=block_scores):
                _, scores = block_scores(index)
                return jnp.maximum(top, jnp.max(scores, axis=0, keepdims=True))

            top = lax.fori_loop(0, blocks, find_top, jnp.full((1, 2 * tok), 4 * NEG, f32))

            def add_block(index, carry, block_scores=block_scores, top=top, heads=heads):
                total, mixed = carry
                here, scores = block_scores(index)
                weights = jnp.exp2((scores - top) * EXP_SCALE)
                values_t = kvs[here, dim:].T
                mixed = mixed + mm(values_t[heads], weights.astype(bf16))
                return total + jnp.sum(weights, axis=0, keepdims=True), mixed

            start = (jnp.zeros((1, 2 * tok), f32), jnp.zeros((2 * HDIM, 2 * tok), f32))
            total, mixed = lax.fori_loop(0, blocks, add_block, start)
            inverse = 1.0 / total
            stats[pair, 0:1] = inverse
            stats[pair, 1:2] = top
            attf[heads] = split_pair(mixed * inverse, tok)
    attended[...] = attf[...].T.astype(bf16)


def mlp_kernel(dims, *refs):
    n_fs, batches, row_dev, cols, dim, hid = dims
    ins, attended, own, mine, other, _, outs, scratch = take(refs, 4, batches, 3, n_fs - 1, n_fs - 1, 1, 6)
    tokens, cotangent, mask_ref, vec_ref = ins
    acts_ref, middle_ref, gatt, keep_ref, send_ref, gvec_ref = outs
    wh, wr, wo, lows, highs = scratch
    tok = row_dev * cols
    shard = dim // n_fs
    chunks = hid // dim
    fs = lax.axis_index("fs")
    is_low = lax.axis_index("sp") % 2 == 0
    wh[shard_rows(fs, shard), :] = own[0][...]
    wr[shard_rows(fs, dim), :] = own[1][...]
    wo[shard_rows(fs, shard), :] = own[2][...]
    for step in range(1, n_fs):
        low, high = both_halves(mine[step - 1], other[step - 1])
        place = fs ^ step
        here = shard_rows(place, shard)
        for chunk in range(chunks):
            wh[here, chunk * dim : (chunk + 1) * dim] = low[chunk * shard : (chunk + 1) * shard]
        wr[shard_rows(place, dim), :] = high[:dim]
        wo[here, :] = jnp.concatenate([low[dim:], high[dim:]], axis=0)

    def vec(index):
        return vec_ref[index : index + 1, :]

    x = jnp.concatenate([tokens[b, 0].reshape(tok, dim).astype(f32) for b in range(batches)], axis=0)
    mask = mask_ref[...]
    attended = jnp.concatenate([part[...] for part in attended], axis=0)
    middle = x + mm(attended, wo[...]) + vec(OUTPUT_B)
    normal, rstd = normalize(middle)
    second = (normal * vec(SECOND_G) + vec(SECOND_B)).astype(bf16)
    grad_out = jnp.concatenate([cotangent[b, 0].reshape(tok, dim) for b in range(batches)], axis=0) * mask
    grad_mlp = grad_out.astype(bf16)
    second_t, grad_mlp_t = second.T, grad_mlp.T
    total = middle + vec(RETURN_B)
    grad_second = jnp.zeros((batches * tok, dim), f32)
    gvec_ref[...] = jnp.zeros_like(gvec_ref)
    for chunk in range(chunks):
        lanes = slice(chunk * dim, (chunk + 1) * dim)
        hidden = mm(second, wh[:, lanes]) + vec(HIDDEN_B + chunk)
        phi = 0.5 + 0.5 * lax.erf(hidden * 0.7071067811865476)
        density = 0.3989422804014327 * jnp.exp2(hidden * hidden * (-0.5 * 1.4426950408889634))
        activated = (hidden * phi).astype(bf16)
        total = total + mm(activated, wr[lanes, :])
        grad_activated = mm_nt(grad_mlp, wr[lanes, :])
        grad_hidden = ((phi + hidden * density) * grad_activated).astype(bf16)
        gvec_ref[HIDDEN_B + chunk : HIDDEN_B + chunk + 1] = jnp.sum(
            grad_hidden.astype(f32), axis=0, keepdims=True
        )
        grad_second = grad_second + mm_nt(grad_hidden, wh[:, lanes])
        highs[chunk] = mm(grad_mlp_t, activated).T.astype(bf16)
        grad_wh = mm(second_t, grad_hidden).astype(bf16)
        for owner in range(n_fs):
            lows[owner, chunk * shard : (chunk + 1) * shard] = grad_wh[owner * shard : (owner + 1) * shard]
    low, high = lows[...], highs[...]
    keep_ref[...] = jnp.where(is_low, low, high)
    send_ref[...] = jnp.where(is_low, high, low)
    total = total * mask
    for batch in range(batches):
        acts_ref[batch, 0] = total[batch * tok : (batch + 1) * tok].reshape(row_dev, cols, dim)
    grad_middle = grad_out + normalize_back(grad_second, normal, rstd, vec(SECOND_G))
    middle_ref[...] = grad_middle
    grad_branch = grad_middle.astype(bf16)
    gatt[...] = mm_nt(grad_branch, wo[...]).astype(bf16)
    for index, value in (
        (OUTPUT_B, grad_branch.astype(f32)),
        (SECOND_G, grad_second * normal),
        (SECOND_B, grad_second),
        (RETURN_B, grad_mlp.astype(f32)),
    ):
        gvec_ref[index : index + 1] = jnp.sum(value, axis=0, keepdims=True)


def backward_kernel(dims, *refs):
    n_sp, batch, tok, key_dev, keys, block, n_pieces = dims
    gatt, queries_ref, kvs, attf, stats, probs, bias_ref, wkv, _ = refs[:9]
    near_ref, far_ref, scores_ref, gks, gvs, gvec_ref = refs[9:15]
    dim = wkv.shape[0]
    blocks = keys // block
    per_block = block // key_dev
    rows = slice(batch * tok, (batch + 1) * tok)
    queries = queries_ref[...]
    grad_att_t = gatt[rows].astype(f32).T
    product = grad_att_t * attf[...]

    def pair_terms(pair):
        inverse = stats[pair, 0:1]
        piece = product[2 * HDIM * pair : 2 * HDIM * (pair + 1)]
        delta = jnp.concatenate(
            [jnp.sum(piece[:HDIM], axis=0, keepdims=True), jnp.sum(piece[HDIM:], axis=0, keepdims=True)],
            axis=1,
        )
        stacked = head_stack_t(grad_att_t, pair, tok) * inverse
        return delta * inverse, stacked.astype(bf16)

    if blocks == 1:
        (wide,) = refs[15:]
        values = kvs[:, dim:]
        grad_k = jnp.zeros((keys, dim), f32)
        grad_v = jnp.zeros((keys, dim), f32)
        terms = []

        def grad_prob(pair):
            delta, stacked = pair_terms(pair)
            wide[pair % 2] = mm(values, stacked)
            terms.append((delta, stacked))

        grad_prob(0)
        for pair in range(PAIRS):
            if pair + 1 < PAIRS:
                grad_prob(pair + 1)
            delta, stacked = terms[pair]
            low = probs[pair]
            grad_scores = (low.astype(f32) * (wide[pair % 2] - delta)).astype(bf16)
            scores_ref[pair] = grad_scores
            grad_k = grad_k + mm(grad_scores, head_stack(queries, pair))
            grad_v = grad_v + mm(low, stacked.T)
    else:
        wide_k, wide_v = refs[15:]
        wide_k[...] = jnp.zeros_like(wide_k)
        wide_v[...] = jnp.zeros_like(wide_v)
        queries_t = queries.T
        for pair in range(PAIRS):
            heads = slice(2 * HDIM * pair, 2 * HDIM * (pair + 1))
            lane_id = mask_lane(pair, dim)
            delta, stacked = pair_terms(pair)
            stacked_n = stacked.T
            query_t = query_stack(queries_t, pair, lane_id, tok)
            query_n = head_stack(queries, pair)
            top = stats[pair, 1:2]

            def back_block(index, gq, heads=heads, lane_id=lane_id, delta=delta, stacked=stacked, stacked_n=stacked_n, query_t=query_t, query_n=query_n, top=top):
                here = pl.ds(pl.multiple_of(index * block, block), block)
                key_block = kvs[here, :dim]
                masked = with_bias(key_block, bias_ref[batch, here, :], lane_id)
                weights = jnp.exp2((mm(masked, query_t) - top) * EXP_SCALE)
                grad_probs = mm(kvs[here, dim:], stacked)
                grad_scores = (weights * (grad_probs - delta)).astype(bf16)
                wide_k[here, :] += mm(grad_scores, query_n)
                wide_v[here, :] += mm(weights.astype(bf16), stacked_n)
                return gq + mm(key_block.T[heads], grad_scores)

            gq = lax.fori_loop(0, blocks, back_block, jnp.zeros((2 * HDIM, 2 * tok), f32))
            scores_ref[heads] = split_pair(gq, tok)
    bias_value = jnp.zeros((1, dim), f32)
    for index in range(blocks):
        here = slice(index * block, (index + 1) * block)
        if blocks > 1:
            grad_k, grad_v = wide_k[here], wide_v[here]
        grad_k = (grad_k * SCALE).astype(bf16)
        bias_value = bias_value + jnp.sum(grad_v, axis=0, keepdims=True)
        grad_v = grad_v.astype(bf16)
        gks[here] = grad_k
        gvs[here] = grad_v
        grad_key = (mm_nt(grad_k, wkv[:, :dim]) + mm_nt(grad_v, wkv[:, dim:])).astype(bf16)
        if n_pieces > 1:
            pairs = grad_key.reshape(n_sp // 2, 2, key_dev, dim)
            near_ref[...] = pairs[:, 0]
            far_ref[...] = pairs[:, 1]
        else:
            near_ref[index * per_block : (index + 1) * per_block] = grad_key.reshape(per_block, key_dev, dim)
    gvec_ref[...] = jnp.broadcast_to(bias_value, gvec_ref.shape)


def query_kernel(dims, *refs):
    n_fs, batches, tok, key_dev, keys, block, n_pieces = dims
    ins, attended, kvs, scores, gks, gvs, gvecs, pieces, outs = take(refs, 3, *([batches] * 6), n_pieces)
    normed, wq, middle = ins
    keep_ref, send_ref, gnormed_ref, gvec_ref, wide = outs
    dim = wq.shape[0]
    shard = dim // n_fs
    blocks = keys // block
    per_block = block // key_dev
    grad_queries = []
    grad_wk = jnp.zeros((dim, dim), f32)
    grad_wv = jnp.zeros((dim, dim), f32)
    for batch in range(batches):
        if blocks == 1:
            keys_t = kvs[batch][:, :dim].T
            for pair in range(PAIRS):
                heads = slice(2 * HDIM * pair, 2 * HDIM * (pair + 1))
                wide[heads] = split_pair(mm(keys_t[heads], scores[batch][pair]), tok)
            grad_t = wide[...]
        else:
            grad_t = scores[batch][...]
        grad_queries.append((grad_t.T * SCALE).astype(bf16))
        for index in range(blocks):
            here = slice(index * block, (index + 1) * block)
            key_rows = key_rows_of(pieces, key_dev, per_block, batch, index)
            grad_wk = grad_wk + mm_tn(key_rows, gks[batch][here])
            grad_wv = grad_wv + mm_tn(key_rows, gvs[batch][here])
    grad_queries = jnp.concatenate(grad_queries, axis=0)
    grad_wq = mm_tn(normed[...], grad_queries)
    attended = jnp.concatenate([part[...] for part in attended], axis=0)
    grad_wo = mm_tn(attended, middle[...].astype(bf16))
    is_low = lax.axis_index("sp") % 2 == 0
    for owner in range(n_fs):
        part = slice(owner * shard, (owner + 1) * shard)
        low = jnp.concatenate([grad_wq[part], grad_wk[part]], axis=0).astype(bf16)
        high = jnp.concatenate([grad_wv[part], grad_wo[part]], axis=0).astype(bf16)
        keep_ref[owner] = jnp.where(is_low, low, high)
        send_ref[owner] = jnp.where(is_low, high, low)
    gnormed_ref[...] = mm_nt(grad_queries, wq[...])
    gvec_ref[...] = jnp.zeros_like(gvec_ref)
    gvec_ref[QUERY_B : QUERY_B + 1] = jnp.sum(grad_queries.astype(f32), axis=0, keepdims=True)
    bias_value = gvecs[0][0:1]
    for gvec in gvecs[1:]:
        bias_value = bias_value + gvec[0:1]
    gvec_ref[VALUE_B : VALUE_B + 1] = bias_value


def sum_parts(parts):
    if len(parts) == 1:
        total = parts[0][0].astype(f32)
        for index in range(1, parts[0].shape[0]):
            total = total + parts[0][index].astype(f32)
        return total
    total = parts[0][...].astype(f32)
    for part in parts[1:]:
        total = total + part[...].astype(f32)
    return total


def reduction_kernel(n_parts, batches, reduced, vec_ref, *refs):
    parts, gvec_ref, outs = refs[:n_parts], refs[-1], refs[-1 - batches : -1]
    grad_key = sum_parts(parts)
    normal, rstd = normalize(reduced[...])
    grad_low = normalize_back(grad_key, normal, rstd, vec_ref[KEYS_G : KEYS_G + 1]).astype(bf16)
    rows = outs[0].shape[0]
    for batch, out in enumerate(outs):
        out[...] = grad_low[batch * rows : (batch + 1) * rows]
    gvec_ref[...] = jnp.zeros_like(gvec_ref)
    for index, value in (
        (REDUCE_B, grad_low.astype(f32)),
        (KEYS_G, grad_key * normal),
        (KEYS_B, grad_key),
    ):
        gvec_ref[index : index + 1] = jnp.sum(value, axis=0, keepdims=True)


def weight_kernel(batches, *refs):
    (own_cols, other_cols), own, other, (vectors, *outs) = take(refs, 2, batches, batches)
    fs = lax.axis_index("fs")
    own = jnp.concatenate([part[...] for part in own], axis=0)
    other = jnp.concatenate([part[...] for part in other], axis=0)
    rows = own_cols.shape[2]
    for step, out in enumerate(outs):
        place = lax.rem(fs + step, len(outs))
        out[:rows] = (mm_tn(own_cols[place], own) + mm_tn(other_cols[place], other)).astype(out.dtype)
        out[rows:] = vectors[...]


def normed_kernel(dims, gnormed, mask_ref, weight, normal_ref, vec_a, vec_b, vec_c, *refs):
    batches, row_dev, cols, dim = dims
    grads, (grad_ref, gvec_ref, wide) = take(refs, batches)
    tok = row_dev * cols
    half_cols = cols // 2
    gain_first = jnp.zeros((1, dim), f32)
    bias_first = jnp.zeros((1, dim), f32)
    for batch in range(batches):
        for offset in range(4):
            dr, dc = offset // 2, offset % 2
            back = mm_nt(grads[batch][...], weight[offset])
            for row in range(row_dev // 2):
                for part in range(dim // 128):
                    wide[part, pl.ds((2 * row + dr) * cols + dc, half_cols, stride=2), :] = back[
                        row * half_cols : (row + 1) * half_cols, part * 128 : (part + 1) * 128
                    ]
        rows = slice(batch * tok, (batch + 1) * tok)
        spread = jnp.concatenate([wide[part, :tok] for part in range(dim // 128)], axis=1)
        grad_normed = gnormed[rows] + spread * mask_ref[rows]
        grad_ref[rows] = grad_normed
        gain_first = gain_first + jnp.sum(grad_normed * normal_ref[rows], axis=0, keepdims=True)
        bias_first = bias_first + jnp.sum(grad_normed, axis=0, keepdims=True)
    index = lax.broadcasted_iota(jnp.int32, (VECS, dim), 0)
    vectors = vec_a[...] + vec_b[...] + vec_c[...]
    vectors = jnp.where(index == FIRST_G, gain_first, vectors)
    vectors = jnp.where(index == FIRST_B, bias_first, vectors)
    gvec_ref[...] = vectors.astype(bf16)


def input_kernel(dims, middle, grad_normed, normal_ref, rstd_ref, vec_ref, _, grad_ref, done_ref):
    batches, row_dev, cols, dim = dims
    tok = row_dev * cols
    rstd = jnp.concatenate([rstd_ref[...]] * (dim // rstd_ref.shape[1]), axis=1)
    back = normalize_back(grad_normed[...], normal_ref[...], rstd, vec_ref[FIRST_G : FIRST_G + 1])
    grad_x = middle[...] + back
    for batch in range(batches):
        grad_ref[batch, 0] = grad_x[batch * tok : (batch + 1) * tok].reshape(row_dev, cols, dim)
    done_ref[...] = jnp.zeros_like(done_ref)


def key_sum_kernel(batches, *refs):
    near, far, _, outs = take(refs, batches, batches, 2)
    for step, out in enumerate(outs):
        rows = near[0].shape[1]
        for batch in range(batches):
            total = near[batch][step].astype(f32) + far[batch][step].astype(f32)
            out[batch * rows : (batch + 1) * rows] = total.astype(out.dtype)


def owner_kernel(keep, arrived, *outs):
    fs = lax.axis_index("fs")
    for step, out in enumerate(outs):
        place = lax.rem(fs + step, len(outs))
        out[...] = (keep[place].astype(f32) + arrived[place].astype(f32)).astype(out.dtype)


def chip_kernel(keep, arrived, _, *outs):
    chip = lax.axis_index("sp") // 2
    rows = outs[0].shape[1]
    for step, out in enumerate(outs):
        here = shard_rows(chip ^ step, rows)
        out[...] = (keep[:, here, :].astype(f32) + arrived[:, here, :].astype(f32)).astype(out.dtype)


def chip_sum_kernel(*refs):
    refs[-1][...] = sum_parts(refs[:-1]).astype(refs[-1].dtype)


def owners_kernel(total, keep, arrived, *outs):
    fs = lax.axis_index("fs")
    rows = total.shape[1]
    for step, out in enumerate(outs):
        place = lax.rem(fs + step, len(outs))
        out[:rows] = total[place]
        out[rows:] = (keep[place].astype(f32) + arrived[place].astype(f32)).astype(out.dtype)


def join_kernel(n, *refs):
    refs[-1][...] = sum_parts(refs[:n]).astype(refs[-1].dtype)


def merge_kernel(rows, *refs):
    parts, out = refs[:4], refs[5]
    chip = lax.axis_index("sp") // 2
    if rows:
        for step, part in enumerate(parts):
            out[shard_rows(chip ^ step, rows), :] = part[:rows]
    rest = [part[rows:].astype(f32) for part in parts]
    out[4 * rows :] = ((rest[0] + rest[1]) + (rest[2] + rest[3])).astype(out.dtype)


def final_kernel(n_fs, mine, other, mine_b, other_b, *outs):
    query_w, keyval_w, output_w, hidden_w, return_w, reduce_w = outs[:6]
    smalls, hidden_b = outs[6:-1], outs[-1]
    shard, dim = query_w.shape
    half = dim // 2
    fs = lax.axis_index("fs")
    low, high = both_halves(mine, other)
    low, high = low.astype(f32), high.astype(f32)
    for chunk in range(hidden_w.shape[1] // dim):
        hidden_w[:, chunk * dim : (chunk + 1) * dim] = low[chunk * shard : (chunk + 1) * shard]
    return_w[...] = high[:dim]
    low, high = low[dim:], high[dim:]
    query_w[...] = low[:shard]
    keyval_w[:, :dim] = low[shard : 2 * shard]
    keyval_w[:, dim:] = high[:shard]
    output_w[...] = high[shard : 2 * shard]
    low, high = both_halves(mine_b, other_b)
    low, high = low.astype(f32), high.astype(f32)
    reduce_w[:half] = low[:half]
    reduce_w[half:] = high[:half]
    vecs = low[half:] + high[half:]
    lane = lax.broadcasted_iota(jnp.int32, vecs.shape, 1)
    chosen = jnp.where(lane // shard == fs, vecs, 0.0)
    folded = chosen[:, :shard]
    for index in range(1, n_fs):
        folded = folded + chosen[:, index * shard : (index + 1) * shard]
    for index, small in enumerate(smalls):
        small[...] = folded[index : index + 1].reshape(shard)
    row = lax.broadcasted_iota(jnp.int32, vecs.shape, 0)
    hidden_b[...] = jnp.sum(jnp.where(row == HIDDEN_B + fs, vecs, 0.0), axis=0)


def rotate(value, n, step):
    return lax.ppermute(value, "fs", [(i, (i + step) % n) for i in range(n)])


def swap(value, n, bits):
    return lax.ppermute(value, "fs", [(i, i ^ bits) for i in range(n)])


def flip(value, n, bits):
    return lax.ppermute(value, "sp", [(i, i ^ bits) for i in range(n)])


def sum_over_rows(value, n_sp):
    bit = 2
    while bit < n_sp:
        if 2 * bit < n_sp:
            a, b, c = flip(value, n_sp, bit), flip(value, n_sp, 2 * bit), flip(value, n_sp, 3 * bit)
            value = (
                (value.astype(f32) + a.astype(f32)) + (b.astype(f32) + c.astype(f32))
            ).astype(value.dtype)
            bit = 4 * bit
        else:
            a = flip(value, n_sp, bit)
            value = (value.astype(f32) + a.astype(f32)).astype(value.dtype)
            bit = 2 * bit
    return value


def exchange(pieces, n_sp):
    return [pieces[0]] + [flip(pieces[step], n_sp, 2 * step) for step in range(1, n_sp // 2)]


def to_owners(pieces, n_fs):
    return [pieces[0]] + [rotate(pieces[step], n_fs, step) for step in range(1, n_fs)]


def call(kernel, out_shape, in_specs=None, scratch=(), limit=SMALL_VMEM, micros=0):
    specs = {} if in_specs is None else {"in_specs": in_specs}
    return pl.pallas_call(
        kernel,
        out_shape=out_shape,
        **specs,
        scratch_shapes=scratch,
        compiler_params=pltpu.CompilerParams(vmem_limit_bytes=limit),
        cost_estimate=pl.CostEstimate(flops=int(micros * 1e9), bytes_accessed=0, transcendentals=0),
    )


def on_device(
    n_fs,
    n_sp,
    tokens,
    cotangent,
    image_sizes,
    first_gain,
    first_bias,
    query_weight,
    query_bias,
    reduce_weight,
    reduce_bias,
    keys_gain,
    keys_bias,
    keyval_weight,
    value_bias,
    output_weight,
    output_bias,
    second_gain,
    second_bias,
    hidden_weight,
    hidden_bias,
    return_weight,
    return_bias,
):
    batches, _, row_dev, cols, dim = tokens.shape
    hid = hidden_weight.shape[1]
    tok = row_dev * cols
    key_dev = tok // 4
    keys = n_sp * key_dev
    shard = dim // n_fs
    half = dim // 2
    vmem = pl.BlockSpec(memory_space=pltpu.VMEM)
    smem = pl.BlockSpec(memory_space=pltpu.SMEM)
    single = keys <= KEY_BLOCK
    split = n_sp == 8
    block = keys if single else KEY_BLOCK
    limit = MAIN_VMEM if single else WHOLE_VMEM

    def shape(*dims, dtype=bf16):
        return jax.ShapeDtypeStruct(dims, dtype)

    smalls = (
        first_gain,
        first_bias,
        query_bias,
        reduce_bias,
        keys_gain,
        keys_bias,
        value_bias,
        output_bias,
        second_gain,
        second_bias,
        return_bias,
    )
    first_half = call(
        functools.partial(pack_first_kernel, n_fs),
        shape(half + VECS + 3 * shard // 2, dim),
        scratch=[pltpu.VMEM((VECS, dim), f32)],
        limit=WHOLE_VMEM,
    )(*smalls, hidden_bias, reduce_weight, query_weight, keyval_weight)
    arrived_first = to_owners([first_half] * n_fs, n_fs)[1:]

    begun = call(
        functools.partial(begin_kernel, (n_sp, batches, row_dev, cols, dim)),
        [
            shape(batches * tok, dim, dtype=f32),
            shape(batches * tok, 128, dtype=f32),
            shape(batches * tok, dim, dtype=f32),
            shape(batches, keys, dim),
            shape(*first_half.shape),
            shape(8, 128, dtype=f32),
            shape(dim + shard // 2, dim),
        ],
        in_specs=[smem] + [vmem] * 7,
        limit=SMALL_VMEM if single else WHOLE_VMEM,
    )(
        image_sizes,
        tokens,
        hidden_weight,
        return_weight,
        output_weight,
        first_half,
        reduce_weight,
        keyval_weight,
    )
    normal_first, rstd_first, mask, bias, own_half, done, second_half = begun
    mine_first = call(functools.partial(relay_kernel, n_fs), [shape(*first_half.shape)] * n_fs)(
        own_half, *arrived_first, done
    )
    other_first = [flip(piece, n_sp, 1) for piece in mine_first]
    normed, patch_cols, patch_send, reduced, key_low, whole_reduce, wq, wkv, vec = call(
        functools.partial(reduce_kernel, (n_fs, batches, row_dev, cols, dim)),
        [
            shape(batches * tok, dim),
            shape(4, batches * key_dev, half),
            shape(4, batches * key_dev, half),
            shape(batches * key_dev, dim, dtype=f32),
            shape(batches * key_dev, dim),
            shape(n_fs, dim, dim),
            shape(dim, dim),
            shape(dim, 2 * dim),
            shape(VECS, dim, dtype=f32),
        ],
        scratch=[pltpu.VMEM((batches * key_dev, 4 * dim), bf16), pltpu.VMEM((dim // 128, tok + 8, 128), f32)],
    )(normal_first, mask, *mine_first, *other_first)
    across = swap(second_half, n_fs, 2)
    passed = call(functools.partial(relay_kernel, 1), [shape(dim + shard // 2, dim)], micros=15)(across, done)
    mine_second = [swap(second_half, n_fs, 1), across, swap(passed[0], n_fs, 1)]

    if split:
        same = exchange([key_low] * (n_sp // 2), n_sp)
        key_pieces = [piece for part in same for piece in (part, flip(part, n_sp, 1))]
    else:
        key_pieces = [lax.all_gather(key_low, "sp")]
    n_pieces = len(key_pieces)

    kept = [
        call(
            functools.partial(forward_kernel, (batch, tok, key_dev, keys, block, n_pieces)),
            [
                shape(tok, dim),
                shape(tok, dim),
                shape(keys, 2 * dim),
                shape(dim, tok, dtype=f32),
                shape(PAIRS, 8, 2 * tok, dtype=f32),
                shape(PAIRS, keys, 2 * tok) if single else shape(16, 128),
            ],
            scratch=[pltpu.VMEM((2, block, 2 * tok) if single else (8, 128), f32)],
            limit=limit,
        )(normed, vec, bias, wq, wkv, *key_pieces)
        for batch in range(batches)
    ]
    attended = [results[0] for results in kept]
    kept = [results[1:] for results in kept]
    mine_second = call(functools.partial(relay_kernel, n_fs - 1), [shape(dim + shard // 2, dim)] * (n_fs - 1))(
        *mine_second, kept[0][3]
    )
    patch_other = flip(patch_send, n_sp, 1)
    other_second = [flip(piece, n_sp, 1) for piece in mine_second]

    acts, middle, gatt, keep_a, send_a, gvec_a = call(
        functools.partial(mlp_kernel, (n_fs, batches, row_dev, cols, dim, hid)),
        [
            shape(batches, 1, row_dev, cols, dim, dtype=f32),
            shape(batches * tok, dim, dtype=f32),
            shape(batches * tok, dim),
            shape(n_fs, dim, dim),
            shape(n_fs, dim, dim),
            shape(VECS, dim, dtype=f32),
        ],
        scratch=[
            pltpu.VMEM((dim, hid), bf16),
            pltpu.VMEM((hid, dim), bf16),
            pltpu.VMEM((dim, dim), bf16),
            pltpu.VMEM((n_fs, dim, dim), bf16),
            pltpu.VMEM((n_fs, dim, dim), bf16),
        ],
        limit=limit,
    )(
        tokens,
        cotangent,
        mask,
        vec,
        *attended,
        hidden_weight,
        return_weight,
        output_weight,
        *mine_second,
        *other_second,
        patch_other,
    )
    arrived_a = flip(send_a, n_sp, 1)
    gkey_dims = (n_sp // 2, key_dev, dim) if split else (n_sp, key_dev, dim)
    back = []
    for batch in range(batches):
        queries, kvs, attf, stats, probs = kept[batch]
        order = vec
        if split and batch == batches - 1:
            pieces_a = call(chip_kernel, [shape(n_fs, dim // 4, dim)] * 4)(keep_a, arrived_a, back[0][5])
            total_a = call(chip_sum_kernel, shape(n_fs, dim // 4, dim), micros=5)(*exchange(pieces_a, n_sp))
            order = pieces_a[0]
        back.append(
            call(
                functools.partial(backward_kernel, (n_sp, batch, tok, key_dev, keys, block, n_pieces)),
                [
                    shape(*gkey_dims),
                    shape(*(gkey_dims if split else (16, 128))),
                    shape(PAIRS, keys, 2 * tok) if single else shape(dim, tok, dtype=f32),
                    shape(keys, dim),
                    shape(keys, dim),
                    shape(8, dim, dtype=f32),
                ],
                scratch=[pltpu.VMEM((2, keys, 2 * tok), f32)] if single else [pltpu.VMEM((keys, dim), f32)] * 2,
                limit=limit,
            )(gatt, queries, kvs, attf, stats, probs, bias, wkv, order)
        )
    near = [results[0] for results in back]
    keep_c, send_c, gnormed, gvec_c = call(
        functools.partial(query_kernel, (n_fs, batches, tok, key_dev, keys, block, n_pieces)),
        [
            shape(n_fs, half, dim),
            shape(n_fs, half, dim),
            shape(batches * tok, dim, dtype=f32),
            shape(VECS, dim, dtype=f32),
        ],
        scratch=[pltpu.VMEM((dim, tok), f32)],
        limit=limit,
    )(
        normed,
        wq,
        middle,
        *attended,
        *[kept[batch][1] for batch in range(batches)],
        *[results[2] for results in back],
        *[results[3] for results in back],
        *[results[4] for results in back],
        *[results[5] for results in back],
        *key_pieces,
    )
    arrived_c = flip(send_c, n_sp, 1)
    if split:
        far = [flip(results[1], n_sp, 1) for results in back]
        sums = call(functools.partial(key_sum_kernel, batches), [shape(batches * key_dev, dim)] * 4)(
            *near, *far, total_a, gvec_c
        )
        parts = exchange(sums, n_sp)
    else:
        parts = [lax.all_to_all(jnp.concatenate(near, axis=1), "sp", 0, 0)]
    *grad_reduced, gvec_b = call(
        functools.partial(reduction_kernel, len(parts), batches),
        [shape(key_dev, dim)] * batches + [shape(VECS, dim, dtype=f32)],
    )(reduced, vec, *parts)
    grad_other = [flip(part, n_sp, 1) for part in grad_reduced]
    grad_normed, vectors = call(
        functools.partial(normed_kernel, (batches, row_dev, cols, dim)),
        [shape(batches * tok, dim, dtype=f32), shape(VECS, dim)],
        scratch=[pltpu.VMEM((dim // 128, tok + 8, 128), f32)],
    )(gnormed, mask, whole_reduce, normal_first, gvec_a, gvec_b, gvec_c, *grad_reduced)
    chunks_b = call(functools.partial(weight_kernel, batches), [shape(half + VECS, dim)] * n_fs)(
        patch_cols, patch_other, *grad_reduced, *grad_other, vectors
    )
    if split:
        rows = dim // 4
        chunks = call(owners_kernel, [shape(rows + half, dim)] * n_fs)(total_a, keep_c, arrived_c)
        join = functools.partial(join_kernel, n_fs)
        first_a = to_owners(chunks, n_fs)
        last_a = first_a.pop(1)
        joined_a = call(functools.partial(join_kernel, n_fs - 1), shape(rows + half, dim), micros=5)(*first_a, vec)
        joined_a = call(functools.partial(join_kernel, 2), shape(rows + half, dim))(joined_a, last_a, vec)
        joined_b = call(join, shape(half + VECS, dim), micros=1)(*to_owners(chunks_b, n_fs), vec)
        mine = call(functools.partial(merge_kernel, rows), shape(4 * rows + half, dim))(
            *exchange([joined_a] * 4, n_sp), joined_b
        )
        order = mine
    else:
        order = vec
        groups = [to_owners(chunks_b, n_fs)]
        for keep, arrived in ((keep_c, arrived_c), (keep_a, arrived_a)):
            pieces = call(owner_kernel, [shape(*keep.shape[1:])] * n_fs)(keep, arrived)
            groups.insert(0, to_owners(pieces, n_fs))
        mine_a, mine_c, mine_b = (
            sum_over_rows(sum(piece.astype(f32) for piece in group).astype(bf16), n_sp) for group in groups
        )
        mine = jnp.concatenate([mine_a, mine_c], axis=0)

    grads, done = call(
        functools.partial(input_kernel, (batches, row_dev, cols, dim)),
        [shape(batches, 1, row_dev, cols, dim, dtype=f32), shape(8, 128, dtype=f32)],
    )(middle, grad_normed, normal_first, rstd_first, vec, order)

    if split:
        mine_b = call(functools.partial(merge_kernel, 0), shape(half + VECS, dim))(
            *exchange([joined_b] * 4, n_sp), done
        )
    (other_b,) = call(functools.partial(relay_kernel, 1), [shape(half + VECS, dim)], micros=1)(
        flip(mine_b, n_sp, 1), vec
    )
    gquery, gkeyval, goutput, ghidden, greturn, greduce, *vectors = call(
        functools.partial(final_kernel, n_fs),
        [
            shape(shard, dim, dtype=f32),
            shape(shard, 2 * dim, dtype=f32),
            shape(shard, dim, dtype=f32),
            shape(shard, hid, dtype=f32),
            shape(dim, dim, dtype=f32),
            shape(dim, dim, dtype=f32),
        ]
        + [shape(shard, dtype=f32)] * HIDDEN_B
        + [shape(dim, dtype=f32)],
    )(mine, flip(mine, n_sp, 1), mine_b, other_b)
    return (
        acts,
        grads,
        vectors[FIRST_G],
        vectors[FIRST_B],
        gquery,
        vectors[QUERY_B],
        greduce,
        vectors[REDUCE_B],
        vectors[KEYS_G],
        vectors[KEYS_B],
        gkeyval,
        vectors[VALUE_B],
        goutput,
        vectors[OUTPUT_B],
        vectors[SECOND_G],
        vectors[SECOND_B],
        ghidden,
        vectors[HIDDEN_B],
        greturn,
        vectors[RETURN_B],
    )


def solution(mesh):
    vec, mat = P("fs"), P("fs", None)
    image = P(None, "fs", "sp", None, None)
    weights = (vec, vec, mat, vec, mat, vec, vec, vec, mat, vec, mat, vec, vec, vec, mat, vec, mat, vec)
    return jax.shard_map(
        functools.partial(on_device, mesh.shape["fs"], mesh.shape["sp"]),
        mesh=mesh,
        in_specs=(image, image, P(None, "fs", None)) + weights,
        out_specs=(image, image) + weights,
        check_vma=False,
    )
```
